32 devices in a mesh: band: 8 (over z, x), rows: 4 (over y, core).
Axes of the slice: x: 2, y: 2, z: 4, core: 2. Of those that a mesh axis runs over, the one named last changes fastest.
Arguments:
- pixels: bfloat16 [2048, 256, 196], P('band', 'rows'), may hold values from -6 to 6
- band_counts: int32 [8, 12], P('band'), may hold values from 1 to 202, 256 in all within a row
- band_waves: int32 [8, 256], P('band'), may hold values from 0 to 31
- wavelengths: float32 [32], replicated, may hold values from 0.4 to 2.5
- bias_token: float32 [128], replicated, may hold values from -6 to 6
- wave_qkv: float32 [128, 384], replicated, may hold values from -1 to 1
- wave_proj: float32 [128, 128], replicated, may hold values from -0.5 to 0.5
- wave_gain: float32 [128], replicated, may hold values from 0.5 to 1.5
- wave_shift: float32 [128], replicated, may hold values from -3 to 3
- wave_up: float32 [128, 2048], replicated, may hold values from -0.5 to 0.5
- wave_down: float32 [2048, 128], replicated, may hold values from -0.125 to 0.125
- kernel_gain: float32 [128], replicated, may hold values from 0.5 to 1.5
- kernel_shift: float32 [128], replicated, may hold values from -3 to 3
- bias_head: float32 [128, 768], replicated, may hold values from -0.5 to 0.5
- kernel_weight: bfloat16 [256, 128, 768], P('rows'), may hold values from -0.0078125 to 0.0078125
- attention_gain: float32 [768], replicated, may hold values from 0.5 to 1.5
- attention_shift: float32 [768], replicated, may hold values from -3 to 3
- block_qkv: bfloat16 [768, 2304], replicated, may hold values from -0.21875 to 0.21875
- block_proj: bfloat16 [768, 768], replicated, may hold values from -0.625 to 0.625
- hidden_gain: float32 [768], replicated, may hold values from 0.5 to 1.5
- hidden_shift: float32 [768], replicated, may hold values from -3 to 3
- block_up: bfloat16 [768, 3072], replicated, may hold values from -0.21875 to 0.21875
- block_down: bfloat16 [3072, 768], replicated, may hold values from -0.109375 to 0.109375
- cotangent: bfloat16 [18816, 768], P(('band', 'rows')), may hold values from -6 to 6
Outputs:
- layer_output: bfloat16 [18816, 768], P(('band', 'rows'))
- pixel_grad: bfloat16 [2048, 256, 196], P('band', 'rows')
- kernel_weight_grad: float32 [256, 128, 768], P('rows', 'band')
- bias_token_grad: float32 [128], replicated
- wave_qkv_grad: float32 [128, 384], replicated
- wave_proj_grad: float32 [128, 128], replicated
- wave_gain_grad: float32 [128], replicated
- wave_shift_grad: float32 [128], replicated
- wave_up_grad: float32 [128, 2048], replicated
- wave_down_grad: float32 [2048, 128], replicated
- kernel_gain_grad: float32 [128], replicated
- kernel_shift_grad: float32 [128], replicated
- bias_head_grad: float32 [128, 768], replicated
- attention_gain_grad: float32 [768], replicated
- attention_shift_grad: float32 [768], replicated
- block_qkv_grad: float32 [768, 2304], P('band')
- block_proj_grad: float32 [768, 768], P('band')
- hidden_gain_grad: float32 [768], replicated
- hidden_shift_grad: float32 [768], replicated
- block_up_grad: float32 [768, 3072], P('band')
- block_down_grad: float32 [3072, 768], P('band')
The draws below stay inside these ranges and needn't reach their ends.
Inputs may be any that keep to these rules, and one draw needn't show every extreme that they name: `band_counts`: each row holds the band counts of the 12 images of one group; they sum to 256, the largest is exactly 202, and the slots of a group belong to its images in order.
All inputs are finite; a program needn't handle non-finite values.
Results may differ from the reference program's by a relative error of at most 0.015.
Values may be sent and summed in bfloat16 or wider, within the bound.
No kernel may reach another device: no remote copies, remote signals or barrier semaphores. Data moves between devices by JAX's collectives and lax.ppermute only.
A program may use at most 320 MiB of HBM per device.

```python
import math
from functools import partial
import jax
import jax.numpy as jnp
import numpy as np
from jax import lax

D = 768
HEADS = 12
FF = 3072
WD = 128
WHEADS = 4
WFF = 2048
PIX = 256
PATCHES = 196
HYPER = 202
SLOTS = 256
IMG_GRP = 12
TOKENS = 18816
BANDS = 2048
NWAVE = 32
N_BAND = 8


def with_ends(array, key, low, high):
    shape = array.shape
    place = [jax.random.randint(jax.random.fold_in(key, axis), (), 0, shape[axis]) for axis in range(len(shape))]
    array = array.at[tuple(place)].set(low)
    longest = shape.index(max(shape))
    place[longest] = (place[longest] + 1) % shape[longest]
    return array.at[tuple(place)].set(high)


def levels(stream_key, dims, shards, smallest, largest):
    gain, own = 1.0, jax.random.fold_in(stream_key, 6)
    for position, parts in shards:
        draws = jnp.exp(jax.random.uniform(jax.random.fold_in(own, position), (parts,), jnp.float32, smallest / len(shards), largest / len(shards)))
        gain = gain * jnp.repeat(draws, dims[position] // parts).reshape([-1 if axis == position else 1 for axis in range(len(dims))])
    return gain


def length_profile(amount, total, most, skew):
    loads = [(1 << 20) // math.isqrt(rank ** skew) + 1 for rank in range(2, amount + 1)]
    rest, given = total - most - (amount - 1), [1] * (amount - 1)
    while rest > 0:
        candidates = [i for i in range(amount - 1) if given[i] < most]
        pool, remaining = sum([loads[i] for i in candidates]), rest
        for i in candidates:
            addition = min(most - given[i], max(1, remaining * loads[i] // pool), rest)
            given[i] = given[i] + addition
            rest = rest - addition
    return np.array([most] + given)


def uneven(key, amount, total, bound, slope):
    if amount == 2:
        one = jax.random.randint(key, (), max(1, total - bound), min(bound, total - 1) + 1)
        return jnp.stack([one, total - one])
    tallies = jnp.asarray(length_profile(amount, total, bound, slope), jnp.int32)
    pairs = (amount - 1) // 2
    giver, sink = tallies[1:1 + 2 * pairs:2], tallies[2:2 + 2 * pairs:2]
    slack = jnp.minimum(giver - 1, bound - sink)
    passed = jax.random.randint(jax.random.fold_in(key, 1), (pairs,), 0, 1 << 20) % (slack + 1)
    tallies = tallies.at[1:1 + 2 * pairs:2].set(giver - passed).at[2:2 + 2 * pairs:2].set(sink + passed)
    return tallies[jax.random.permutation(jax.random.fold_in(key, 2), amount)]


def scatter_about(key, dims, scale, bound, cuts=(), kind=jnp.bfloat16):
    factor_of = levels(key, dims, cuts, -0.22, 0.18) if cuts else 1.0
    array = jax.random.normal(key, dims, jnp.float32) * scale * factor_of
    return jnp.minimum(jnp.maximum(array, -bound), bound).astype(kind)


def setup_inputs(seed: int = 0) -> dict:
    splits = jax.random.split(jax.random.key(seed), 25)
    return {
        "pixels": scatter_about(splits[0], (BANDS, PIX, PATCHES), 1.0, 6.0, ((0, 8), (1, 4))),
        "band_counts": jax.vmap(lambda own: uneven(own, IMG_GRP, SLOTS, HYPER, 2))(jax.random.split(splits[1], N_BAND)).reshape((N_BAND, IMG_GRP)).astype(jnp.int32),
        "band_waves": with_ends(jax.random.randint(splits[2], (N_BAND, SLOTS), 0, NWAVE), jax.random.fold_in(splits[2], 1), 0, NWAVE - 1).astype(jnp.int32),
        "wavelengths": jnp.clip(jax.random.uniform(splits[3], (NWAVE,), jnp.float32, 0.4, 2.5), 0.4, 2.5),
        "bias_token": scatter_about(splits[4], (WD,), 1.0, 6.0, (), jnp.float32),
        "wave_qkv": scatter_about(splits[5], (WD, 3 * WD), (WD // 4) ** -0.5, 1.0, (), jnp.float32),
        "wave_proj": scatter_about(splits[6], (WD, WD), WD ** -0.5, 0.5, (), jnp.float32),
        "wave_gain": jnp.clip(1.0 + 0.1 * jax.random.normal(splits[7], (WD,), jnp.float32), 0.5, 1.5),
        "wave_shift": scatter_about(splits[8], (WD,), 0.5, 3.0, (), jnp.float32),
        "wave_up": scatter_about(splits[9], (WD, WFF), WD ** -0.5, 0.5, (), jnp.float32),
        "wave_down": scatter_about(splits[10], (WFF, WD), WFF ** -0.5, 0.125, (), jnp.float32),
        "kernel_gain": jnp.clip(1.0 + 0.1 * jax.random.normal(splits[11], (WD,), jnp.float32), 0.5, 1.5),
        "kernel_shift": scatter_about(splits[12], (WD,), 0.5, 3.0, (), jnp.float32),
        "bias_head": scatter_about(splits[13], (WD, D), WD ** -0.5, 0.5, (), jnp.float32),
        "kernel_weight": scatter_about(splits[14], (PIX, WD, D), (WD * PIX * 16) ** -0.5, 0.0078125, ((0, 4),)),
        "attention_gain": jnp.clip(1.0 + 0.1 * jax.random.normal(splits[15], (D,), jnp.float32), 0.5, 1.5),
        "attention_shift": scatter_about(splits[16], (D,), 0.5, 3.0, (), jnp.float32),
        "block_qkv": scatter_about(splits[17], (D, 3 * D), D ** -0.5, 0.21875),
        "block_proj": scatter_about(splits[18], (D, D), (D // 8) ** -0.5, 0.625),
        "hidden_gain": jnp.clip(1.0 + 0.1 * jax.random.normal(splits[19], (D,), jnp.float32), 0.5, 1.5),
        "hidden_shift": scatter_about(splits[20], (D,), 0.5, 3.0, (), jnp.float32),
        "block_up": scatter_about(splits[21], (D, FF), D ** -0.5, 0.21875),
        "block_down": scatter_about(splits[22], (FF, D), FF ** -0.5, 0.109375),
        "cotangent": scatter_about(splits[23], (TOKENS, D), 1.0, 6.0, ((0, 32),)),
    }


@jax.custom_vjp
def low(v):
    return lax.optimization_barrier(v.astype(jnp.bfloat16)).astype(jnp.float32)

@jax.custom_vjp
def low_back(v):
    return v

def low_keep(v):
    return (low(v), None)

def low_pass(kept, grad):
    return (grad,)

def back_keep(v):
    return (v, None)

def back_low(kept, grad):
    return (low(grad),)
low.defvjp(low_keep, low_pass)
low_back.defvjp(back_keep, back_low)
highest = lax.Precision.HIGHEST

def matmul_high(left, right):
    return jnp.dot(left, right, precision=highest, preferred_element_type=jnp.float32)

def layer_norm(values, norm_gain, norm_shift, epsilon):
    centered = values - lax.optimization_barrier(jnp.mean(values, axis=-1, keepdims=True))
    variance = lax.optimization_barrier(jnp.mean(centered * centered, axis=-1, keepdims=True))
    return centered * lax.rsqrt(variance + epsilon) * norm_gain + norm_shift

def wave_embed(wavelengths):
    halfwidth = WD // 2
    indices = jnp.arange(halfwidth, dtype=jnp.float32)
    frequency = 1.0 / 10000.0 ** (indices / halfwidth)
    angles = (wavelengths * 1000.0)[:, None] * frequency[None, :]
    return jnp.concatenate([jnp.sin(angles), jnp.cos(angles)], axis=1)

def hypernet(embedded, params):
    bias_token, wave_qkv, wave_proj, wave_gain, wave_shift, wave_up, wave_down, kernel_gain, kernel_shift, bias_head = params
    sequence = jnp.concatenate([embedded, bias_token[None, :]], axis=0)
    length = sequence.shape[0]
    head_width = WD // WHEADS
    projected = matmul_high(sequence, wave_qkv).reshape(length, 3, WHEADS, head_width)
    scores = jnp.einsum('qhd,khd->hqk', projected[:, 0], projected[:, 1], precision=highest) / math.sqrt(head_width)
    weights = jax.nn.softmax(scores, axis=-1)
    attended = jnp.einsum('hqk,khd->qhd', weights, projected[:, 2], precision=highest).reshape(length, WD)
    normed_first = layer_norm(sequence + matmul_high(attended, wave_proj), wave_gain, wave_shift, 1e-05)
    widened = jax.nn.gelu(matmul_high(normed_first, wave_up), approximate=False)
    second = layer_norm(normed_first + matmul_high(widened, wave_down), kernel_gain, kernel_shift, 1e-05)
    return (second[:-1] + embedded, matmul_high(second[-1:], bias_head)[0])

def vit_block(embedded_rows, block_params):
    attention_gain, attention_shift, block_qkv, block_proj, hidden_gain, hidden_shift, block_up, block_down = block_params
    row_count = embedded_rows.shape[0]
    width = embedded_rows.shape[1]
    head_size = width // HEADS
    images = row_count // PATCHES
    normed = low(layer_norm(embedded_rows, attention_gain, attention_shift, 1e-06))
    projected = low(low_back(matmul_high(normed, block_qkv))).reshape(images, PATCHES, 3, HEADS, head_size)
    queries = projected[:, :, 0]
    keys_all = projected[:, :, 1]
    values_all = projected[:, :, 2]
    scores = low_back(jnp.einsum('iqhd,ikhd->ihqk', queries, keys_all, precision=highest) / math.sqrt(head_size))
    probs = low(jax.nn.softmax(scores, axis=-1))
    mixed_rows = low(low_back(jnp.einsum('ihqk,ikhd->iqhd', probs, values_all, precision=highest))).reshape(row_count, width)
    middle = embedded_rows + low_back(matmul_high(mixed_rows, block_proj))
    normed_mid = low(layer_norm(middle, hidden_gain, hidden_shift, 1e-06))
    upward = low_back(matmul_high(normed_mid, block_up))
    activated = low(jax.nn.gelu(upward, approximate=False))
    return middle + low_back(matmul_high(activated, block_down))

def forward(wavelengths, band_counts, band_waves, pixels, hyper_params, kernel_weight, block_params):
    embedded = wave_embed(wavelengths)
    kernel_in, conv_bias = hypernet(embedded, hyper_params)
    kernel = low(jnp.einsum('wk,qkc->wqc', low(kernel_in), kernel_weight, precision=highest))
    grouped = pixels.reshape(N_BAND, SLOTS, PIX, PATCHES)

    def group_rows(inputs):
        group_pixels, counts_row, waves_row = inputs
        bounds = jnp.cumsum(counts_row)
        slot_index = jnp.arange(SLOTS, dtype=jnp.int32)
        owners = lax.optimization_barrier(jnp.sum((bounds[None, :] <= slot_index[:, None]).astype(jnp.int32), axis=1))
        member = (owners[None, :] == jnp.arange(IMG_GRP, dtype=jnp.int32)[:, None]).astype(jnp.float32)
        chosen = kernel[waves_row]
        per_slot = jnp.einsum('sqp,sqc->spc', group_pixels, chosen, precision=highest)
        summed = jnp.einsum('is,spc->ipc', member, per_slot, precision=highest).reshape(IMG_GRP * PATCHES, D)
        return vit_block(low_back(summed) + conv_bias, block_params)
    outputs = lax.map(jax.checkpoint(group_rows), (grouped, band_counts, band_waves))
    return outputs.reshape(TOKENS, D)

def reference(pixels, band_counts, band_waves, wavelengths, bias_token, wave_qkv, wave_proj, wave_gain, wave_shift, wave_up, wave_down, kernel_gain, kernel_shift, bias_head, kernel_weight, attention_gain, attention_shift, block_qkv, block_proj, hidden_gain, hidden_shift, block_up, block_down, cotangent):
    hyper_params = (bias_token, wave_qkv, wave_proj, wave_gain, wave_shift, wave_up, wave_down, kernel_gain, kernel_shift, bias_head)
    block_params = (attention_gain, attention_shift, block_qkv.astype(jnp.float32), block_proj.astype(jnp.float32), hidden_gain, hidden_shift, block_up.astype(jnp.float32), block_down.astype(jnp.float32))
    primal = partial(forward, wavelengths, band_counts, band_waves)
    result, pullback = jax.vjp(primal, pixels.astype(jnp.float32), hyper_params, kernel_weight.astype(jnp.float32), block_params)
    grad_pixels, grad_hyper, grad_kernel, grad_block = pullback(cotangent.astype(jnp.float32))
    return (result.astype(jnp.bfloat16), grad_pixels.astype(jnp.bfloat16), grad_kernel, grad_hyper[0], grad_hyper[1], grad_hyper[2], grad_hyper[3], grad_hyper[4], grad_hyper[5], grad_hyper[6], grad_hyper[7], grad_hyper[8], grad_hyper[9], grad_block[0], grad_block[1], grad_block[2], grad_block[3], grad_block[4], grad_block[5], grad_block[6], grad_block[7])
```

```python
import functools
import math

import jax
import jax.numpy as jnp
from jax import lax
from jax.experimental import pallas as pl
from jax.experimental.pallas import tpu as pltpu
from jax.sharding import PartitionSpec as P

VMEM_LIMIT = 60 * 1024 * 1024
STEPS = 8
QUAD = 4
LANES = 128


def pad_rows(rows):
    return (rows + 15) // 16 * 16


def fill_starts(counts_ref, starts_ref):
    images = counts_ref.shape[0]
    total, big, most, first = 0, 0, counts_ref[0], 0
    for m in range(images):
        starts_ref[m] = jnp.int32(total)
        if m:
            better = counts_ref[m] > most
            big = jnp.where(better, m, big)
            first = jnp.where(better, total, first)
            most = jnp.where(better, counts_ref[m], most)
        total = total + counts_ref[m]
    starts_ref[images] = jnp.int32(total)
    return big, first, first + most


def strided(ref, first, count, stride):
    parts = [ref[c, pl.ds(first, count, stride=stride), :] for c in range(ref.shape[0])]
    return jnp.concatenate(parts, axis=1)


def embed_kernel(
    counts_ref, waves_ref, kin_ref, weight_ref, pix_ref, out_ref, sums_ref, table_ref,
    starts_ref, rows_ref, total_ref, keep_ref, acc_ref,
):
    step = pl.program_id(0)
    waves, positions, patches = sums_ref.shape
    images = counts_ref.shape[0]
    per_step = weight_ref.shape[0]
    chunk = pix_ref.shape[0]
    big, big_lo, big_hi = fill_starts(counts_ref, starts_ref)

    @pl.when(step == 0)
    def _():
        total_ref[...] = jnp.zeros_like(total_ref)

    for q in range(per_step):
        row = pl.multiple_of((step * per_step + q) * waves, waves)
        made = jnp.dot(kin_ref[...], weight_ref[q], preferred_element_type=jnp.float32)
        for c in range(rows_ref.shape[0]):
            rows_ref[c, pl.ds(row, waves), :] = made[:, c * LANES : (c + 1) * LANES]
    lo = step * chunk
    hi = lo + chunk
    cut_lo = jnp.clip(big_lo, lo, hi)
    cut_hi = jnp.clip(big_hi, lo, hi)

    def keep(s, carry):
        keep_ref[s] = pix_ref[s - lo]
        return carry

    def gather(s, carry):
        w = waves_ref[s]
        total_ref[w] = total_ref[w] + pix_ref[s - lo].astype(jnp.float32)
        return carry

    lax.fori_loop(lo, cut_lo, keep, 0)
    lax.fori_loop(cut_lo, cut_hi, gather, 0)
    lax.fori_loop(cut_hi, hi, keep, 0)

    @pl.when(step == pl.num_programs(0) - 1)
    def _():
        def turn(w, carry):
            table_ref[w] = strided(rows_ref, w, positions, waves).astype(jnp.bfloat16)
            sums_ref[w] = total_ref[w].astype(jnp.bfloat16)
            return carry

        lax.fori_loop(0, waves, turn, 0)
        over_rows = (((0,), (0,)), ((), ()))

        def product(left, right):
            return lax.dot_general(left, right, over_rows, preferred_element_type=jnp.float32)

        acc_ref[...] = jnp.zeros_like(acc_ref)
        group = 8

        def big_part(j, carry):
            first = pl.multiple_of(j * group, group)
            left = sums_ref[pl.ds(first, group)].reshape(group * positions, patches)
            right = table_ref[pl.ds(first, group)].reshape(group * positions, -1)
            acc_ref[:patches] += product(left, right)
            return carry

        lax.fori_loop(0, waves // group, big_part, 0)
        out_ref[big] = acc_ref[...].astype(jnp.bfloat16)

        def image(m, carry):
            first, last = starts_ref[m], starts_ref[m + 1]

            @pl.when(m != big)
            def _():
                acc_ref[...] = jnp.zeros_like(acc_ref)

                def part(j, carry):
                    lefts, rights = [], []
                    for k in range(QUAD):
                        s = first + j * QUAD + k
                        here = jnp.minimum(s, last - 1)
                        factor = jnp.where(s < last, 1.0, 0.0).astype(jnp.bfloat16)
                        lefts.append(keep_ref[here] * factor)
                        rights.append(table_ref[waves_ref[here]])
                    acc_ref[:patches] += product(
                        jnp.concatenate(lefts, axis=0), jnp.concatenate(rights, axis=0)
                    )
                    return carry

                lax.fori_loop(0, (last - first + QUAD - 1) // QUAD, part, 0)
                out_ref[m] = acc_ref[...].astype(jnp.bfloat16)

            return carry

        lax.fori_loop(0, images, image, 0)


def embed_call(counts, band_waves, kernel_low, kernel_weight, pixels):
    slots, positions, patches = pixels.shape
    waves = kernel_low.shape[0]
    depth, width = kernel_weight.shape[1:]
    images = counts.shape[0]
    padded = pad_rows(patches)
    smem = pl.BlockSpec(memory_space=pltpu.SMEM)
    return pl.pallas_call(
        embed_kernel,
        grid=(STEPS,),
        in_specs=[
            smem,
            smem,
            pl.BlockSpec((waves, depth), lambda i: (0, 0)),
            pl.BlockSpec((positions // STEPS, depth, width), lambda i: (i, 0, 0)),
            pl.BlockSpec((slots // STEPS, positions, patches), lambda i: (i, 0, 0)),
        ],
        out_specs=[
            pl.BlockSpec((images, padded, width), lambda i: (0, 0, 0)),
            pl.BlockSpec((waves, positions, patches), lambda i: (0, 0, 0)),
            pl.BlockSpec((waves, positions, width), lambda i: (0, 0, 0)),
        ],
        out_shape=[
            jax.ShapeDtypeStruct((images, padded, width), jnp.bfloat16),
            jax.ShapeDtypeStruct((waves, positions, patches), jnp.bfloat16),
            jax.ShapeDtypeStruct((waves, positions, width), jnp.bfloat16),
        ],
        scratch_shapes=[
            pltpu.SMEM((images + 1,), jnp.int32),
            pltpu.VMEM((width // LANES, positions * waves, LANES), jnp.float32),
            pltpu.VMEM((waves, positions, patches), jnp.float32),
            pltpu.VMEM((slots, positions, patches), jnp.bfloat16),
            pltpu.VMEM((padded, width), jnp.float32),
        ],
        compiler_params=pltpu.CompilerParams(vmem_limit_bytes=VMEM_LIMIT),
        name="embed",
    )(counts, band_waves, kernel_low, kernel_weight, pixels)


def embed_back_kernel(
    counts_ref, waves_ref, grad_ref, table_ref, sums_ref, pix_ref, weight_ref,
    pix_grad_ref, kernel_grad_ref, in_grad_ref,
    starts_ref, owner_ref, wide_ref, big_ref,
):
    step = pl.program_id(0)
    waves, positions, patches = sums_ref.shape
    images = counts_ref.shape[0]
    width = table_ref.shape[2]
    chunk = pix_ref.shape[0]
    slot_steps = waves_ref.shape[0] // chunk
    big, big_lo, big_hi = fill_starts(counts_ref, starts_ref)
    over_width = (((1,), (1,)), ((), ()))

    @pl.when(step == 0)
    def _():
        for m in range(images):
            def own(s, carry, m=m):
                owner_ref[s] = jnp.int32(m)
                return carry

            lax.fori_loop(starts_ref[m], starts_ref[m + 1], own, 0)
        group = 8
        slope = grad_ref[big]

        def big_part(j, carry):
            first = pl.multiple_of(j * group, group)
            rows = pl.ds(pl.multiple_of(j * group * positions, group * positions), group * positions)
            left = table_ref[pl.ds(first, group)].reshape(group * positions, width)
            both = lax.dot_general(left, slope, over_width, preferred_element_type=jnp.float32)
            big_ref[pl.ds(first, group)] = (
                both[:, :patches].astype(jnp.bfloat16).reshape(group, positions, patches)
            )
            left = sums_ref[pl.ds(first, group)].reshape(group * positions, patches)
            made = jnp.dot(left, slope[:patches], preferred_element_type=jnp.float32)
            for c in range(wide_ref.shape[0]):
                wide_ref[c, rows, :] = made[:, c * LANES : (c + 1) * LANES]
            return carry

        lax.fori_loop(0, waves // group, big_part, 0)

    @pl.when(step < slot_steps)
    def _():
        lo = step * chunk
        hi = lo + chunk
        cut_lo = jnp.clip(big_lo, lo, hi)
        cut_hi = jnp.clip(big_hi, lo, hi)

        def copy(s, carry):
            pix_grad_ref[s - lo] = big_ref[waves_ref[s]]
            return carry

        lax.fori_loop(cut_lo, cut_hi, copy, 0)

        def small(end):
            def part(s):
                m = owner_ref[s]
                slope = grad_ref[m]
                last = jnp.minimum(jnp.minimum(starts_ref[m + 1], end), s + QUAD)
                lefts, rights, index = [], [], []
                for k in range(QUAD):
                    here = jnp.minimum(s + k, last - 1)
                    factor = jnp.where(s + k < last, 1.0, 0.0).astype(jnp.bfloat16)
                    index.append(here)
                    lefts.append(table_ref[waves_ref[here]])
                    rights.append(pix_ref[here - lo] * factor)
                both = lax.dot_general(
                    jnp.concatenate(lefts, axis=0),
                    slope,
                    over_width,
                    preferred_element_type=jnp.float32,
                )[:, :patches].astype(jnp.bfloat16)
                more = jnp.dot(
                    jnp.concatenate(rights, axis=0),
                    slope[:patches],
                    preferred_element_type=jnp.float32,
                )
                for k in range(QUAD):
                    part_rows = slice(k * positions, (k + 1) * positions)
                    pix_grad_ref[index[k] - lo] = both[part_rows]
                    row = pl.multiple_of(waves_ref[index[k]] * positions, positions)
                    for c in range(wide_ref.shape[0]):
                        wide_ref[c, pl.ds(row, positions), :] += more[
                            part_rows, c * LANES : (c + 1) * LANES
                        ]
                return last

            return part

        lax.while_loop(lambda s: s < cut_lo, small(cut_lo), lo)
        lax.while_loop(lambda s: s < hi, small(hi), cut_hi)

    @pl.when(step == slot_steps)
    def _():
        in_grad_ref[...] = jnp.zeros_like(in_grad_ref)

    @pl.when(step >= slot_steps)
    def _():
        per_step = weight_ref.shape[0]
        found = jnp.zeros(in_grad_ref.shape, jnp.float32)
        for q in range(per_step):
            place = (step - slot_steps) * per_step + q
            rows = strided(wide_ref, place, waves, positions)
            high = rows.astype(jnp.bfloat16)
            kernel_grad_ref[q] = high
            rest = (rows - high.astype(jnp.float32)).astype(jnp.bfloat16)
            both = lax.dot_general(
                jnp.concatenate([high, rest], axis=0),
                weight_ref[q],
                over_width,
                preferred_element_type=jnp.float32,
            )
            found = found + (both[:waves] + both[waves:])
        in_grad_ref[...] += found


def embed_back_call(counts, band_waves, grads, table, sums, pixels, kernel_weight):
    slots, positions, patches = pixels.shape
    waves = table.shape[0]
    depth, width = kernel_weight.shape[1:]
    images, padded = grads.shape[:2]
    smem = pl.BlockSpec(memory_space=pltpu.SMEM)
    slot_block = (slots // STEPS, positions, patches)
    weight_block = (positions // STEPS, depth, width)

    def early(i):
        return (jnp.minimum(i, STEPS - 1), 0, 0)

    def late(i):
        return (jnp.maximum(i - STEPS, 0), 0, 0)

    return pl.pallas_call(
        embed_back_kernel,
        grid=(2 * STEPS,),
        in_specs=[
            smem,
            smem,
            pl.BlockSpec((images, padded, width), lambda i: (0, 0, 0)),
            pl.BlockSpec((waves, positions, width), lambda i: (0, 0, 0)),
            pl.BlockSpec((waves, positions, patches), lambda i: (0, 0, 0)),
            pl.BlockSpec(slot_block, early),
            pl.BlockSpec(weight_block, late),
        ],
        out_specs=[
            pl.BlockSpec(slot_block, early),
            pl.BlockSpec((positions // STEPS, waves, width), late),
            pl.BlockSpec((waves, depth), lambda i: (0, 0)),
        ],
        out_shape=[
            jax.ShapeDtypeStruct((slots, positions, patches), jnp.bfloat16),
            jax.ShapeDtypeStruct((positions, waves, width), jnp.bfloat16),
            jax.ShapeDtypeStruct((waves, depth), jnp.float32),
        ],
        scratch_shapes=[
            pltpu.SMEM((images + 1,), jnp.int32),
            pltpu.SMEM((slots,), jnp.int32),
            pltpu.VMEM((width // LANES, waves * positions, LANES), jnp.float32),
            pltpu.VMEM((waves, positions, patches), jnp.bfloat16),
        ],
        compiler_params=pltpu.CompilerParams(vmem_limit_bytes=VMEM_LIMIT),
        name="embed_back",
    )(counts, band_waves, grads, table, sums, pixels, kernel_weight)


HEADS = 12
WD = 128
WHEADS = 4


highest = lax.Precision.HIGHEST


def matmul_high(left, right):
    return jnp.dot(left, right, precision=highest, preferred_element_type=jnp.float32)


def layer_norm(values, norm_gain, norm_shift, epsilon):
    centered = values - jnp.mean(values, axis=-1, keepdims=True)
    variance = jnp.mean(centered * centered, axis=-1, keepdims=True)
    return centered * lax.rsqrt(variance + epsilon) * norm_gain + norm_shift


def block_norm(values, norm_gain, norm_shift):
    return layer_norm(values, norm_gain, norm_shift, 1e-06)


def exact_gelu(values):
    return jax.nn.gelu(values, approximate=False)


def wave_embed(wavelengths):
    halfwidth = WD // 2
    indices = jnp.arange(halfwidth, dtype=jnp.float32)
    frequency = 1.0 / 10000.0 ** (indices / halfwidth)
    angles = (wavelengths * 1000.0)[:, None] * frequency[None, :]
    return jnp.concatenate([jnp.sin(angles), jnp.cos(angles)], axis=1)


def hypernet(embedded, params):
    (
        bias_token,
        wave_qkv,
        wave_proj,
        wave_gain,
        wave_shift,
        wave_up,
        wave_down,
        kernel_gain,
        kernel_shift,
        bias_head,
    ) = params
    sequence = jnp.concatenate([embedded, bias_token[None, :]], axis=0)
    length = sequence.shape[0]
    head_width = WD // WHEADS
    projected = matmul_high(sequence, wave_qkv).reshape(length, 3, WHEADS, head_width)
    scores = jnp.einsum(
        "qhd,khd->hqk", projected[:, 0], projected[:, 1], precision=highest
    ) / math.sqrt(head_width)
    weights = jax.nn.softmax(scores, axis=-1)
    attended = jnp.einsum("hqk,khd->qhd", weights, projected[:, 2], precision=highest).reshape(
        length, WD
    )
    normed_first = layer_norm(
        sequence + matmul_high(attended, wave_proj), wave_gain, wave_shift, 1e-05
    )
    widened = jax.nn.gelu(matmul_high(normed_first, wave_up), approximate=False)
    second = layer_norm(
        normed_first + matmul_high(widened, wave_down), kernel_gain, kernel_shift, 1e-05
    )
    return (second[:-1] + embedded, matmul_high(second[-1:], bias_head)[0])


def swap_core(array):
    return lax.ppermute(array, "rows", [(0, 1), (1, 0), (2, 3), (3, 2)])


def swap_chip(array):
    return lax.ppermute(array, "rows", [(0, 2), (2, 0), (1, 3), (3, 1)])


def add_wide(left, right):
    return left.astype(jnp.float32) + right.astype(jnp.float32)


def rows_reduce(partial_rows):
    place = lax.axis_index("rows")
    chip, core = place // 2, place % 2
    images = partial_rows.shape[0] // 4

    def block(which_chip, which_core):
        return lax.dynamic_slice_in_dim(
            partial_rows, (which_chip * 2 + which_core) * images, images, 0
        )

    far = add_wide(block(1 - chip, core), swap_core(block(1 - chip, 1 - core)))
    near = add_wide(block(chip, core), swap_core(block(chip, 1 - core)))
    return near + swap_chip(far.astype(jnp.bfloat16)).astype(jnp.float32)


def rows_gather(own):
    place = lax.axis_index("rows")
    chip, core = place // 2, place % 2
    near = swap_core(own)
    across = swap_chip(own)
    far = swap_core(across)

    def by_core(mine, other):
        return jnp.concatenate(
            [jnp.where(core == 0, mine, other), jnp.where(core == 0, other, mine)], axis=0
        )

    here, there = by_core(own, near), by_core(across, far)
    return jnp.concatenate(
        [jnp.where(chip == 0, here, there), jnp.where(chip == 0, there, here)], axis=0
    )


def weight_reduce(grad):
    core = lax.axis_index("rows") % 2
    half = grad.shape[1] // 2
    low = grad.astype(jnp.bfloat16)
    kept = lax.dynamic_slice_in_dim(low, core * half, half, 1)
    sent = lax.dynamic_slice_in_dim(low, (1 - core) * half, half, 1)
    pair = add_wide(kept, swap_core(sent)).astype(jnp.bfloat16)
    part = lax.psum_scatter(pair, "band", scatter_dimension=0, tiled=True)
    whole = add_wide(part, swap_chip(part)).astype(jnp.bfloat16)
    other = swap_core(whole)
    return jnp.where(
        core == 0,
        jnp.concatenate([whole, other], axis=1),
        jnp.concatenate([other, whole], axis=1),
    ).astype(jnp.float32)


def slot_masks(counts, slot_waves, waves):
    index = jnp.arange(counts.shape[0])
    ends = jnp.sum(jnp.where(index[None, :] <= index[:, None], counts[None, :], 0), axis=1)
    slots = jnp.arange(slot_waves.shape[0])
    owners = jnp.sum((ends[None, :] <= slots[:, None]).astype(jnp.int32), axis=1)
    return (
        (owners[:, None] == index[None, :]).astype(jnp.bfloat16),
        (slot_waves[:, None] == jnp.arange(waves)[None, :]).astype(jnp.bfloat16),
    )


def embed_plain(counts, slot_waves, kernel_low, kernel_weight, pixels):
    slots, positions, patches = pixels.shape
    table = jnp.einsum(
        "wk,qkc->wqc", kernel_low, kernel_weight, preferred_element_type=jnp.float32
    ).astype(jnp.bfloat16)
    of_image, of_wave = slot_masks(counts, slot_waves, table.shape[0])
    chunk = min(16, slots)

    def part(running, inputs):
        pixel, image, wave = inputs
        chosen = jnp.einsum("sw,wqc->sqc", wave, table)
        rows = jnp.einsum("sqp,sqc->spc", pixel, chosen, preferred_element_type=jnp.float32)
        image = image.astype(jnp.float32)
        return (running + jnp.einsum("si,spc->ipc", image, rows, precision=highest), None)

    shape = (counts.shape[0], patches, table.shape[2])
    total = lax.scan(
        part,
        jnp.zeros(shape, jnp.float32),
        tuple(a.reshape(-1, chunk, *a.shape[1:]) for a in (pixels, of_image, of_wave)),
    )[0]
    extra = pad_rows(patches) - patches
    return (jnp.pad(total.astype(jnp.bfloat16), ((0, 0), (0, extra), (0, 0))), table)


def embed_back_plain(counts, slot_waves, grads, table, pixels, kernel_weight):
    slots, positions, patches = pixels.shape
    waves, _, width = table.shape
    of_image, of_wave = slot_masks(counts, slot_waves, waves)
    grads = grads[:, :patches]
    chunk = min(16, slots)

    def part(running, inputs):
        pixel, image, wave = inputs
        chosen = jnp.einsum("sw,wqc->sqc", wave, table)
        slope = jnp.einsum("si,ipc->spc", image, grads)
        own = jnp.einsum("sqc,spc->sqp", chosen, slope, preferred_element_type=jnp.float32)
        more = jnp.einsum("sqp,spc->sqc", pixel, slope, preferred_element_type=jnp.float32)
        wave = wave.astype(jnp.float32)
        added = jnp.einsum("sw,sqc->qwc", wave, more, precision=highest)
        return (running + added, own.astype(jnp.bfloat16))

    kernel_grad, pixel_grad = lax.scan(
        part,
        jnp.zeros((positions, waves, width), jnp.float32),
        tuple(a.reshape(-1, chunk, *a.shape[1:]) for a in (pixels, of_image, of_wave)),
    )
    in_part = jnp.einsum(
        "qwc,qkc->wk",
        kernel_grad,
        kernel_weight.astype(jnp.float32),
        precision=highest,
        preferred_element_type=jnp.float32,
    )
    return (pixel_grad.reshape(pixels.shape), kernel_grad.astype(jnp.bfloat16), in_part)


def body(
    pixels,
    band_counts,
    band_waves,
    wavelengths,
    bias_token,
    wave_qkv,
    wave_proj,
    wave_gain,
    wave_shift,
    wave_up,
    wave_down,
    kernel_gain,
    kernel_shift,
    bias_head,
    kernel_weight,
    attention_gain,
    attention_shift,
    block_qkv,
    block_proj,
    hidden_gain,
    hidden_shift,
    block_up,
    block_down,
    cotangent,
):
    embedded = wave_embed(wavelengths)
    hyper_params = (
        bias_token,
        wave_qkv,
        wave_proj,
        wave_gain,
        wave_shift,
        wave_up,
        wave_down,
        kernel_gain,
        kernel_shift,
        bias_head,
    )

    def hyper_apply(params):
        return hypernet(embedded, params)

    (kernel_in, conv_bias), hyper_back = jax.vjp(hyper_apply, hyper_params)
    kernel_low = kernel_in.astype(jnp.bfloat16)
    counts = band_counts[0]
    slot_waves = band_waves[0]
    slot_total, positions, patches = pixels.shape
    images = counts.shape[0]
    waves, width = kernel_low.shape[0], kernel_weight.shape[2]
    fits = waves * positions * width <= 1 << 21
    if fits:
        partial_rows, wave_sums, kernel_table = embed_call(
            counts, slot_waves, kernel_low, kernel_weight, pixels
        )
    else:
        partial_rows, kernel_table = embed_plain(
            counts, slot_waves, kernel_low, kernel_weight, pixels
        )
    embedded_rows = (
        rows_reduce(partial_rows)[:, :patches].reshape(-1, width) + conv_bias
    )
    row_count = embedded_rows.shape[0]
    local_images = row_count // patches
    head_size = width // HEADS
    divisor = math.sqrt(head_size)
    normed_in, norm_in_back = jax.vjp(block_norm, embedded_rows, attention_gain, attention_shift)
    normed_low = normed_in.astype(jnp.bfloat16)
    projected = jnp.dot(normed_low, block_qkv, preferred_element_type=jnp.float32).astype(
        jnp.bfloat16
    )
    heads_view = projected.reshape(local_images, patches, 3, HEADS, head_size)
    queries = heads_view[:, :, 0]
    keys_all = heads_view[:, :, 1]
    values_all = heads_view[:, :, 2]
    scores = (
        jnp.einsum("iqhd,ikhd->ihqk", queries, keys_all, preferred_element_type=jnp.float32)
        / divisor
    )
    log_total = jax.nn.logsumexp(scores, axis=-1, keepdims=True)
    probs_low = jnp.exp(scores - log_total).astype(jnp.bfloat16)
    mixed_low = (
        jnp.einsum("ihqk,ikhd->iqhd", probs_low, values_all, preferred_element_type=jnp.float32)
        .reshape(row_count, width)
        .astype(jnp.bfloat16)
    )
    middle = embedded_rows + jnp.dot(mixed_low, block_proj, preferred_element_type=jnp.float32)
    normed_mid, norm_mid_back = jax.vjp(block_norm, middle, hidden_gain, hidden_shift)
    mid_low = normed_mid.astype(jnp.bfloat16)
    upward = jnp.dot(mid_low, block_up, preferred_element_type=jnp.float32)
    activated, gelu_back = jax.vjp(exact_gelu, upward)
    activated_low = activated.astype(jnp.bfloat16)
    result = middle + jnp.dot(activated_low, block_down, preferred_element_type=jnp.float32)
    layer_output = result.astype(jnp.bfloat16)
    down_grad = jnp.einsum(
        "rf,rd->fd", activated_low, cotangent, preferred_element_type=jnp.float32
    )
    grad_activated = jnp.einsum(
        "rd,fd->rf", cotangent, block_down, preferred_element_type=jnp.float32
    )
    grad_up = gelu_back(grad_activated)[0].astype(jnp.bfloat16)
    up_grad = jnp.einsum("rd,rf->df", mid_low, grad_up, preferred_element_type=jnp.float32)
    grad_normed_mid = jnp.einsum("rf,df->rd", grad_up, block_up, preferred_element_type=jnp.float32)
    grad_mid_norm, hidden_gain_part, hidden_shift_part = norm_mid_back(grad_normed_mid)
    grad_middle = cotangent.astype(jnp.float32) + grad_mid_norm
    grad_attended = grad_middle.astype(jnp.bfloat16)
    proj_grad = jnp.einsum(
        "re,rd->ed", mixed_low, grad_attended, preferred_element_type=jnp.float32
    )
    grad_mixed = jnp.einsum(
        "rd,ed->re", grad_attended, block_proj, preferred_element_type=jnp.float32
    ).astype(jnp.bfloat16)
    grad_mixed_heads = grad_mixed.reshape(local_images, patches, HEADS, head_size)
    again = (
        jnp.einsum("iqhd,ikhd->ihqk", queries, keys_all, preferred_element_type=jnp.float32)
        / divisor
    )
    probs_again = jnp.exp(again - log_total)
    grad_probs = jnp.einsum(
        "iqhd,ikhd->ihqk", grad_mixed_heads, values_all, preferred_element_type=jnp.float32
    )
    grad_values = jnp.einsum(
        "ihqk,iqhd->ikhd",
        probs_again.astype(jnp.bfloat16),
        grad_mixed_heads,
        preferred_element_type=jnp.float32,
    )
    grad_scores = (
        probs_again * (grad_probs - jnp.sum(grad_probs * probs_again, axis=-1, keepdims=True))
    ).astype(jnp.bfloat16)
    grad_queries = (
        jnp.einsum("ihqk,ikhd->iqhd", grad_scores, keys_all, preferred_element_type=jnp.float32)
        / divisor
    )
    grad_keys = (
        jnp.einsum("ihqk,iqhd->ikhd", grad_scores, queries, preferred_element_type=jnp.float32)
        / divisor
    )
    grad_projected = (
        jnp.stack([grad_queries, grad_keys, grad_values], axis=2)
        .reshape(row_count, 3 * width)
        .astype(jnp.bfloat16)
    )
    qkv_grad = jnp.einsum(
        "rd,re->de", normed_low, grad_projected, preferred_element_type=jnp.float32
    )
    grad_normed_in = jnp.einsum(
        "re,de->rd", grad_projected, block_qkv, preferred_element_type=jnp.float32
    )
    grad_in_norm, attention_gain_part, attention_shift_part = norm_in_back(grad_normed_in)
    grad_embedded = grad_middle + grad_in_norm
    grad_rows = jnp.pad(
        grad_embedded.astype(jnp.bfloat16).reshape(local_images, patches, width),
        ((0, 0), (0, pad_rows(patches) - patches), (0, 0)),
    )
    gathered = rows_gather(grad_rows)
    block_down_grad = weight_reduce(down_grad)
    block_up_grad = weight_reduce(up_grad)
    block_proj_grad = weight_reduce(proj_grad)
    block_qkv_grad = weight_reduce(qkv_grad)
    if fits:
        pixel_grad, kernel_grad, in_part = embed_back_call(
            counts, slot_waves, gathered, kernel_table, wave_sums, pixels, kernel_weight
        )
    else:
        pixel_grad, kernel_grad, in_part = embed_back_plain(
            counts, slot_waves, gathered, kernel_table, pixels, kernel_weight
        )
    vectors = jnp.stack(
        [
            jnp.sum(grad_embedded, axis=0),
            attention_gain_part,
            attention_shift_part,
            hidden_gain_part,
            hidden_shift_part,
        ]
    )
    summed = lax.psum(
        jnp.concatenate([in_part, vectors.reshape(-1, in_part.shape[1])], axis=0),
        ("band", "rows"),
    )
    grad_kernel_in = summed[:waves]
    bias_grad, attention_gain_grad, attention_shift_grad, hidden_gain_grad, hidden_shift_grad = (
        summed[waves:].reshape(5, width)
    )
    owned = lax.psum_scatter(kernel_grad, "band", scatter_dimension=0, tiled=True)
    owned_weight = jnp.einsum(
        "wk,qwc->qkc", kernel_low, owned, preferred_element_type=jnp.float32
    ).astype(jnp.bfloat16)
    kernel_weight_grad = lax.all_to_all(
        owned_weight, "band", split_axis=1, concat_axis=0, tiled=True
    ).astype(jnp.float32)
    hyper_grads = hyper_back((grad_kernel_in, bias_grad))[0]
    return (
        layer_output,
        pixel_grad,
        kernel_weight_grad,
        hyper_grads[0],
        hyper_grads[1],
        hyper_grads[2],
        hyper_grads[3],
        hyper_grads[4],
        hyper_grads[5],
        hyper_grads[6],
        hyper_grads[7],
        hyper_grads[8],
        hyper_grads[9],
        attention_gain_grad,
        attention_shift_grad,
        block_qkv_grad,
        block_proj_grad,
        hidden_gain_grad,
        hidden_shift_grad,
        block_up_grad,
        block_down_grad,
    )


def solution(mesh):
    in_specs = (
        P("band", "rows", None),
        P("band", None),
        P("band", None),
        P(),
        P(),
        P(),
        P(),
        P(),
        P(),
        P(),
        P(),
        P(),
        P(),
        P(),
        P("rows", None, None),
        P(),
        P(),
        P(),
        P(),
        P(),
        P(),
        P(),
        P(),
        P(("band", "rows"), None),
    )
    out_specs = (
        P(("band", "rows"), None),
        P("band", "rows", None),
        P("rows", "band", None),
        P(),
        P(),
        P(),
        P(),
        P(),
        P(),
        P(),
        P(),
        P(),
        P(),
        P(),
        P(),
        P("band", None),
        P("band", None),
        P(),
        P(),
        P("band", None),
        P("band", None),
    )
    return jax.shard_map(body, mesh=mesh, in_specs=in_specs, out_specs=out_specs, check_vma=False)
```

```python
import functools
import math

import jax
import jax.numpy as jnp
from jax import lax
from jax.experimental import pallas as pl
from jax.experimental.pallas import tpu as pltpu
from jax.sharding import PartitionSpec as P

VMEM_LIMIT = 60 * 1024 * 1024
STEPS = 8
QUAD = 4
LANES = 128
EPSILON = 1e-06
ROW_STEP = 48


def pad_rows(rows):
    return (rows + 15) // 16 * 16


def fill_starts(counts_ref, starts_ref):
    images = counts_ref.shape[0]
    total, big, most, first = 0, 0, counts_ref[0], 0
    for m in range(images):
        starts_ref[m] = jnp.int32(total)
        if m:
            better = counts_ref[m] > most
            big = jnp.where(better, m, big)
            first = jnp.where(better, total, first)
            most = jnp.where(better, counts_ref[m], most)
        total = total + counts_ref[m]
    starts_ref[images] = jnp.int32(total)
    return big, first, first + most


def strided(ref, first, count, stride):
    parts = [ref[c, pl.ds(first, count, stride=stride), :] for c in range(ref.shape[0])]
    return jnp.concatenate(parts, axis=1)


def embed_kernel(
    counts_ref, waves_ref, kin_ref, weight_ref, pix_ref, out_ref, sums_ref, table_ref,
    starts_ref, rows_ref, total_ref, keep_ref, acc_ref,
):
    step = pl.program_id(0)
    waves, positions, patches = sums_ref.shape
    images = counts_ref.shape[0]
    per_step = weight_ref.shape[0]
    chunk = pix_ref.shape[0]
    big, big_lo, big_hi = fill_starts(counts_ref, starts_ref)

    @pl.when(step == 0)
    def _():
        total_ref[...] = jnp.zeros_like(total_ref)

    for q in range(per_step):
        row = pl.multiple_of((step * per_step + q) * waves, waves)
        made = jnp.dot(kin_ref[...], weight_ref[q], preferred_element_type=jnp.float32)
        for c in range(rows_ref.shape[0]):
            rows_ref[c, pl.ds(row, waves), :] = made[:, c * LANES : (c + 1) * LANES]
    lo = step * chunk
    hi = lo + chunk
    cut_lo = jnp.clip(big_lo, lo, hi)
    cut_hi = jnp.clip(big_hi, lo, hi)

    def keep(s, carry):
        keep_ref[s] = pix_ref[s - lo]
        return carry

    def gather(s, carry):
        w = waves_ref[s]
        total_ref[w] = total_ref[w] + pix_ref[s - lo].astype(jnp.float32)
        return carry

    lax.fori_loop(lo, cut_lo, keep, 0)
    lax.fori_loop(cut_lo, cut_hi, gather, 0)
    lax.fori_loop(cut_hi, hi, keep, 0)

    @pl.when(step == pl.num_programs(0) - 1)
    def _():
        def turn(w, carry):
            table_ref[w] = strided(rows_ref, w, positions, waves).astype(jnp.bfloat16)
            sums_ref[w] = total_ref[w].astype(jnp.bfloat16)
            return carry

        lax.fori_loop(0, waves, turn, 0)
        over_rows = (((0,), (0,)), ((), ()))

        def product(left, right):
            return lax.dot_general(left, right, over_rows, preferred_element_type=jnp.float32)

        acc_ref[...] = jnp.zeros_like(acc_ref)
        group = 8

        def big_part(j, carry):
            first = pl.multiple_of(j * group, group)
            left = sums_ref[pl.ds(first, group)].reshape(group * positions, patches)
            right = table_ref[pl.ds(first, group)].reshape(group * positions, -1)
            acc_ref[:patches] += product(left, right)
            return carry

        lax.fori_loop(0, waves // group, big_part, 0)
        out_ref[big] = acc_ref[...].astype(jnp.bfloat16)

        def image(m, carry):
            first, last = starts_ref[m], starts_ref[m + 1]

            @pl.when(m != big)
            def _():
                acc_ref[...] = jnp.zeros_like(acc_ref)

                def part(j, carry):
                    lefts, rights = [], []
                    for k in range(QUAD):
                        s = first + j * QUAD + k
                        here = jnp.minimum(s, last - 1)
                        factor = jnp.where(s < last, 1.0, 0.0).astype(jnp.bfloat16)
                        lefts.append(keep_ref[here] * factor)
                        rights.append(table_ref[waves_ref[here]])
                    acc_ref[:patches] += product(
                        jnp.concatenate(lefts, axis=0), jnp.concatenate(rights, axis=0)
                    )
                    return carry

                lax.fori_loop(0, (last - first + QUAD - 1) // QUAD, part, 0)
                out_ref[m] = acc_ref[...].astype(jnp.bfloat16)

            return carry

        lax.fori_loop(0, images, image, 0)


def embed_call(counts, band_waves, kernel_low, kernel_weight, pixels):
    slots, positions, patches = pixels.shape
    waves = kernel_low.shape[0]
    depth, width = kernel_weight.shape[1:]
    images = counts.shape[0]
    padded = pad_rows(patches)
    smem = pl.BlockSpec(memory_space=pltpu.SMEM)
    return pl.pallas_call(
        embed_kernel,
        grid=(STEPS,),
        in_specs=[
            smem,
            smem,
            pl.BlockSpec((waves, depth), lambda i: (0, 0)),
            pl.BlockSpec((positions // STEPS, depth, width), lambda i: (i, 0, 0)),
            pl.BlockSpec((slots // STEPS, positions, patches), lambda i: (i, 0, 0)),
        ],
        out_specs=[
            pl.BlockSpec((images, padded, width), lambda i: (0, 0, 0)),
            pl.BlockSpec((waves, positions, patches), lambda i: (0, 0, 0)),
            pl.BlockSpec((waves, positions, width), lambda i: (0, 0, 0)),
        ],
        out_shape=[
            jax.ShapeDtypeStruct((images, padded, width), jnp.bfloat16),
            jax.ShapeDtypeStruct((waves, positions, patches), jnp.bfloat16),
            jax.ShapeDtypeStruct((waves, positions, width), jnp.bfloat16),
        ],
        scratch_shapes=[
            pltpu.SMEM((images + 1,), jnp.int32),
            pltpu.VMEM((width // LANES, positions * waves, LANES), jnp.float32),
            pltpu.VMEM((waves, positions, patches), jnp.float32),
            pltpu.VMEM((slots, positions, patches), jnp.bfloat16),
            pltpu.VMEM((padded, width), jnp.float32),
        ],
        compiler_params=pltpu.CompilerParams(vmem_limit_bytes=VMEM_LIMIT),
        name="embed",
    )(counts, band_waves, kernel_low, kernel_weight, pixels)


def embed_back_kernel(
    counts_ref, waves_ref, grad_ref, table_ref, sums_ref, pix_ref, weight_ref,
    pix_grad_ref, kernel_grad_ref, in_grad_ref,
    starts_ref, owner_ref, wide_ref, big_ref,
):
    step = pl.program_id(0)
    waves, positions, patches = sums_ref.shape
    images = counts_ref.shape[0]
    width = table_ref.shape[2]
    chunk = pix_ref.shape[0]
    slot_steps = waves_ref.shape[0] // chunk
    big, big_lo, big_hi = fill_starts(counts_ref, starts_ref)
    over_width = (((1,), (1,)), ((), ()))

    @pl.when(step == 0)
    def _():
        for m in range(images):
            def own(s, carry, m=m):
                owner_ref[s] = jnp.int32(m)
                return carry

            lax.fori_loop(starts_ref[m], starts_ref[m + 1], own, 0)
        group = 8
        slope = grad_ref[big]

        def big_part(j, carry):
            first = pl.multiple_of(j * group, group)
            rows = pl.ds(pl.multiple_of(j * group * positions, group * positions), group * positions)
            left = table_ref[pl.ds(first, group)].reshape(group * positions, width)
            both = lax.dot_general(left, slope, over_width, preferred_element_type=jnp.float32)
            big_ref[pl.ds(first, group)] = (
                both[:, :patches].astype(jnp.bfloat16).reshape(group, positions, patches)
            )
            left = sums_ref[pl.ds(first, group)].reshape(group * positions, patches)
            made = jnp.dot(left, slope[:patches], preferred_element_type=jnp.float32)
            for c in range(wide_ref.shape[0]):
                wide_ref[c, rows, :] = made[:, c * LANES : (c + 1) * LANES]
            return carry

        lax.fori_loop(0, waves // group, big_part, 0)

    @pl.when(step < slot_steps)
    def _():
        lo = step * chunk
        hi = lo + chunk
        cut_lo = jnp.clip(big_lo, lo, hi)
        cut_hi = jnp.clip(big_hi, lo, hi)

        def copy(s, carry):
            pix_grad_ref[s - lo] = big_ref[waves_ref[s]]
            return carry

        lax.fori_loop(cut_lo, cut_hi, copy, 0)

        def small(end):
            def part(s):
                m = owner_ref[s]
                slope = grad_ref[m]
                last = jnp.minimum(jnp.minimum(starts_ref[m + 1], end), s + QUAD)
                lefts, rights, index = [], [], []
                for k in range(QUAD):
                    here = jnp.minimum(s + k, last - 1)
                    factor = jnp.where(s + k < last, 1.0, 0.0).astype(jnp.bfloat16)
                    index.append(here)
                    lefts.append(table_ref[waves_ref[here]])
                    rights.append(pix_ref[here - lo] * factor)
                both = lax.dot_general(
                    jnp.concatenate(lefts, axis=0),
                    slope,
                    over_width,
                    preferred_element_type=jnp.float32,
                )[:, :patches].astype(jnp.bfloat16)
                more = jnp.dot(
                    jnp.concatenate(rights, axis=0),
                    slope[:patches],
                    preferred_element_type=jnp.float32,
                )
                for k in range(QUAD):
                    part_rows = slice(k * positions, (k + 1) * positions)
                    pix_grad_ref[index[k] - lo] = both[part_rows]
                    row = pl.multiple_of(waves_ref[index[k]] * positions, positions)
                    for c in range(wide_ref.shape[0]):
                        wide_ref[c, pl.ds(row, positions), :] += more[
                            part_rows, c * LANES : (c + 1) * LANES
                        ]
                return last

            return part

        lax.while_loop(lambda s: s < cut_lo, small(cut_lo), lo)
        lax.while_loop(lambda s: s < hi, small(hi), cut_hi)

    @pl.when(step == slot_steps)
    def _():
        in_grad_ref[...] = jnp.zeros_like(in_grad_ref)

    @pl.when(step >= slot_steps)
    def _():
        per_step = weight_ref.shape[0]
        found = jnp.zeros(in_grad_ref.shape, jnp.float32)
        for q in range(per_step):
            place = (step - slot_steps) * per_step + q
            rows = strided(wide_ref, place, waves, positions)
            high = rows.astype(jnp.bfloat16)
            kernel_grad_ref[q] = high
            rest = (rows - high.astype(jnp.float32)).astype(jnp.bfloat16)
            both = lax.dot_general(
                jnp.concatenate([high, rest], axis=0),
                weight_ref[q],
                over_width,
                preferred_element_type=jnp.float32,
            )
            found = found + (both[:waves] + both[waves:])
        in_grad_ref[...] += found


def embed_back_call(counts, band_waves, grads, table, sums, pixels, kernel_weight):
    slots, positions, patches = pixels.shape
    waves = table.shape[0]
    depth, width = kernel_weight.shape[1:]
    images, padded = grads.shape[:2]
    smem = pl.BlockSpec(memory_space=pltpu.SMEM)
    slot_block = (slots // STEPS, positions, patches)
    weight_block = (positions // STEPS, depth, width)

    def early(i):
        return (jnp.minimum(i, STEPS - 1), 0, 0)

    def late(i):
        return (jnp.maximum(i - STEPS, 0), 0, 0)

    return pl.pallas_call(
        embed_back_kernel,
        grid=(2 * STEPS,),
        in_specs=[
            smem,
            smem,
            pl.BlockSpec((images, padded, width), lambda i: (0, 0, 0)),
            pl.BlockSpec((waves, positions, width), lambda i: (0, 0, 0)),
            pl.BlockSpec((waves, positions, patches), lambda i: (0, 0, 0)),
            pl.BlockSpec(slot_block, early),
            pl.BlockSpec(weight_block, late),
        ],
        out_specs=[
            pl.BlockSpec(slot_block, early),
            pl.BlockSpec((positions // STEPS, waves, width), late),
            pl.BlockSpec((waves, depth), lambda i: (0, 0)),
        ],
        out_shape=[
            jax.ShapeDtypeStruct((slots, positions, patches), jnp.bfloat16),
            jax.ShapeDtypeStruct((positions, waves, width), jnp.bfloat16),
            jax.ShapeDtypeStruct((waves, depth), jnp.float32),
        ],
        scratch_shapes=[
            pltpu.SMEM((images + 1,), jnp.int32),
            pltpu.SMEM((slots,), jnp.int32),
            pltpu.VMEM((width // LANES, waves * positions, LANES), jnp.float32),
            pltpu.VMEM((waves, positions, patches), jnp.bfloat16),
        ],
        compiler_params=pltpu.CompilerParams(vmem_limit_bytes=VMEM_LIMIT),
        name="embed_back",
    )(counts, band_waves, grads, table, sums, pixels, kernel_weight)


over_last = (((1,), (1,)), ((), ()))
over_first = (((0,), (0,)), ((), ()))


def times(left, right):
    return jnp.dot(left, right, preferred_element_type=jnp.float32)


def times_turned(left, right):
    return lax.dot_general(left, right, over_last, preferred_element_type=jnp.float32)


def turned_times(left, right):
    return lax.dot_general(left, right, over_first, preferred_element_type=jnp.float32)


def norm_parts(values):
    centered = values - jnp.mean(values, axis=-1, keepdims=True)
    variance = jnp.mean(centered * centered, axis=-1, keepdims=True)
    scale = lax.rsqrt(variance + EPSILON)
    return centered * scale, scale


def norm_backward(values, slope, gain):
    unit, scale = norm_parts(values)
    inner = slope * gain
    mean = jnp.mean(inner, axis=-1, keepdims=True)
    along = jnp.mean(inner * unit, axis=-1, keepdims=True)
    return scale * (inner - mean - unit * along), slope * unit


def by_rows(total, fn):
    def part(i, carry):
        fn(pl.ds(pl.multiple_of(i * ROW_STEP, ROW_STEP), ROW_STEP))
        return carry

    lax.fori_loop(0, total // ROW_STEP, part, 0)


def attend_kernel(
    near_ref, far_ref, bias_ref, gain_ref, shift_ref, qkv_ref, proj_ref, mid_gain_ref, mid_shift_ref,
    x_ref, normed_ref, projected_ref, probs_ref, mixed_ref, middle_ref, normed_mid_ref,
    *, padded, patches,
):
    rows, width = x_ref.shape
    head = width // HEADS
    images, pairs = rows // padded, HEADS // 2

    def first(r):
        x = near_ref[r, :] + far_ref[r, :].astype(jnp.float32) + bias_ref[...]
        x_ref[r, :] = x
        normed_ref[r, :] = (norm_parts(x)[0] * gain_ref[...] + shift_ref[...]).astype(jnp.bfloat16)

    by_rows(rows, first)
    for part in range(3):
        columns = slice(part * width, (part + 1) * width)
        projected_ref[:, columns] = times(normed_ref[...], qkv_ref[:, columns]).astype(jnp.bfloat16)
    lane = lax.broadcasted_iota(jnp.int32, (padded, LANES), 1)
    key = lax.broadcasted_iota(jnp.int32, (padded, padded), 1)
    factor = jnp.bfloat16(1.0 / math.sqrt(head))

    def pair_of(index, carry):
        image, pair = index // pairs, index % pairs
        r = pl.ds(pl.multiple_of(image * padded, padded), padded)

        def columns(part):
            return pl.ds(pl.multiple_of(part * width + pair * LANES, LANES), LANES)

        queries, keys, values = (projected_ref[r, columns(part)] for part in range(3))
        found = []
        for h in range(2):
            mine = (lane // head) == h
            scores = times_turned(jnp.where(mine, queries * factor, jnp.zeros_like(queries)), keys)
            scores = jnp.where(key < patches, scores, -1e30)
            raised = jnp.exp(scores - jnp.max(scores, axis=-1, keepdims=True))
            probs = raised * (1.0 / jnp.sum(raised, axis=-1, keepdims=True))
            low = probs.astype(jnp.bfloat16)
            probs_ref[index * 2 + h] = low
            found.append(times(low, values))
        mixed_ref[r, pl.ds(pl.multiple_of(pair * LANES, LANES), LANES)] = jnp.where(
            lane < head, found[0], found[1]
        ).astype(jnp.bfloat16)
        return carry

    lax.fori_loop(0, images * pairs, pair_of, 0)
    middle_ref[...] = times(mixed_ref[...], proj_ref[...])

    def last(r):
        middle = middle_ref[r, :] + x_ref[r, :]
        middle_ref[r, :] = middle
        normed_mid_ref[r, :] = (
            norm_parts(middle)[0] * mid_gain_ref[...] + mid_shift_ref[...]
        ).astype(jnp.bfloat16)

    by_rows(rows, last)


def whole(*shape):
    return pl.BlockSpec(shape, lambda *index: (0,) * len(shape))


def attend_call(near, far, bias, gain, shift, qkv, proj, mid_gain, mid_shift, padded, patches):
    rows, width = near.shape
    images = rows // padded
    row = lambda v: v.reshape(1, width)
    shapes = [
        ((rows, width), jnp.float32),
        ((rows, width), jnp.bfloat16),
        ((rows, 3 * width), jnp.bfloat16),
        ((images * HEADS, padded, padded), jnp.bfloat16),
        ((rows, width), jnp.bfloat16),
        ((rows, width), jnp.float32),
        ((rows, width), jnp.bfloat16),
    ]
    return pl.pallas_call(
        functools.partial(attend_kernel, padded=padded, patches=patches),
        out_shape=[jax.ShapeDtypeStruct(*s) for s in shapes],
        compiler_params=pltpu.CompilerParams(vmem_limit_bytes=VMEM_LIMIT),
        name="attend",
    )(near, far, row(bias), row(gain), row(shift), qkv, proj, row(mid_gain), row(mid_shift))


def mlp_kernel(
    normed_ref, middle_ref, cot_ref, gain_ref, up_ref, down_ref,
    out_ref, grad_ref, low_ref, down_grad_ref, up_grad_ref, gain_grad_ref, shift_grad_ref,
    result_ref, slope_ref, wide_ref, back_ref, active_ref, grad_up_ref,
):
    step = pl.program_id(0)
    rows = normed_ref.shape[0]
    wide_ref[...] = times(normed_ref[...], up_ref[...])
    back_ref[...] = times_turned(cot_ref[...], down_ref[...])

    def middle_part(r):
        x = wide_ref[r, :]
        below = 0.5 * (1.0 + lax.erf(x * math.sqrt(0.5)))
        density = jnp.exp(-0.5 * x * x) * (1.0 / math.sqrt(2.0 * math.pi))
        active_ref[r, :] = (x * below).astype(jnp.bfloat16)
        grad_up_ref[r, :] = (back_ref[r, :] * (below + x * density)).astype(jnp.bfloat16)

    by_rows(rows, middle_part)
    down_grad_ref[...] = turned_times(active_ref[...], cot_ref[...]).astype(jnp.bfloat16)
    up_grad_ref[0] = turned_times(normed_ref[...], grad_up_ref[...]).astype(jnp.bfloat16)

    @pl.when(step == 0)
    def _():
        result_ref[...] = times(active_ref[...], down_ref[...])
        slope_ref[...] = times_turned(grad_up_ref[...], up_ref[...])

    @pl.when(step > 0)
    def _():
        result_ref[...] += times(active_ref[...], down_ref[...])
        slope_ref[...] += times_turned(grad_up_ref[...], up_ref[...])

    @pl.when(step == pl.num_programs(0) - 1)
    def _():
        gain_grad_ref[...] = jnp.zeros_like(gain_grad_ref)
        shift_grad_ref[...] = jnp.zeros_like(shift_grad_ref)

        def last(r):
            middle, slope = middle_ref[r, :], slope_ref[r, :]
            out_ref[r, :] = (middle + result_ref[r, :]).astype(jnp.bfloat16)
            back, terms = norm_backward(middle, slope, gain_ref[...])
            grad = cot_ref[r, :].astype(jnp.float32) + back
            grad_ref[r, :] = grad
            low_ref[r, :] = grad.astype(jnp.bfloat16)
            gain_grad_ref[...] += jnp.sum(terms, axis=0, keepdims=True)
            shift_grad_ref[...] += jnp.sum(slope, axis=0, keepdims=True)

        by_rows(rows, last)


def mlp_call(normed, middle, cot, gain, up, down):
    rows, width = middle.shape
    hidden = up.shape[1]
    steps = hidden // width
    f32, bf16 = jnp.float32, jnp.bfloat16
    return pl.pallas_call(
        mlp_kernel,
        grid=(steps,),
        in_specs=[
            whole(rows, width),
            whole(rows, width),
            whole(rows, width),
            whole(1, width),
            pl.BlockSpec((width, width), lambda j: (0, j)),
            pl.BlockSpec((width, width), lambda j: (j, 0)),
        ],
        out_specs=[
            whole(rows, width),
            whole(rows, width),
            whole(rows, width),
            pl.BlockSpec((width, width), lambda j: (j, 0)),
            pl.BlockSpec((1, width, width), lambda j: (j, 0, 0)),
            whole(1, width),
            whole(1, width),
        ],
        out_shape=[
            jax.ShapeDtypeStruct((rows, width), bf16),
            jax.ShapeDtypeStruct((rows, width), f32),
            jax.ShapeDtypeStruct((rows, width), bf16),
            jax.ShapeDtypeStruct((hidden, width), bf16),
            jax.ShapeDtypeStruct((steps, width, width), bf16),
            jax.ShapeDtypeStruct((1, width), f32),
            jax.ShapeDtypeStruct((1, width), f32),
        ],
        scratch_shapes=[pltpu.VMEM((rows, width), t) for t in (f32, f32, f32, f32, bf16, bf16)],
        compiler_params=pltpu.CompilerParams(vmem_limit_bytes=VMEM_LIMIT),
        name="mlp",
    )(normed, middle, cot, gain.reshape(1, width), up, down)


def attend_back_kernel(
    low_ref, grad_ref, x_ref, projected_ref, probs_ref, gain_ref, qkv_ref, proj_ref,
    grad_x_ref, grad_projected_ref, bias_grad_ref, gain_grad_ref, shift_grad_ref,
    mixed_grad_ref, slope_ref,
    *, padded,
):
    rows, width = x_ref.shape
    head = width // HEADS
    images, pairs = rows // padded, HEADS // 2
    mixed_grad_ref[...] = times_turned(low_ref[...], proj_ref[...]).astype(jnp.bfloat16)
    lane = lax.broadcasted_iota(jnp.int32, (padded, LANES), 1)
    factor = jnp.bfloat16(1.0 / math.sqrt(head))

    def pair_of(index, carry):
        image, pair = index // pairs, index % pairs
        r = pl.ds(pl.multiple_of(image * padded, padded), padded)

        def columns(part):
            return pl.ds(pl.multiple_of(part * width + pair * LANES, LANES), LANES)

        queries, keys, values = (projected_ref[r, columns(part)] for part in range(3))
        queries, keys = queries * factor, keys * factor
        grads = mixed_grad_ref[r, columns(0)]
        found = [], [], []
        for h in range(2):
            mine = (lane // head) == h
            low = probs_ref[index * 2 + h]
            probs = low.astype(jnp.float32)
            grad_probs = times_turned(jnp.where(mine, grads, jnp.zeros_like(grads)), values)
            scaled = grad_probs * probs
            total = jnp.sum(scaled, axis=-1, keepdims=True)
            grad_scores = (scaled - probs * total).astype(jnp.bfloat16)
            found[0].append(times(grad_scores, keys))
            found[1].append(turned_times(grad_scores, queries))
            found[2].append(turned_times(low, grads))
        for part in range(3):
            grad_projected_ref[r, columns(part)] = jnp.where(
                lane < head, found[part][0], found[part][1]
            ).astype(jnp.bfloat16)
        return carry

    lax.fori_loop(0, images * pairs, pair_of, 0)
    slope_ref[...] = times_turned(grad_projected_ref[:, :width], qkv_ref[:, :width])
    for part in range(1, 3):
        columns = slice(part * width, (part + 1) * width)
        slope_ref[...] += times_turned(grad_projected_ref[:, columns], qkv_ref[:, columns])
    for ref in (bias_grad_ref, gain_grad_ref, shift_grad_ref):
        ref[...] = jnp.zeros_like(ref)

    def last(r):
        slope = slope_ref[r, :]
        back, terms = norm_backward(x_ref[r, :], slope, gain_ref[...])
        grad = grad_ref[r, :] + back
        grad_x_ref[r, :] = grad.astype(jnp.bfloat16)
        bias_grad_ref[...] += jnp.sum(grad, axis=0, keepdims=True)
        gain_grad_ref[...] += jnp.sum(terms, axis=0, keepdims=True)
        shift_grad_ref[...] += jnp.sum(slope, axis=0, keepdims=True)

    by_rows(rows, last)


def attend_back_call(low, grad, x, projected, probs, gain, qkv, proj, padded):
    rows, width = x.shape
    f32, bf16 = jnp.float32, jnp.bfloat16
    shapes = [
        ((rows, width), bf16),
        ((rows, 3 * width), bf16),
        ((1, width), f32),
        ((1, width), f32),
        ((1, width), f32),
    ]
    return pl.pallas_call(
        functools.partial(attend_back_kernel, padded=padded),
        out_shape=[jax.ShapeDtypeStruct(*s) for s in shapes],
        scratch_shapes=[pltpu.VMEM((rows, width), bf16), pltpu.VMEM((rows, width), f32)],
        compiler_params=pltpu.CompilerParams(vmem_limit_bytes=VMEM_LIMIT),
        name="attend_back",
    )(low, grad, x, projected, probs, gain.reshape(1, width), qkv, proj)


def attend_weights_kernel(normed_ref, mixed_ref, grad_projected_ref, low_ref, out_ref):
    step = pl.program_id(0)

    @pl.when(step < 3)
    def _():
        out_ref[0] = turned_times(normed_ref[...], grad_projected_ref[...]).astype(jnp.bfloat16)

    @pl.when(step == 3)
    def _():
        out_ref[0] = turned_times(mixed_ref[...], low_ref[...]).astype(jnp.bfloat16)


def attend_weights_call(normed, mixed, grad_projected, low):
    rows, width = normed.shape
    return pl.pallas_call(
        attend_weights_kernel,
        grid=(4,),
        in_specs=[
            whole(rows, width),
            whole(rows, width),
            pl.BlockSpec((rows, width), lambda j: (0, jnp.minimum(j, 2))),
            whole(rows, width),
        ],
        out_specs=pl.BlockSpec((1, width, width), lambda j: (j, 0, 0)),
        out_shape=jax.ShapeDtypeStruct((4, width, width), jnp.bfloat16),
        compiler_params=pltpu.CompilerParams(vmem_limit_bytes=VMEM_LIMIT),
        name="attend_weights",
    )(normed, mixed, grad_projected, low)


HEADS = 12
WD = 128
WHEADS = 4


highest = lax.Precision.HIGHEST


def matmul_high(left, right):
    return jnp.dot(left, right, precision=highest, preferred_element_type=jnp.float32)


def layer_norm(values, norm_gain, norm_shift, epsilon):
    centered = values - jnp.mean(values, axis=-1, keepdims=True)
    variance = jnp.mean(centered * centered, axis=-1, keepdims=True)
    return centered * lax.rsqrt(variance + epsilon) * norm_gain + norm_shift


def wave_embed(wavelengths):
    halfwidth = WD // 2
    indices = jnp.arange(halfwidth, dtype=jnp.float32)
    frequency = 1.0 / 10000.0 ** (indices / halfwidth)
    angles = (wavelengths * 1000.0)[:, None] * frequency[None, :]
    return jnp.concatenate([jnp.sin(angles), jnp.cos(angles)], axis=1)


def hypernet(embedded, params):
    (
        bias_token,
        wave_qkv,
        wave_proj,
        wave_gain,
        wave_shift,
        wave_up,
        wave_down,
        kernel_gain,
        kernel_shift,
        bias_head,
    ) = params
    sequence = jnp.concatenate([embedded, bias_token[None, :]], axis=0)
    length = sequence.shape[0]
    head_width = WD // WHEADS
    projected = matmul_high(sequence, wave_qkv).reshape(length, 3, WHEADS, head_width)
    scores = jnp.einsum(
        "qhd,khd->hqk", projected[:, 0], projected[:, 1], precision=highest
    ) / math.sqrt(head_width)
    weights = jax.nn.softmax(scores, axis=-1)
    attended = jnp.einsum("hqk,khd->qhd", weights, projected[:, 2], precision=highest).reshape(
        length, WD
    )
    normed_first = layer_norm(
        sequence + matmul_high(attended, wave_proj), wave_gain, wave_shift, 1e-05
    )
    widened = jax.nn.gelu(matmul_high(normed_first, wave_up), approximate=False)
    second = layer_norm(
        normed_first + matmul_high(widened, wave_down), kernel_gain, kernel_shift, 1e-05
    )
    return (second[:-1] + embedded, matmul_high(second[-1:], bias_head)[0])


def swap_core(array):
    return lax.ppermute(array, "rows", [(0, 1), (1, 0), (2, 3), (3, 2)])


def swap_chip(array):
    return lax.ppermute(array, "rows", [(0, 2), (2, 0), (1, 3), (3, 1)])


def add_wide(left, right):
    return left.astype(jnp.float32) + right.astype(jnp.float32)


def rows_reduce(partial_rows):
    place = lax.axis_index("rows")
    chip, core = place // 2, place % 2
    images = partial_rows.shape[0] // 4

    def block(which_chip, which_core):
        return lax.dynamic_slice_in_dim(
            partial_rows, (which_chip * 2 + which_core) * images, images, 0
        )

    far = add_wide(block(1 - chip, core), swap_core(block(1 - chip, 1 - core)))
    near = add_wide(block(chip, core), swap_core(block(chip, 1 - core)))
    return near, swap_chip(far.astype(jnp.bfloat16))


def rows_gather(own):
    place = lax.axis_index("rows")
    chip, core = place // 2, place % 2
    near = swap_core(own)
    across = swap_chip(own)
    far = swap_core(across)

    def by_core(mine, other):
        return jnp.concatenate(
            [jnp.where(core == 0, mine, other), jnp.where(core == 0, other, mine)], axis=0
        )

    here, there = by_core(own, near), by_core(across, far)
    return jnp.concatenate(
        [jnp.where(chip == 0, here, there), jnp.where(chip == 0, there, here)], axis=0
    )


def swap_band(array, bit):
    count = lax.axis_size("band")
    return lax.ppermute(array, "band", [(i, i ^ (1 << bit)) for i in range(count)])


def halve(array, axis, bit, swap):
    half = array.shape[axis] // 2
    kept = lax.dynamic_slice_in_dim(array, bit * half, half, axis)
    sent = lax.dynamic_slice_in_dim(array, (1 - bit) * half, half, axis)
    return add_wide(kept, swap(sent)).astype(array.dtype)


def band_halve(array, axis):
    place = lax.axis_index("band")
    for bit in range(lax.axis_size("band").bit_length() - 1):
        shape = array.shape
        split = (*shape[:axis], shape[axis] // 2, 2, *shape[axis + 1 :])
        array = halve(
            array.reshape(split),
            axis + 1,
            (place >> bit) & 1,
            functools.partial(swap_band, bit=bit),
        )
        array = array.reshape(*shape[:axis], shape[axis] // 2, *shape[axis + 1 :])
    return array


def join(own, other, bit, axis):
    return jnp.where(
        bit == 0,
        jnp.concatenate([own, other], axis=axis),
        jnp.concatenate([other, own], axis=axis),
    )


def weight_reduce(grad, chip_first):
    place = lax.axis_index("rows")
    chip, core = place // 2, place % 2
    parts, rows, width = grad.shape
    bands = lax.axis_size("band")
    array = halve(grad.reshape(parts, bands, rows // bands, width), 3, core, swap_core)
    if chip_first:
        array = halve(array, 2, chip, swap_chip)
    array = band_halve(array, 1)[:, 0]
    if chip_first:
        array = join(array, swap_chip(array), chip, 1)
    else:
        array = add_wide(array, swap_chip(array)).astype(array.dtype)
    return join(array, swap_core(array), core, 2).astype(jnp.float32)


def side_by_side(parts):
    return parts.transpose(1, 0, 2).reshape(parts.shape[1], -1)


def sum_all(array):
    for swap in (swap_core, swap_chip):
        array = array + swap(array)
    for bit in range(lax.axis_size("band").bit_length() - 1):
        array = array + swap_band(array, bit)
    return array


def slot_masks(counts, slot_waves, waves):
    index = jnp.arange(counts.shape[0])
    ends = jnp.sum(jnp.where(index[None, :] <= index[:, None], counts[None, :], 0), axis=1)
    slots = jnp.arange(slot_waves.shape[0])
    owners = jnp.sum((ends[None, :] <= slots[:, None]).astype(jnp.int32), axis=1)
    return (
        (owners[:, None] == index[None, :]).astype(jnp.bfloat16),
        (slot_waves[:, None] == jnp.arange(waves)[None, :]).astype(jnp.bfloat16),
    )


def embed_plain(counts, slot_waves, kernel_low, kernel_weight, pixels):
    slots, positions, patches = pixels.shape
    table = jnp.einsum(
        "wk,qkc->wqc", kernel_low, kernel_weight, preferred_element_type=jnp.float32
    ).astype(jnp.bfloat16)
    of_image, of_wave = slot_masks(counts, slot_waves, table.shape[0])
    chunk = min(16, slots)

    def part(running, inputs):
        pixel, image, wave = inputs
        chosen = jnp.einsum("sw,wqc->sqc", wave, table)
        rows = jnp.einsum("sqp,sqc->spc", pixel, chosen, preferred_element_type=jnp.float32)
        image = image.astype(jnp.float32)
        return (running + jnp.einsum("si,spc->ipc", image, rows, precision=highest), None)

    shape = (counts.shape[0], patches, table.shape[2])
    total = lax.scan(
        part,
        jnp.zeros(shape, jnp.float32),
        tuple(a.reshape(-1, chunk, *a.shape[1:]) for a in (pixels, of_image, of_wave)),
    )[0]
    extra = pad_rows(patches) - patches
    return (jnp.pad(total.astype(jnp.bfloat16), ((0, 0), (0, extra), (0, 0))), table)


def embed_back_plain(counts, slot_waves, grads, table, pixels, kernel_weight):
    slots, positions, patches = pixels.shape
    waves, _, width = table.shape
    of_image, of_wave = slot_masks(counts, slot_waves, waves)
    grads = grads[:, :patches]
    chunk = min(16, slots)

    def part(running, inputs):
        pixel, image, wave = inputs
        chosen = jnp.einsum("sw,wqc->sqc", wave, table)
        slope = jnp.einsum("si,ipc->spc", image, grads)
        own = jnp.einsum("sqc,spc->sqp", chosen, slope, preferred_element_type=jnp.float32)
        more = jnp.einsum("sqp,spc->sqc", pixel, slope, preferred_element_type=jnp.float32)
        wave = wave.astype(jnp.float32)
        added = jnp.einsum("sw,sqc->qwc", wave, more, precision=highest)
        return (running + added, own.astype(jnp.bfloat16))

    kernel_grad, pixel_grad = lax.scan(
        part,
        jnp.zeros((positions, waves, width), jnp.float32),
        tuple(a.reshape(-1, chunk, *a.shape[1:]) for a in (pixels, of_image, of_wave)),
    )
    in_part = jnp.einsum(
        "qwc,qkc->wk",
        kernel_grad,
        kernel_weight.astype(jnp.float32),
        precision=highest,
        preferred_element_type=jnp.float32,
    )
    return (pixel_grad.reshape(pixels.shape), kernel_grad.astype(jnp.bfloat16), in_part)


def body(
    pixels,
    band_counts,
    band_waves,
    wavelengths,
    bias_token,
    wave_qkv,
    wave_proj,
    wave_gain,
    wave_shift,
    wave_up,
    wave_down,
    kernel_gain,
    kernel_shift,
    bias_head,
    kernel_weight,
    attention_gain,
    attention_shift,
    block_qkv,
    block_proj,
    hidden_gain,
    hidden_shift,
    block_up,
    block_down,
    cotangent,
):
    embedded = wave_embed(wavelengths)
    hyper_params = (
        bias_token,
        wave_qkv,
        wave_proj,
        wave_gain,
        wave_shift,
        wave_up,
        wave_down,
        kernel_gain,
        kernel_shift,
        bias_head,
    )

    def hyper_apply(params):
        return hypernet(embedded, params)

    (kernel_in, conv_bias), hyper_back = jax.vjp(hyper_apply, hyper_params)
    kernel_low = kernel_in.astype(jnp.bfloat16)
    counts = band_counts[0]
    slot_waves = band_waves[0]
    slot_total, positions, patches = pixels.shape
    images = counts.shape[0]
    waves, width = kernel_low.shape[0], kernel_weight.shape[2]
    fits = waves * positions * width <= 1 << 21
    if fits:
        partial_rows, wave_sums, kernel_table = embed_call(
            counts, slot_waves, kernel_low, kernel_weight, pixels
        )
    else:
        partial_rows, kernel_table = embed_plain(
            counts, slot_waves, kernel_low, kernel_weight, pixels
        )
    padded = pad_rows(patches)
    near, far = rows_reduce(partial_rows)
    local_images = near.shape[0]
    cot = jnp.pad(
        cotangent.reshape(local_images, patches, width), ((0, 0), (0, padded - patches), (0, 0))
    ).reshape(-1, width)
    x, normed, projected, probs, mixed, middle, normed_mid = attend_call(
        near.reshape(-1, width),
        far.reshape(-1, width),
        conv_bias,
        attention_gain,
        attention_shift,
        block_qkv,
        block_proj,
        hidden_gain,
        hidden_shift,
        padded,
        patches,
    )
    result, grad_middle, grad_low, down_part, up_part, hidden_gain_part, hidden_shift_part = (
        mlp_call(normed_mid, middle, cot, hidden_gain, block_up, block_down)
    )
    layer_output = result.reshape(local_images, padded, width)[:, :patches].reshape(-1, width)
    grad_x, grad_projected, bias_part, attention_gain_part, attention_shift_part = (
        attend_back_call(
            grad_low, grad_middle, x, projected, probs, attention_gain, block_qkv, block_proj, padded
        )
    )
    attend_part = attend_weights_call(normed, mixed, grad_projected, grad_low)
    gathered = rows_gather(grad_x.reshape(local_images, padded, width))
    block_down_grad = weight_reduce(down_part[None], False)[0]
    block_up_grad = side_by_side(weight_reduce(up_part, True))
    attend_grads = weight_reduce(attend_part, True)
    block_qkv_grad, block_proj_grad = side_by_side(attend_grads[:3]), attend_grads[3]
    if fits:
        pixel_grad, kernel_grad, in_part = embed_back_call(
            counts, slot_waves, gathered, kernel_table, wave_sums, pixels, kernel_weight
        )
    else:
        pixel_grad, kernel_grad, in_part = embed_back_plain(
            counts, slot_waves, gathered, kernel_table, pixels, kernel_weight
        )
    vectors = jnp.concatenate(
        [
            bias_part,
            attention_gain_part,
            attention_shift_part,
            hidden_gain_part,
            hidden_shift_part,
        ]
    )
    summed = sum_all(
        jnp.concatenate([in_part, vectors.reshape(-1, in_part.shape[1])], axis=0)
    )
    grad_kernel_in = summed[:waves]
    bias_grad, attention_gain_grad, attention_shift_grad, hidden_gain_grad, hidden_shift_grad = (
        summed[waves:].reshape(5, width)
    )
    bands = lax.axis_size("band")
    owned = band_halve(kernel_grad.reshape(bands, -1, waves, width), 0)[0]
    owned_weight = jnp.einsum(
        "wk,qwc->qkc", kernel_low, owned, preferred_element_type=jnp.float32
    ).astype(jnp.bfloat16)
    kernel_weight_grad = lax.all_to_all(
        owned_weight, "band", split_axis=1, concat_axis=0, tiled=True
    ).astype(jnp.float32)
    hyper_grads = hyper_back((grad_kernel_in, bias_grad))[0]
    return (
        layer_output,
        pixel_grad,
        kernel_weight_grad,
        hyper_grads[0],
        hyper_grads[1],
        hyper_grads[2],
        hyper_grads[3],
        hyper_grads[4],
        hyper_grads[5],
        hyper_grads[6],
        hyper_grads[7],
        hyper_grads[8],
        hyper_grads[9],
        attention_gain_grad,
        attention_shift_grad,
        block_qkv_grad,
        block_proj_grad,
        hidden_gain_grad,
        hidden_shift_grad,
        block_up_grad,
        block_down_grad,
    )


def solution(mesh):
    in_specs = (
        P("band", "rows", None),
        P("band", None),
        P("band", None),
        P(),
        P(),
        P(),
        P(),
        P(),
        P(),
        P(),
        P(),
        P(),
        P(),
        P(),
        P("rows", None, None),
        P(),
        P(),
        P(),
        P(),
        P(),
        P(),
        P(),
        P(),
        P(("band", "rows"), None),
    )
    out_specs = (
        P(("band", "rows"), None),
        P("band", "rows", None),
        P("rows", "band", None),
        P(),
        P(),
        P(),
        P(),
        P(),
        P(),
        P(),
        P(),
        P(),
        P(),
        P(),
        P(),
        P("band", None),
        P("band", None),
        P(),
        P(),
        P("band", None),
        P("band", None),
    )
    return jax.shard_map(body, mesh=mesh, in_specs=in_specs, out_specs=out_specs, check_vma=False)
```

```python
import functools
import math

import jax
import jax.numpy as jnp
from jax import lax
from jax.experimental import pallas as pl
from jax.experimental.pallas import tpu as pltpu
from jax.sharding import PartitionSpec as P

VMEM_LIMIT = 60 * 1024 * 1024
STEPS = 4
QUAD = 4
GROUP = 8
SMALL = 64
LANES = 128
EPSILON = 1e-06
ROW_STEP = 48


def pad_rows(rows):
    return (rows + 15) // 16 * 16


over_last = (((1,), (1,)), ((), ()))
over_first = (((0,), (0,)), ((), ()))


def times(left, right):
    return jnp.dot(left, right, preferred_element_type=jnp.float32)


def times_turned(left, right):
    return lax.dot_general(left, right, over_last, preferred_element_type=jnp.float32)


def turned_times(left, right):
    return lax.dot_general(left, right, over_first, preferred_element_type=jnp.float32)


def norm_parts(values):
    centered = values - jnp.mean(values, axis=-1, keepdims=True)
    variance = jnp.mean(centered * centered, axis=-1, keepdims=True)
    scale = lax.rsqrt(variance + EPSILON)
    return centered * scale, scale


def norm_backward(values, slope, gain):
    unit, scale = norm_parts(values)
    inner = slope * gain
    mean = jnp.mean(inner, axis=-1, keepdims=True)
    along = jnp.mean(inner * unit, axis=-1, keepdims=True)
    return scale * (inner - mean - unit * along), slope * unit


def by_rows(total, fn):
    def part(i, carry):
        fn(pl.ds(pl.multiple_of(i * ROW_STEP, ROW_STEP), ROW_STEP))
        return carry

    lax.fori_loop(0, total // ROW_STEP, part, 0)


def attend_kernel(
    own_ref, core_ref, chip_ref, bias_ref, gain_ref, shift_ref, qkv_ref, proj_ref, mid_gain_ref, mid_shift_ref,
    x_ref, normed_ref, projected_ref, probs_ref, mixed_ref, middle_ref, normed_mid_ref,
    *, padded, patches,
):
    rows, width = x_ref.shape
    head = width // HEADS
    images, pairs = rows // padded, HEADS // 2

    def first(r):
        x = sum(ref[r, :].astype(jnp.float32) for ref in (own_ref, core_ref, chip_ref))
        x = x + bias_ref[...]
        x_ref[r, :] = x
        normed_ref[r, :] = (norm_parts(x)[0] * gain_ref[...] + shift_ref[...]).astype(jnp.bfloat16)

    by_rows(rows, first)
    for part in range(3):
        columns = slice(part * width, (part + 1) * width)
        projected_ref[:, columns] = times(normed_ref[...], qkv_ref[:, columns]).astype(jnp.bfloat16)
    lane = lax.broadcasted_iota(jnp.int32, (padded, LANES), 1)
    key = lax.broadcasted_iota(jnp.int32, (padded, padded), 1)
    factor = jnp.bfloat16(1.0 / math.sqrt(head))

    def pair_of(index, carry):
        image, pair = index // pairs, index % pairs
        r = pl.ds(pl.multiple_of(image * padded, padded), padded)

        def columns(part):
            return pl.ds(pl.multiple_of(part * width + pair * LANES, LANES), LANES)

        queries, keys, values = (projected_ref[r, columns(part)] for part in range(3))
        found = []
        for h in range(2):
            mine = (lane // head) == h
            scores = times_turned(jnp.where(mine, queries * factor, jnp.zeros_like(queries)), keys)
            scores = jnp.where(key < patches, scores, -1e30)
            raised = jnp.exp(scores - jnp.max(scores, axis=-1, keepdims=True))
            probs = raised * (1.0 / jnp.sum(raised, axis=-1, keepdims=True))
            low = probs.astype(jnp.bfloat16)
            probs_ref[index * 2 + h] = low
            found.append(times(low, values))
        mixed_ref[r, pl.ds(pl.multiple_of(pair * LANES, LANES), LANES)] = jnp.where(
            lane < head, found[0], found[1]
        ).astype(jnp.bfloat16)
        return carry

    lax.fori_loop(0, images * pairs, pair_of, 0)
    middle_ref[...] = times(mixed_ref[...], proj_ref[...])

    def last(r):
        middle = middle_ref[r, :] + x_ref[r, :]
        middle_ref[r, :] = middle
        normed_mid_ref[r, :] = (
            norm_parts(middle)[0] * mid_gain_ref[...] + mid_shift_ref[...]
        ).astype(jnp.bfloat16)

    by_rows(rows, last)


def cost(flops, moved):
    return pl.CostEstimate(flops=flops, bytes_accessed=moved, transcendentals=0)


def whole(*shape):
    return pl.BlockSpec(shape, lambda *index: (0,) * len(shape))


def attend_call(terms, bias, gain, shift, qkv, proj, mid_gain, mid_shift, padded, patches):
    rows, width = terms[0].shape
    images = rows // padded
    row = lambda v: v.reshape(1, width)
    shapes = [
        ((rows, width), jnp.float32),
        ((rows, width), jnp.bfloat16),
        ((rows, 3 * width), jnp.bfloat16),
        ((images * HEADS, padded, padded), jnp.bfloat16),
        ((rows, width), jnp.bfloat16),
        ((rows, width), jnp.float32),
        ((rows, width), jnp.bfloat16),
    ]
    return pl.pallas_call(
        functools.partial(attend_kernel, padded=padded, patches=patches),
        out_shape=[jax.ShapeDtypeStruct(*s) for s in shapes],
        compiler_params=pltpu.CompilerParams(vmem_limit_bytes=VMEM_LIMIT),
        cost_estimate=cost(20 << 30, 25 << 20),
        name="attend",
    )(*terms, row(bias), row(gain), row(shift), qkv, proj, row(mid_gain), row(mid_shift))


def store_halves(core_ref, product, kept_ref, sent_ref):
    half = product.shape[1] // 2
    left, right = product[:, :half].astype(jnp.bfloat16), product[:, half:].astype(jnp.bfloat16)
    first = core_ref[0] == 0
    kept_ref[0] = jnp.where(first, left, right)
    sent_ref[0] = jnp.where(first, right, left)


def mlp_kernel(
    core_ref, normed_ref, middle_ref, cot_ref, gain_ref, up_ref, down_ref,
    out_ref, grad_ref, low_ref, down_kept_ref, down_sent_ref, up_kept_ref, up_sent_ref,
    gain_grad_ref, shift_grad_ref,
    result_ref, slope_ref, wide_ref, back_ref, active_ref, grad_up_ref,
):
    step = pl.program_id(0)
    rows = normed_ref.shape[0]
    wide_ref[...] = times(normed_ref[...], up_ref[...])
    back_ref[...] = times_turned(cot_ref[...], down_ref[...])

    def middle_part(r):
        x = wide_ref[r, :]
        below = 0.5 * (1.0 + lax.erf(x * math.sqrt(0.5)))
        density = jnp.exp(-0.5 * x * x) * (1.0 / math.sqrt(2.0 * math.pi))
        active_ref[r, :] = (x * below).astype(jnp.bfloat16)
        grad_up_ref[r, :] = (back_ref[r, :] * (below + x * density)).astype(jnp.bfloat16)

    by_rows(rows, middle_part)
    product = turned_times(active_ref[...], cot_ref[...])
    store_halves(core_ref, product, down_kept_ref, down_sent_ref)
    product = turned_times(normed_ref[...], grad_up_ref[...])
    store_halves(core_ref, product, up_kept_ref, up_sent_ref)

    @pl.when(step == 0)
    def _():
        result_ref[...] = times(active_ref[...], down_ref[...])
        slope_ref[...] = times_turned(grad_up_ref[...], up_ref[...])

    @pl.when(step > 0)
    def _():
        result_ref[...] += times(active_ref[...], down_ref[...])
        slope_ref[...] += times_turned(grad_up_ref[...], up_ref[...])

    @pl.when(step == pl.num_programs(0) - 1)
    def _():
        gain_grad_ref[...] = jnp.zeros_like(gain_grad_ref)
        shift_grad_ref[...] = jnp.zeros_like(shift_grad_ref)

        def last(r):
            middle, slope = middle_ref[r, :], slope_ref[r, :]
            out_ref[r, :] = (middle + result_ref[r, :]).astype(jnp.bfloat16)
            back, terms = norm_backward(middle, slope, gain_ref[...])
            grad = cot_ref[r, :].astype(jnp.float32) + back
            grad_ref[r, :] = grad
            low_ref[r, :] = grad.astype(jnp.bfloat16)
            gain_grad_ref[...] += jnp.sum(terms, axis=0, keepdims=True)
            shift_grad_ref[...] += jnp.sum(slope, axis=0, keepdims=True)

        by_rows(rows, last)


def mlp_call(core, normed, middle, cot, gain, up, down):
    rows, width = middle.shape
    hidden = up.shape[1]
    steps = hidden // width
    f32, bf16 = jnp.float32, jnp.bfloat16
    half = (1, width, width // 2)
    return pl.pallas_call(
        mlp_kernel,
        grid=(steps,),
        in_specs=[
            pl.BlockSpec(memory_space=pltpu.SMEM),
            whole(rows, width),
            whole(rows, width),
            whole(rows, width),
            whole(1, width),
            pl.BlockSpec((width, width), lambda j: (0, j)),
            pl.BlockSpec((width, width), lambda j: (j, 0)),
        ],
        out_specs=[
            whole(rows, width),
            whole(rows, width),
            whole(rows, width),
            *[pl.BlockSpec(half, lambda j: (j, 0, 0))] * 4,
            whole(1, width),
            whole(1, width),
        ],
        out_shape=[
            jax.ShapeDtypeStruct((rows, width), bf16),
            jax.ShapeDtypeStruct((rows, width), f32),
            jax.ShapeDtypeStruct((rows, width), bf16),
            *[jax.ShapeDtypeStruct((steps, width, width // 2), bf16)] * 4,
            jax.ShapeDtypeStruct((1, width), f32),
            jax.ShapeDtypeStruct((1, width), f32),
        ],
        scratch_shapes=[pltpu.VMEM((rows, width), t) for t in (f32, f32, f32, f32, bf16, bf16)],
        compiler_params=pltpu.CompilerParams(vmem_limit_bytes=VMEM_LIMIT),
        cost_estimate=cost(12 * rows * width * hidden, 30 << 20),
        name="mlp",
    )(core, normed, middle, cot, gain.reshape(1, width), up, down)


def attend_back_kernel(
    low_ref, projected_ref, probs_ref, proj_ref, grad_projected_ref, mixed_grad_ref, *, padded
):
    rows, width = low_ref.shape
    head = width // HEADS
    images, pairs = rows // padded, HEADS // 2
    mixed_grad_ref[...] = times_turned(low_ref[...], proj_ref[...]).astype(jnp.bfloat16)
    lane = lax.broadcasted_iota(jnp.int32, (padded, LANES), 1)
    factor = jnp.bfloat16(1.0 / math.sqrt(head))

    def pair_of(index, carry):
        image, pair = index // pairs, index % pairs
        r = pl.ds(pl.multiple_of(image * padded, padded), padded)

        def columns(part):
            return pl.ds(pl.multiple_of(part * width + pair * LANES, LANES), LANES)

        queries, keys, values = (projected_ref[r, columns(part)] for part in range(3))
        queries, keys = queries * factor, keys * factor
        grads = mixed_grad_ref[r, columns(0)]
        found = [], [], []
        for h in range(2):
            mine = (lane // head) == h
            low = probs_ref[index * 2 + h]
            probs = low.astype(jnp.float32)
            grad_probs = times_turned(jnp.where(mine, grads, jnp.zeros_like(grads)), values)
            scaled = grad_probs * probs
            total = jnp.sum(scaled, axis=-1, keepdims=True)
            grad_scores = (scaled - probs * total).astype(jnp.bfloat16)
            found[0].append(times(grad_scores, keys))
            found[1].append(turned_times(grad_scores, queries))
            found[2].append(turned_times(low, grads))
        for part in range(3):
            grad_projected_ref[r, columns(part)] = jnp.where(
                lane < head, found[part][0], found[part][1]
            ).astype(jnp.bfloat16)
        return carry

    lax.fori_loop(0, images * pairs, pair_of, 0)


def attend_back_call(low, projected, probs, proj, padded):
    rows, width = low.shape
    return pl.pallas_call(
        functools.partial(attend_back_kernel, padded=padded),
        out_shape=jax.ShapeDtypeStruct((rows, 3 * width), jnp.bfloat16),
        scratch_shapes=[pltpu.VMEM((rows, width), jnp.bfloat16)],
        compiler_params=pltpu.CompilerParams(vmem_limit_bytes=VMEM_LIMIT),
        cost_estimate=cost(18 << 30, 15 << 20),
        name="attend_back",
    )(low, projected, probs, proj)


def first_norm_back_kernel(
    grad_projected_ref, grad_ref, x_ref, gain_ref, qkv_ref,
    grad_x_ref, bias_grad_ref, gain_grad_ref, shift_grad_ref, slope_ref,
):
    rows, width = x_ref.shape
    slope_ref[...] = times_turned(grad_projected_ref[:, :width], qkv_ref[:, :width])
    for part in range(1, 3):
        columns = slice(part * width, (part + 1) * width)
        slope_ref[...] += times_turned(grad_projected_ref[:, columns], qkv_ref[:, columns])
    for ref in (bias_grad_ref, gain_grad_ref, shift_grad_ref):
        ref[...] = jnp.zeros_like(ref)

    def last(r):
        slope = slope_ref[r, :]
        back, terms = norm_backward(x_ref[r, :], slope, gain_ref[...])
        grad = grad_ref[r, :] + back
        grad_x_ref[r, :] = grad.astype(jnp.bfloat16)
        bias_grad_ref[...] += jnp.sum(grad, axis=0, keepdims=True)
        gain_grad_ref[...] += jnp.sum(terms, axis=0, keepdims=True)
        shift_grad_ref[...] += jnp.sum(slope, axis=0, keepdims=True)

    by_rows(rows, last)


def first_norm_back_call(grad_projected, grad, x, gain, qkv):
    rows, width = x.shape
    row = jax.ShapeDtypeStruct((1, width), jnp.float32)
    return pl.pallas_call(
        first_norm_back_kernel,
        out_shape=[jax.ShapeDtypeStruct((rows, width), jnp.bfloat16), row, row, row],
        scratch_shapes=[pltpu.VMEM((rows, width), jnp.float32)],
        compiler_params=pltpu.CompilerParams(vmem_limit_bytes=VMEM_LIMIT),
        cost_estimate=cost(9 << 30, 12 << 20),
        name="first_norm_back",
    )(grad_projected, grad, x, gain.reshape(1, width), qkv)


def attend_weights_kernel(
    core_ref, normed_ref, mixed_ref, grad_projected_ref, low_ref, kept_ref, sent_ref
):
    step = pl.program_id(0)

    @pl.when(step < 3)
    def _():
        product = turned_times(normed_ref[...], grad_projected_ref[...])
        store_halves(core_ref, product, kept_ref, sent_ref)

    @pl.when(step == 3)
    def _():
        product = turned_times(mixed_ref[...], low_ref[...])
        store_halves(core_ref, product, kept_ref, sent_ref)


def attend_weights_call(core, normed, mixed, grad_projected, low):
    rows, width = normed.shape
    half = (width, width // 2)
    return pl.pallas_call(
        attend_weights_kernel,
        grid=(4,),
        in_specs=[
            pl.BlockSpec(memory_space=pltpu.SMEM),
            whole(rows, width),
            whole(rows, width),
            pl.BlockSpec((rows, width), lambda j: (0, jnp.minimum(j, 2))),
            whole(rows, width),
        ],
        out_specs=[pl.BlockSpec((1, *half), lambda j: (j, 0, 0))] * 2,
        out_shape=[jax.ShapeDtypeStruct((4, *half), jnp.bfloat16)] * 2,
        compiler_params=pltpu.CompilerParams(vmem_limit_bytes=VMEM_LIMIT),
        cost_estimate=cost(8 * rows * width * width, 30 << 20),
        name="attend_weights",
    )(core, normed, mixed, grad_projected, low)


def fill_starts(counts_ref, starts_ref):
    images = counts_ref.shape[0]
    total, big, most, first = 0, 0, counts_ref[0], 0
    for m in range(images):
        starts_ref[m] = jnp.int32(total)
        if m:
            better = counts_ref[m] > most
            big = jnp.where(better, m, big)
            first = jnp.where(better, total, first)
            most = jnp.where(better, counts_ref[m], most)
        total = total + counts_ref[m]
    starts_ref[images] = jnp.int32(total)
    return big, first, first + most


def strided(ref, first, count, stride):
    parts = [ref[c, pl.ds(first, count, stride=stride), :] for c in range(ref.shape[0])]
    return jnp.concatenate(parts, axis=1)


def fill_choice(wave_row_ref, choice_ref, waves, big_lo, big_hi):
    slots = wave_row_ref.shape[1]
    slot = lax.broadcasted_iota(jnp.int32, (1, slots), 1)
    alone = waves + slot - jnp.where(slot >= big_hi, big_hi - big_lo, 0)
    column = jnp.where((slot >= big_lo) & (slot < big_hi), wave_row_ref[...], alone)
    index = lax.broadcasted_iota(jnp.int32, choice_ref.shape, 0)
    choice_ref[...] = jnp.where(index == column, 1.0, 0.0).astype(jnp.bfloat16)


def fill_spread(kin_ref, spread_ref):
    waves, depth = kin_ref.shape
    rows = waves * GROUP
    of_wave = lax.broadcasted_iota(jnp.int32, (rows, waves), 0) // GROUP
    pick = of_wave == lax.broadcasted_iota(jnp.int32, (rows, waves), 1)
    repeated = times(jnp.where(pick, 1.0, 0.0).astype(jnp.bfloat16), kin_ref[...])
    place = lax.broadcasted_iota(jnp.int32, (rows, depth), 0) % GROUP
    for q in range(GROUP):
        spread_ref[:, q * depth : (q + 1) * depth] = jnp.where(place == q, repeated, 0.0).astype(
            jnp.bfloat16
        )


def embed_kernel(
    place_ref, counts_ref, waves_ref, wave_row_ref, kin_ref, weight_ref, pix_ref,
    own_ref, core_ref, chip_ref, far_ref, big_out, small_out, rows_out, table_out,
    starts_ref, choice_ref, spread_ref, big_ref, small_ref, rows_ref, table_ref,
    turn_ref, wide_ref, acc_ref, semaphores,
):
    step = pl.program_id(0)
    waves, positions, width = table_ref.shape
    depth = kin_ref.shape[1]
    images = counts_ref.shape[0]
    patches, per_step, slots = pix_ref.shape
    padded = acc_ref.shape[0]
    held = own_ref.shape[0]
    big, big_lo, big_hi = fill_starts(counts_ref, starts_ref)

    @pl.when(step == 0)
    def _():
        fill_choice(wave_row_ref, choice_ref, waves, big_lo, big_hi)
        fill_spread(kin_ref, spread_ref)
        turn_ref[...] = jnp.zeros_like(turn_ref)

    first_q = pl.multiple_of(step * per_step, per_step)
    for q in range(per_step):
        rows_ref[first_q + q] = times(kin_ref[...], weight_ref[q]).astype(jnp.bfloat16)
    parts = []
    for q in range(0, per_step, GROUP):
        made = times(spread_ref[...], weight_ref[q : q + GROUP].reshape(GROUP * depth, width))
        parts.append(made.reshape(waves, GROUP, width))
    table_ref[:, pl.ds(first_q, per_step), :] = jnp.concatenate(parts, axis=1).astype(jnp.bfloat16)
    turn_ref[: patches * per_step] = times_turned(
        pix_ref[...].reshape(patches * per_step, slots), choice_ref[...]
    )
    for q in range(per_step):
        turned = turn_ref[pl.ds(q, 2 * LANES, stride=per_step), :].T
        big_ref[first_q + q] = turned[:waves, :padded].astype(jnp.bfloat16)
        for c in range(2):
            wide_ref[c, pl.ds(first_q + q, SMALL, stride=positions), :] = turned[
                waves : waves + SMALL, c * LANES : (c + 1) * LANES
            ]

    @pl.when(step == pl.num_programs(0) - 1)
    def _():
        def narrow(j, carry):
            rows = pl.ds(pl.multiple_of(j * positions, positions), positions)
            both = jnp.concatenate([wide_ref[0, rows, :], wide_ref[1, rows, :]], axis=1)
            small_ref[j] = both[:, :padded].astype(jnp.bfloat16)
            return carry

        lax.fori_loop(0, slots - (big_hi - big_lo), narrow, 0)
        pairs = ((big_ref, big_out), (small_ref, small_out), (rows_ref, rows_out), (table_ref, table_out))
        copies = [
            pltpu.make_async_copy(source, target, semaphores.at[k])
            for k, (source, target) in enumerate(pairs)
        ]
        for copy in copies:
            copy.start()

        def store(m):
            block = (m // held) ^ place_ref[0]
            low = acc_ref[...].astype(jnp.bfloat16)
            for index, ref in enumerate((own_ref, core_ref, chip_ref, far_ref)):

                @pl.when(block == index)
                def _(ref=ref):
                    ref[m % held] = low

        acc_ref[...] = jnp.zeros_like(acc_ref)

        def big_part(j, carry):
            first = pl.ds(pl.multiple_of(j * GROUP, GROUP), GROUP)
            left = big_ref[first].reshape(GROUP * waves, padded)
            acc_ref[...] += turned_times(left, rows_ref[first].reshape(GROUP * waves, width))
            return carry

        lax.fori_loop(0, positions // GROUP, big_part, 0)
        store(big)

        def image(m, carry):
            first, last = starts_ref[m], starts_ref[m + 1]
            shift = jnp.where(first >= big_hi, big_lo - big_hi, 0)

            @pl.when(m != big)
            def _():
                acc_ref[...] = jnp.zeros_like(acc_ref)

                def part(j, carry):
                    lefts, rights = [], []
                    for k in range(QUAD):
                        s = first + j * QUAD + k
                        here = jnp.minimum(s, last - 1)
                        factor = jnp.where(s < last, 1.0, 0.0).astype(jnp.bfloat16)
                        lefts.append(small_ref[here + shift] * factor)
                        rights.append(table_ref[waves_ref[here]])
                    acc_ref[...] += turned_times(
                        jnp.concatenate(lefts, axis=0), jnp.concatenate(rights, axis=0)
                    )
                    return carry

                lax.fori_loop(0, (last - first + QUAD - 1) // QUAD, part, 0)
                store(m)

            return carry

        lax.fori_loop(0, images, image, 0)
        for copy in copies:
            copy.wait()


def embed_call(place, counts, band_waves, kernel_low, kernel_weight, pixels):
    patches, positions, slots = pixels.shape
    waves = kernel_low.shape[0]
    depth, width = kernel_weight.shape[1:]
    images = counts.shape[0]
    padded = pad_rows(patches)
    per_step = positions // STEPS
    smem = pl.BlockSpec(memory_space=pltpu.SMEM)
    block = (images // 4, padded, width)
    kept = [
        (positions, waves, padded),
        (SMALL, positions, padded),
        (positions, waves, width),
        (waves, positions, width),
    ]
    return pl.pallas_call(
        embed_kernel,
        grid=(STEPS,),
        in_specs=[
            smem,
            smem,
            smem,
            whole(1, slots),
            whole(waves, depth),
            pl.BlockSpec((per_step, depth, width), lambda i: (i, 0, 0)),
            pl.BlockSpec((patches, per_step, slots), lambda i: (0, i, 0)),
        ],
        out_specs=[*[whole(*block)] * 4, *[pl.BlockSpec(memory_space=pl.ANY)] * 4],
        out_shape=[
            *[jax.ShapeDtypeStruct(block, jnp.bfloat16)] * 4,
            *[jax.ShapeDtypeStruct(shape, jnp.bfloat16) for shape in kept],
        ],
        scratch_shapes=[
            pltpu.SMEM((images + 1,), jnp.int32),
            pltpu.VMEM((LANES, slots), jnp.bfloat16),
            pltpu.VMEM((waves * GROUP, GROUP * depth), jnp.bfloat16),
            *[pltpu.VMEM(shape, jnp.bfloat16) for shape in kept],
            pltpu.VMEM((2 * LANES * per_step, LANES), jnp.float32),
            pltpu.VMEM((2, SMALL * positions, LANES), jnp.float32),
            pltpu.VMEM((padded, width), jnp.float32),
            pltpu.SemaphoreType.DMA((4,)),
        ],
        compiler_params=pltpu.CompilerParams(vmem_limit_bytes=VMEM_LIMIT),
        name="embed",
    )(place, counts, band_waves, band_waves[None], kernel_low, kernel_weight, pixels)


def embed_back_kernel(
    place_ref, counts_ref, waves_ref, wave_row_ref, own_ref, core_ref, chip_ref, far_ref,
    big_ref, small_ref, rows_ref, table_ref,
    pix_grad_ref, kernel_grad_ref,
    starts_ref, choice_ref, order_ref, grad_ref, sum_ref, wide_ref, big_slope_ref, slope_ref, turn_ref,
    semaphores,
):
    step = pl.program_id(0)
    waves, positions, width = table_ref.shape
    padded = big_ref.shape[2]
    images = counts_ref.shape[0]
    held = own_ref.shape[0]
    patches, per_step, _ = pix_grad_ref.shape
    place = place_ref[0]
    count = GROUP * waves

    def grads_of(m):
        return grad_ref[((m // held) ^ place) * held + m % held]

    @pl.when(step == 0)
    def _():
        copies = [
            pltpu.make_async_copy(ref, grad_ref.at[pl.ds(k * held, held)], semaphores.at[k])
            for k, ref in enumerate((own_ref, core_ref, chip_ref, far_ref))
        ]
        for copy in copies:
            copy.start()
        big, big_lo, big_hi = fill_starts(counts_ref, starts_ref)
        fill_choice(wave_row_ref, choice_ref, waves, big_lo, big_hi)
        row = lax.broadcasted_iota(jnp.int32, (count, count), 0)
        column = lax.broadcasted_iota(jnp.int32, (count, count), 1)
        same = (row // waves == column % GROUP) & (row % waves == column // GROUP)
        order_ref[...] = jnp.where(same, 1.0, 0.0).astype(jnp.bfloat16)
        slope_ref[...] = jnp.zeros_like(slope_ref)
        wide_ref[...] = jnp.zeros_like(wide_ref)
        for copy in copies:
            copy.wait()
        grads = grads_of(big)

        def big_part(j, carry):
            first = pl.ds(pl.multiple_of(j * GROUP, GROUP), GROUP)
            slope = times_turned(rows_ref[first].reshape(count, width), grads)
            big_slope_ref[first, :, :padded] = slope.astype(jnp.bfloat16).reshape(
                GROUP, waves, padded
            )
            sum_ref[pl.ds(pl.multiple_of(j * count, count), count), :] = times(
                big_ref[first].reshape(count, padded), grads
            )
            return carry

        lax.fori_loop(0, positions // GROUP, big_part, 0)

        def image(m, carry):
            first, last = starts_ref[m], starts_ref[m + 1]
            shift = jnp.where(first >= big_hi, big_lo - big_hi, 0)

            @pl.when(m != big)
            def _():
                grads = grads_of(m)

                def part(j, carry):
                    lefts, rights, index = [], [], []
                    for k in range(QUAD):
                        s = first + j * QUAD + k
                        here = jnp.minimum(s, last - 1)
                        factor = jnp.where(s < last, 1.0, 0.0).astype(jnp.bfloat16)
                        index.append(here)
                        lefts.append(table_ref[waves_ref[here]])
                        rights.append(small_ref[here + shift] * factor)
                    own = times_turned(jnp.concatenate(lefts, axis=0), grads)
                    more = times(jnp.concatenate(rights, axis=0), grads)
                    for k in range(QUAD):
                        part_rows = slice(k * positions, (k + 1) * positions)
                        row = pl.multiple_of((index[k] + shift) * positions, positions)
                        slope_ref[0, pl.ds(row, positions), :] = own[part_rows, :LANES]
                        slope_ref[1, pl.ds(row, positions), : padded - LANES] = own[
                            part_rows, LANES:
                        ]
                        wide_ref[waves_ref[index[k]]] += more[part_rows]
                    return carry

                lax.fori_loop(0, (last - first + QUAD - 1) // QUAD, part, 0)

            return carry

        lax.fori_loop(0, images, image, 0)

    first_q = pl.multiple_of(step * per_step, per_step)
    for q in range(0, per_step, GROUP):
        place_q = pl.multiple_of(first_q + q, GROUP)
        block = wide_ref[:, pl.ds(place_q, GROUP), :].reshape(count, width).astype(jnp.bfloat16)
        rows = pl.ds(pl.multiple_of(place_q * waves, count), count)
        total = sum_ref[rows, :] + times(order_ref[...], block)
        kernel_grad_ref[q : q + GROUP] = total.astype(jnp.bfloat16).reshape(GROUP, waves, width)
    for q in range(per_step):
        alone = strided(slope_ref, first_q + q, SMALL, positions).astype(jnp.bfloat16)
        chosen = jnp.concatenate([big_slope_ref[first_q + q], alone], axis=0)
        spread = turned_times(chosen, choice_ref[: waves + SMALL])
        for c in range(turn_ref.shape[0]):
            turn_ref[c, pl.ds(q, patches, stride=per_step), :] = spread[
                :patches, c * LANES : (c + 1) * LANES
            ]
    for c in range(turn_ref.shape[0]):
        pix_grad_ref[:, :, c * LANES : (c + 1) * LANES] = (
            turn_ref[c].astype(jnp.bfloat16).reshape(patches, per_step, LANES)
        )


def embed_back_call(place, counts, band_waves, grads, kept, patches):
    positions, waves, padded = kept[0].shape
    width = kept[2].shape[2]
    slots = band_waves.shape[0]
    images = counts.shape[0]
    per_step = positions // STEPS
    smem = pl.BlockSpec(memory_space=pltpu.SMEM)
    return pl.pallas_call(
        embed_back_kernel,
        grid=(STEPS,),
        in_specs=[
            smem,
            smem,
            smem,
            whole(1, slots),
            *[pl.BlockSpec(memory_space=pl.ANY)] * 4,
            *[whole(*array.shape) for array in kept],
        ],
        out_specs=[
            pl.BlockSpec((patches, per_step, slots), lambda i: (0, i, 0)),
            pl.BlockSpec((per_step, waves, width), lambda i: (i, 0, 0)),
        ],
        out_shape=[
            jax.ShapeDtypeStruct((patches, positions, slots), jnp.bfloat16),
            jax.ShapeDtypeStruct((positions, waves, width), jnp.bfloat16),
        ],
        scratch_shapes=[
            pltpu.SMEM((images + 1,), jnp.int32),
            pltpu.VMEM((LANES, slots), jnp.bfloat16),
            pltpu.VMEM((GROUP * waves, GROUP * waves), jnp.bfloat16),
            pltpu.VMEM((images, padded, width), jnp.bfloat16),
            pltpu.VMEM((positions * waves, width), jnp.float32),
            pltpu.VMEM((waves, positions, width), jnp.float32),
            pltpu.VMEM((positions, waves, 2 * LANES), jnp.bfloat16),
            pltpu.VMEM((2, SMALL * positions, LANES), jnp.float32),
            pltpu.VMEM((slots // LANES, patches * per_step, LANES), jnp.float32),
            pltpu.SemaphoreType.DMA((4,)),
        ],
        compiler_params=pltpu.CompilerParams(vmem_limit_bytes=VMEM_LIMIT),
        name="embed_back",
    )(place, counts, band_waves, band_waves[None], *grads, *kept)


def in_grad_kernel(kernel_grad_ref, weight_ref, out_ref):
    @pl.when(pl.program_id(0) == 0)
    def _():
        out_ref[...] = jnp.zeros_like(out_ref)

    found = times_turned(kernel_grad_ref[0], weight_ref[0])
    for q in range(1, kernel_grad_ref.shape[0]):
        found = found + times_turned(kernel_grad_ref[q], weight_ref[q])
    out_ref[...] += found


def in_grad_call(kernel_grad, kernel_weight):
    positions, waves, width = kernel_grad.shape
    depth = kernel_weight.shape[1]
    return pl.pallas_call(
        in_grad_kernel,
        grid=(8,),
        in_specs=[
            pl.BlockSpec((positions // 8, waves, width), lambda i: (i, 0, 0)),
            pl.BlockSpec((positions // 8, depth, width), lambda i: (i, 0, 0)),
        ],
        out_specs=whole(waves, depth),
        out_shape=jax.ShapeDtypeStruct((waves, depth), jnp.float32),
        compiler_params=pltpu.CompilerParams(vmem_limit_bytes=VMEM_LIMIT),
        cost_estimate=cost(4 << 30, 16 << 20),
        name="in_grad",
    )(kernel_grad, kernel_weight)


HEADS = 12
WD = 128
WHEADS = 4


highest = lax.Precision.HIGHEST


def matmul_high(left, right):
    return jnp.dot(left, right, precision=highest, preferred_element_type=jnp.float32)


def layer_norm(values, norm_gain, norm_shift, epsilon):
    centered = values - jnp.mean(values, axis=-1, keepdims=True)
    variance = jnp.mean(centered * centered, axis=-1, keepdims=True)
    return centered * lax.rsqrt(variance + epsilon) * norm_gain + norm_shift


def wave_embed(wavelengths):
    halfwidth = WD // 2
    indices = jnp.arange(halfwidth, dtype=jnp.float32)
    frequency = 1.0 / 10000.0 ** (indices / halfwidth)
    angles = (wavelengths * 1000.0)[:, None] * frequency[None, :]
    return jnp.concatenate([jnp.sin(angles), jnp.cos(angles)], axis=1)


def hypernet(embedded, params):
    (
        bias_token,
        wave_qkv,
        wave_proj,
        wave_gain,
        wave_shift,
        wave_up,
        wave_down,
        kernel_gain,
        kernel_shift,
        bias_head,
    ) = params
    sequence = jnp.concatenate([embedded, bias_token[None, :]], axis=0)
    length = sequence.shape[0]
    head_width = WD // WHEADS
    projected = matmul_high(sequence, wave_qkv).reshape(length, 3, WHEADS, head_width)
    scores = jnp.einsum(
        "qhd,khd->hqk", projected[:, 0], projected[:, 1], precision=highest
    ) / math.sqrt(head_width)
    weights = jax.nn.softmax(scores, axis=-1)
    attended = jnp.einsum("hqk,khd->qhd", weights, projected[:, 2], precision=highest).reshape(
        length, WD
    )
    normed_first = layer_norm(
        sequence + matmul_high(attended, wave_proj), wave_gain, wave_shift, 1e-05
    )
    widened = jax.nn.gelu(matmul_high(normed_first, wave_up), approximate=False)
    second = layer_norm(
        normed_first + matmul_high(widened, wave_down), kernel_gain, kernel_shift, 1e-05
    )
    return (second[:-1] + embedded, matmul_high(second[-1:], bias_head)[0])


def swap_core(array):
    return lax.ppermute(array, "rows", [(0, 1), (1, 0), (2, 3), (3, 2)])


def swap_chip(array):
    return lax.ppermute(array, "rows", [(0, 2), (2, 0), (1, 3), (3, 1)])


def add_wide(left, right):
    return left.astype(jnp.float32) + right.astype(jnp.float32)


def rows_reduce(own, core, chip, far):
    passed = add_wide(chip, swap_core(far)).astype(jnp.bfloat16)
    return own, swap_core(core), swap_chip(passed)


def rows_gather(own):
    across = swap_chip(own)
    return own, swap_core(own), across, swap_core(across)


def swap_band(array, bit):
    count = lax.axis_size("band")
    return lax.ppermute(array, "band", [(i, i ^ (1 << bit)) for i in range(count)])


def halve(array, axis, bit, swap):
    half = array.shape[axis] // 2
    kept = lax.dynamic_slice_in_dim(array, bit * half, half, axis)
    sent = lax.dynamic_slice_in_dim(array, (1 - bit) * half, half, axis)
    return add_wide(kept, swap(sent)).astype(array.dtype)


def join(own, other, bit, axis):
    return jnp.where(
        bit == 0,
        jnp.concatenate([own, other], axis=axis),
        jnp.concatenate([other, own], axis=axis),
    )


def weight_gather(array, chip_first):
    place = lax.axis_index("rows")
    chip, core = place // 2, place % 2
    if chip_first:
        array = join(array, swap_chip(array), chip, 1)
    else:
        array = add_wide(array, swap_chip(array)).astype(array.dtype)
    return join(array, swap_core(array), core, 2).astype(jnp.float32)


def by_band(array):
    parts, rows, width = array.shape
    bands = lax.axis_size("band")
    return array.reshape(parts, bands, rows // bands, width)


def band_steps(array, axis, steps):
    place = lax.axis_index("band")
    for bit in steps:
        shape = array.shape
        split = (*shape[:axis], shape[axis] // 2, 2, *shape[axis + 1 :])
        array = halve(
            array.reshape(split),
            axis + 1,
            (place >> bit) & 1,
            functools.partial(swap_band, bit=bit),
        )
        array = array.reshape(*shape[:axis], shape[axis] // 2, *shape[axis + 1 :])
    return array


def band_bits():
    return range(lax.axis_size("band").bit_length() - 1)


def together(*arrays):
    return lax.optimization_barrier(arrays)


def side_by_side(parts):
    return parts.transpose(1, 0, 2).reshape(parts.shape[1], -1)


def sum_all(array):
    for swap in (swap_core, swap_chip):
        array = array + swap(array)
    for bit in range(lax.axis_size("band").bit_length() - 1):
        array = array + swap_band(array, bit)
    return array


def slot_masks(counts, slot_waves, waves):
    index = jnp.arange(counts.shape[0])
    ends = jnp.sum(jnp.where(index[None, :] <= index[:, None], counts[None, :], 0), axis=1)
    slots = jnp.arange(slot_waves.shape[0])
    owners = jnp.sum((ends[None, :] <= slots[:, None]).astype(jnp.int32), axis=1)
    return (
        (owners[:, None] == index[None, :]).astype(jnp.bfloat16),
        (slot_waves[:, None] == jnp.arange(waves)[None, :]).astype(jnp.bfloat16),
    )


def embed_plain(counts, slot_waves, kernel_low, kernel_weight, pixels):
    slots, positions, patches = pixels.shape
    table = jnp.einsum(
        "wk,qkc->wqc", kernel_low, kernel_weight, preferred_element_type=jnp.float32
    ).astype(jnp.bfloat16)
    of_image, of_wave = slot_masks(counts, slot_waves, table.shape[0])
    chunk = min(16, slots)

    def part(running, inputs):
        pixel, image, wave = inputs
        chosen = jnp.einsum("sw,wqc->sqc", wave, table)
        rows = jnp.einsum("sqp,sqc->spc", pixel, chosen, preferred_element_type=jnp.float32)
        image = image.astype(jnp.float32)
        return (running + jnp.einsum("si,spc->ipc", image, rows, precision=highest), None)

    shape = (counts.shape[0], patches, table.shape[2])
    total = lax.scan(
        part,
        jnp.zeros(shape, jnp.float32),
        tuple(a.reshape(-1, chunk, *a.shape[1:]) for a in (pixels, of_image, of_wave)),
    )[0]
    extra = pad_rows(patches) - patches
    return (jnp.pad(total.astype(jnp.bfloat16), ((0, 0), (0, extra), (0, 0))), table)


def embed_back_plain(counts, slot_waves, grads, table, pixels):
    slots, positions, patches = pixels.shape
    waves, _, width = table.shape
    of_image, of_wave = slot_masks(counts, slot_waves, waves)
    grads = grads[:, :patches]
    chunk = min(16, slots)

    def part(running, inputs):
        pixel, image, wave = inputs
        chosen = jnp.einsum("sw,wqc->sqc", wave, table)
        slope = jnp.einsum("si,ipc->spc", image, grads)
        own = jnp.einsum("sqc,spc->sqp", chosen, slope, preferred_element_type=jnp.float32)
        more = jnp.einsum("sqp,spc->sqc", pixel, slope, preferred_element_type=jnp.float32)
        wave = wave.astype(jnp.float32)
        added = jnp.einsum("sw,sqc->qwc", wave, more, precision=highest)
        return (running + added, own.astype(jnp.bfloat16))

    kernel_grad, pixel_grad = lax.scan(
        part,
        jnp.zeros((positions, waves, width), jnp.float32),
        tuple(a.reshape(-1, chunk, *a.shape[1:]) for a in (pixels, of_image, of_wave)),
    )
    return (pixel_grad.reshape(pixels.shape), kernel_grad.astype(jnp.bfloat16))


def body(
    pixels,
    band_counts,
    band_waves,
    wavelengths,
    bias_token,
    wave_qkv,
    wave_proj,
    wave_gain,
    wave_shift,
    wave_up,
    wave_down,
    kernel_gain,
    kernel_shift,
    bias_head,
    kernel_weight,
    attention_gain,
    attention_shift,
    block_qkv,
    block_proj,
    hidden_gain,
    hidden_shift,
    block_up,
    block_down,
    cotangent,
):
    embedded = wave_embed(wavelengths)
    hyper_params = (
        bias_token,
        wave_qkv,
        wave_proj,
        wave_gain,
        wave_shift,
        wave_up,
        wave_down,
        kernel_gain,
        kernel_shift,
        bias_head,
    )

    def hyper_apply(params):
        return hypernet(embedded, params)

    (kernel_in, conv_bias), hyper_back = jax.vjp(hyper_apply, hyper_params)
    kernel_low = kernel_in.astype(jnp.bfloat16)
    counts = band_counts[0]
    slot_waves = band_waves[0]
    slot_total, positions, patches = pixels.shape
    images = counts.shape[0]
    waves, width = kernel_low.shape[0], kernel_weight.shape[2]
    fits = waves * positions * width <= 1 << 21
    place = lax.axis_index("rows").astype(jnp.int32)
    padded = pad_rows(patches)
    if fits:
        turned_pixels = pixels.transpose(2, 1, 0)
        *blocks, kept_big, kept_small, kept_rows, kept_table = embed_call(
            place[None], counts, slot_waves, kernel_low, kernel_weight, turned_pixels
        )
    else:
        partial_rows, kernel_table = embed_plain(
            counts, slot_waves, kernel_low, kernel_weight, pixels
        )
        partial_rows = partial_rows.reshape(4, -1, padded, width)
        blocks = [lax.dynamic_index_in_dim(partial_rows, place ^ k, 0, False) for k in range(4)]
    terms = [term.reshape(-1, width) for term in rows_reduce(*blocks)]
    local_images = images // 4
    cot = jnp.pad(
        cotangent.reshape(local_images, patches, width), ((0, 0), (0, padded - patches), (0, 0))
    ).reshape(-1, width)
    x, normed, projected, probs, mixed, middle, normed_mid = attend_call(
        terms,
        conv_bias,
        attention_gain,
        attention_shift,
        block_qkv,
        block_proj,
        hidden_gain,
        hidden_shift,
        padded,
        patches,
    )
    core = (lax.axis_index("rows") % 2).astype(jnp.int32)[None]
    chip = lax.axis_index("rows") // 2
    (
        result,
        grad_middle,
        grad_low,
        down_kept,
        down_sent,
        up_kept,
        up_sent,
        hidden_gain_part,
        hidden_shift_part,
    ) = mlp_call(core, normed_mid, middle, cot, hidden_gain, block_up, block_down)
    layer_output = result.reshape(local_images, padded, width)[:, :patches].reshape(-1, width)
    down_met, up_met = swap_core(down_sent), swap_core(up_sent)
    grad_projected = attend_back_call(grad_low, projected, probs, block_proj, padded)
    grad_projected, down_met, up_met = together(grad_projected, down_met, up_met)
    first_bit, more_bits = band_bits()[:1], band_bits()[1:]
    down_pair = by_band(
        add_wide(down_kept, down_met).astype(jnp.bfloat16).reshape(1, -1, width // 2)
    )
    up_pair = by_band(add_wide(up_kept, up_met).astype(jnp.bfloat16))
    grad_x, bias_part, attention_gain_part, attention_shift_part = first_norm_back_call(
        grad_projected, grad_middle, x, attention_gain, block_qkv
    )
    gathered = rows_gather(grad_x.reshape(local_images, padded, width))
    down_sum = band_steps(down_pair, 1, first_bit)
    attend_kept, attend_sent = attend_weights_call(core, normed, mixed, grad_projected, grad_low)
    attend_met = swap_core(attend_sent)
    gathered, down_sum, up_pair, attend_met = together(gathered, down_sum, up_pair, attend_met)
    up_sum = band_steps(up_pair, 1, first_bit)
    down_sum = band_steps(down_sum, 1, more_bits[:1])
    if fits:
        pixel_grad, kernel_grad = embed_back_call(
            place[None],
            counts,
            slot_waves,
            gathered,
            (kept_big, kept_small, kept_rows, kept_table),
            patches,
        )
        pixel_grad = pixel_grad.transpose(2, 1, 0)
    else:
        stacked = jnp.stack(gathered)
        ordered = jnp.concatenate(
            [lax.dynamic_index_in_dim(stacked, place ^ k, 0, False) for k in range(4)]
        )
        pixel_grad, kernel_grad = embed_back_plain(
            counts, slot_waves, ordered, kernel_table, pixels
        )
    kernel_grad, up_sum, down_sum = together(kernel_grad, up_sum, down_sum)
    bands = lax.axis_size("band")
    owned = band_steps(kernel_grad.reshape(bands, -1, waves, width), 0, first_bit)
    if fits:
        in_part = in_grad_call(kernel_grad, kernel_weight)
    else:
        in_part = jnp.einsum(
            "qwc,qkc->wk", kernel_grad, kernel_weight, preferred_element_type=jnp.float32
        )
    attend_sum = halve(
        by_band(add_wide(attend_kept, attend_met).astype(jnp.bfloat16)), 2, chip, swap_chip
    )
    up_all = band_steps(up_sum, 1, more_bits)[:, 0]
    down_all = band_steps(down_sum, 1, more_bits[1:])[:, 0]
    owned, in_part, attend_sum, up_all, down_all = together(
        owned, in_part, attend_sum, up_all, down_all
    )
    owned = band_steps(owned, 0, more_bits)[0]
    attend_sum = band_steps(attend_sum, 1, first_bit)
    owned, attend_sum = together(owned, attend_sum)
    attend_all = band_steps(attend_sum, 1, more_bits)[:, 0]
    block_down_grad = weight_gather(down_all, False)[0]
    block_up_grad = side_by_side(weight_gather(up_all, False))
    attend_grads = weight_gather(attend_all, True)
    block_qkv_grad, block_proj_grad = side_by_side(attend_grads[:3]), attend_grads[3]
    vectors = jnp.concatenate(
        [
            bias_part,
            attention_gain_part,
            attention_shift_part,
            hidden_gain_part,
            hidden_shift_part,
        ]
    )
    summed = sum_all(jnp.concatenate([in_part, vectors.reshape(-1, in_part.shape[1])], axis=0))
    grad_kernel_in = summed[:waves]
    bias_grad, attention_gain_grad, attention_shift_grad, hidden_gain_grad, hidden_shift_grad = (
        summed[waves:].reshape(5, width)
    )
    owned_weight = jnp.einsum(
        "wk,qwc->qkc", kernel_low, owned, preferred_element_type=jnp.float32
    ).astype(jnp.bfloat16)
    kernel_weight_grad = lax.all_to_all(
        owned_weight, "band", split_axis=1, concat_axis=0, tiled=True
    ).astype(jnp.float32)
    hyper_grads = hyper_back((grad_kernel_in, bias_grad))[0]
    return (
        layer_output,
        pixel_grad,
        kernel_weight_grad,
        hyper_grads[0],
        hyper_grads[1],
        hyper_grads[2],
        hyper_grads[3],
        hyper_grads[4],
        hyper_grads[5],
        hyper_grads[6],
        hyper_grads[7],
        hyper_grads[8],
        hyper_grads[9],
        attention_gain_grad,
        attention_shift_grad,
        block_qkv_grad,
        block_proj_grad,
        hidden_gain_grad,
        hidden_shift_grad,
        block_up_grad,
        block_down_grad,
    )


def solution(mesh):
    in_specs = (
        P("band", "rows", None),
        P("band", None),
        P("band", None),
        P(),
        P(),
        P(),
        P(),
        P(),
        P(),
        P(),
        P(),
        P(),
        P(),
        P(),
        P("rows", None, None),
        P(),
        P(),
        P(),
        P(),
        P(),
        P(),
        P(),
        P(),
        P(("band", "rows"), None),
    )
    out_specs = (
        P(("band", "rows"), None),
        P("band", "rows", None),
        P("rows", "band", None),
        P(),
        P(),
        P(),
        P(),
        P(),
        P(),
        P(),
        P(),
        P(),
        P(),
        P(),
        P(),
        P("band", None),
        P("band", None),
        P(),
        P(),
        P("band", None),
        P("band", None),
    )
    return jax.shard_map(body, mesh=mesh, in_specs=in_specs, out_specs=out_specs, check_vma=False)
```

```python
import functools
import math

import jax
import jax.numpy as jnp
from jax import lax
from jax.experimental import pallas as pl
from jax.experimental.pallas import tpu as pltpu
from jax.sharding import PartitionSpec as P

VMEM_LIMIT = 60 * 1024 * 1024
STEPS = 4
QUAD = 4
GROUP = 8
SMALL = 64
LANES = 128
EPSILON = 1e-06
ROW_STEP = 48


def pad_rows(rows):
    return (rows + 15) // 16 * 16


over_last = (((1,), (1,)), ((), ()))
over_first = (((0,), (0,)), ((), ()))


def times(left, right):
    return jnp.dot(left, right, preferred_element_type=jnp.float32)


def times_turned(left, right):
    return lax.dot_general(left, right, over_last, preferred_element_type=jnp.float32)


def turned_times(left, right):
    return lax.dot_general(left, right, over_first, preferred_element_type=jnp.float32)


def norm_parts(values):
    centered = values - jnp.mean(values, axis=-1, keepdims=True)
    variance = jnp.mean(centered * centered, axis=-1, keepdims=True)
    scale = lax.rsqrt(variance + EPSILON)
    return centered * scale, scale


def norm_backward(values, slope, gain):
    unit, scale = norm_parts(values)
    inner = slope * gain
    mean = jnp.mean(inner, axis=-1, keepdims=True)
    along = jnp.mean(inner * unit, axis=-1, keepdims=True)
    return scale * (inner - mean - unit * along), slope * unit


def by_rows(total, fn):
    def part(i, carry):
        fn(pl.ds(pl.multiple_of(i * ROW_STEP, ROW_STEP), ROW_STEP))
        return carry

    lax.fori_loop(0, total // ROW_STEP, part, 0)


def attend_kernel(
    own_ref, core_ref, chip_ref, bias_ref, gain_ref, shift_ref, qkv_ref, proj_ref, mid_gain_ref, mid_shift_ref,
    x_ref, normed_ref, projected_ref, probs_ref, mixed_ref, middle_ref, normed_mid_ref,
    *, padded, patches,
):
    rows, width = x_ref.shape
    head = width // HEADS
    images, pairs = rows // padded, HEADS // 2

    def first(r):
        x = sum(ref[r, :].astype(jnp.float32) for ref in (own_ref, core_ref, chip_ref))
        x = x + bias_ref[...]
        x_ref[r, :] = x
        normed_ref[r, :] = (norm_parts(x)[0] * gain_ref[...] + shift_ref[...]).astype(jnp.bfloat16)

    by_rows(rows, first)
    for part in range(3):
        columns = slice(part * width, (part + 1) * width)
        projected_ref[:, columns] = times(normed_ref[...], qkv_ref[:, columns]).astype(jnp.bfloat16)
    lane = lax.broadcasted_iota(jnp.int32, (padded, LANES), 1)
    key = lax.broadcasted_iota(jnp.int32, (padded, padded), 1)
    factor = jnp.bfloat16(1.0 / math.sqrt(head))

    def pair_of(index, carry):
        image, pair = index // pairs, index % pairs
        r = pl.ds(pl.multiple_of(image * padded, padded), padded)

        def columns(part):
            return pl.ds(pl.multiple_of(part * width + pair * LANES, LANES), LANES)

        queries, keys, values = (projected_ref[r, columns(part)] for part in range(3))
        found = []
        for h in range(2):
            mine = (lane // head) == h
            scores = times_turned(jnp.where(mine, queries * factor, jnp.zeros_like(queries)), keys)
            scores = jnp.where(key < patches, scores, -1e30)
            raised = jnp.exp(scores - jnp.max(scores, axis=-1, keepdims=True))
            probs = raised * (1.0 / jnp.sum(raised, axis=-1, keepdims=True))
            low = probs.astype(jnp.bfloat16)
            probs_ref[index * 2 + h] = low
            found.append(times(low, values))
        mixed_ref[r, pl.ds(pl.multiple_of(pair * LANES, LANES), LANES)] = jnp.where(
            lane < head, found[0], found[1]
        ).astype(jnp.bfloat16)
        return carry

    lax.fori_loop(0, images * pairs, pair_of, 0)
    middle_ref[...] = times(mixed_ref[...], proj_ref[...])

    def last(r):
        middle = middle_ref[r, :] + x_ref[r, :]
        middle_ref[r, :] = middle
        normed_mid_ref[r, :] = (
            norm_parts(middle)[0] * mid_gain_ref[...] + mid_shift_ref[...]
        ).astype(jnp.bfloat16)

    by_rows(rows, last)


def cost(flops, moved):
    return pl.CostEstimate(flops=flops, bytes_accessed=moved, transcendentals=0)


def whole(*shape):
    return pl.BlockSpec(shape, lambda *index: (0,) * len(shape))


def attend_call(terms, bias, gain, shift, qkv, proj, mid_gain, mid_shift, padded, patches):
    rows, width = terms[0].shape
    images = rows // padded
    row = lambda v: v.reshape(1, width)
    shapes = [
        ((rows, width), jnp.float32),
        ((rows, width), jnp.bfloat16),
        ((rows, 3 * width), jnp.bfloat16),
        ((images * HEADS, padded, padded), jnp.bfloat16),
        ((rows, width), jnp.bfloat16),
        ((rows, width), jnp.float32),
        ((rows, width), jnp.bfloat16),
    ]
    return pl.pallas_call(
        functools.partial(attend_kernel, padded=padded, patches=patches),
        out_shape=[jax.ShapeDtypeStruct(*s) for s in shapes],
        compiler_params=pltpu.CompilerParams(vmem_limit_bytes=VMEM_LIMIT),
        cost_estimate=cost(20 << 30, 25 << 20),
        name="attend",
    )(*terms, row(bias), row(gain), row(shift), qkv, proj, row(mid_gain), row(mid_shift))


def store_halves(core_ref, product, kept_ref, sent_ref):
    half = product.shape[1] // 2
    left, right = product[:, :half].astype(jnp.bfloat16), product[:, half:].astype(jnp.bfloat16)
    first = core_ref[0] == 0
    kept_ref[0] = jnp.where(first, left, right)
    sent_ref[0] = jnp.where(first, right, left)


def mlp_kernel(
    core_ref, normed_ref, middle_ref, cot_ref, gain_ref, up_ref, down_ref,
    out_ref, grad_ref, low_ref, down_kept_ref, down_sent_ref, up_kept_ref, up_sent_ref,
    gain_grad_ref, shift_grad_ref,
    result_ref, slope_ref, wide_ref, back_ref, active_ref, grad_up_ref,
):
    step = pl.program_id(0)
    rows = normed_ref.shape[0]
    wide_ref[...] = times(normed_ref[...], up_ref[...])
    back_ref[...] = times_turned(cot_ref[...], down_ref[...])

    def middle_part(r):
        x = wide_ref[r, :]
        below = 0.5 * (1.0 + lax.erf(x * math.sqrt(0.5)))
        density = jnp.exp(-0.5 * x * x) * (1.0 / math.sqrt(2.0 * math.pi))
        active_ref[r, :] = (x * below).astype(jnp.bfloat16)
        grad_up_ref[r, :] = (back_ref[r, :] * (below + x * density)).astype(jnp.bfloat16)

    by_rows(rows, middle_part)
    product = turned_times(active_ref[...], cot_ref[...])
    store_halves(core_ref, product, down_kept_ref, down_sent_ref)
    product = turned_times(normed_ref[...], grad_up_ref[...])
    store_halves(core_ref, product, up_kept_ref, up_sent_ref)

    @pl.when(step == 0)
    def _():
        result_ref[...] = times(active_ref[...], down_ref[...])
        slope_ref[...] = times_turned(grad_up_ref[...], up_ref[...])

    @pl.when(step > 0)
    def _():
        result_ref[...] += times(active_ref[...], down_ref[...])
        slope_ref[...] += times_turned(grad_up_ref[...], up_ref[...])

    @pl.when(step == pl.num_programs(0) - 1)
    def _():
        gain_grad_ref[...] = jnp.zeros_like(gain_grad_ref)
        shift_grad_ref[...] = jnp.zeros_like(shift_grad_ref)

        def last(r):
            middle, slope = middle_ref[r, :], slope_ref[r, :]
            out_ref[r, :] = (middle + result_ref[r, :]).astype(jnp.bfloat16)
            back, terms = norm_backward(middle, slope, gain_ref[...])
            grad = cot_ref[r, :].astype(jnp.float32) + back
            grad_ref[r, :] = grad
            low_ref[r, :] = grad.astype(jnp.bfloat16)
            gain_grad_ref[...] += jnp.sum(terms, axis=0, keepdims=True)
            shift_grad_ref[...] += jnp.sum(slope, axis=0, keepdims=True)

        by_rows(rows, last)


def mlp_call(core, normed, middle, cot, gain, up, down):
    rows, width = middle.shape
    hidden = up.shape[1]
    steps = hidden // width
    f32, bf16 = jnp.float32, jnp.bfloat16
    half = (1, width, width // 2)
    return pl.pallas_call(
        mlp_kernel,
        grid=(steps,),
        in_specs=[
            pl.BlockSpec(memory_space=pltpu.SMEM),
            whole(rows, width),
            whole(rows, width),
            whole(rows, width),
            whole(1, width),
            pl.BlockSpec((width, width), lambda j: (0, j)),
            pl.BlockSpec((width, width), lambda j: (j, 0)),
        ],
        out_specs=[
            whole(rows, width),
            whole(rows, width),
            whole(rows, width),
            *[pl.BlockSpec(half, lambda j: (j, 0, 0))] * 4,
            whole(1, width),
            whole(1, width),
        ],
        out_shape=[
            jax.ShapeDtypeStruct((rows, width), bf16),
            jax.ShapeDtypeStruct((rows, width), f32),
            jax.ShapeDtypeStruct((rows, width), bf16),
            *[jax.ShapeDtypeStruct((steps, width, width // 2), bf16)] * 4,
            jax.ShapeDtypeStruct((1, width), f32),
            jax.ShapeDtypeStruct((1, width), f32),
        ],
        scratch_shapes=[pltpu.VMEM((rows, width), t) for t in (f32, f32, f32, f32, bf16, bf16)],
        compiler_params=pltpu.CompilerParams(vmem_limit_bytes=VMEM_LIMIT),
        cost_estimate=cost(12 * rows * width * hidden, 30 << 20),
        name="mlp",
    )(core, normed, middle, cot, gain.reshape(1, width), up, down)


def attend_back_kernel(low_ref, projected_ref, probs_ref, proj_ref, *refs):
    grad_projected_ref, mixed_grad_ref = refs[-2:]
    padded, width = low_ref.shape
    head = width // HEADS
    mixed_grad_ref[...] = times_turned(low_ref[...], proj_ref[...]).astype(jnp.bfloat16)
    lane = lax.broadcasted_iota(jnp.int32, (padded, LANES), 1)
    factor = jnp.bfloat16(1.0 / math.sqrt(head))

    def pair_of(pair, carry):
        def columns(part):
            return pl.ds(pl.multiple_of(part * width + pair * LANES, LANES), LANES)

        queries, keys, values = (projected_ref[:, columns(part)] for part in range(3))
        queries, keys = queries * factor, keys * factor
        grads = mixed_grad_ref[:, columns(0)]
        found = [], [], []
        for h in range(2):
            mine = (lane // head) == h
            low = probs_ref[pair * 2 + h]
            probs = low.astype(jnp.float32)
            grad_probs = times_turned(jnp.where(mine, grads, jnp.zeros_like(grads)), values)
            scaled = grad_probs * probs
            total = jnp.sum(scaled, axis=-1, keepdims=True)
            grad_scores = (scaled - probs * total).astype(jnp.bfloat16)
            found[0].append(times(grad_scores, keys))
            found[1].append(turned_times(grad_scores, queries))
            found[2].append(turned_times(low, grads))
        for part in range(3):
            grad_projected_ref[:, columns(part)] = jnp.where(
                lane < head, found[part][0], found[part][1]
            ).astype(jnp.bfloat16)
        return carry

    lax.fori_loop(0, HEADS // 2, pair_of, 0)


def attend_back_call(low, projected, probs, proj, padded, first, count, begun=None):
    rows, width = low.shape
    return pl.pallas_call(
        attend_back_kernel,
        grid=(count,),
        in_specs=[
            pl.BlockSpec((padded, width), lambda i: (i + first, 0)),
            pl.BlockSpec((padded, 3 * width), lambda i: (i + first, 0)),
            pl.BlockSpec((HEADS, padded, padded), lambda i: (i + first, 0, 0)),
            whole(width, width),
            *([] if begun is None else [pl.BlockSpec(memory_space=pl.ANY)]),
        ],
        out_specs=pl.BlockSpec((padded, 3 * width), lambda i: (i + first, 0)),
        out_shape=jax.ShapeDtypeStruct((rows, 3 * width), jnp.bfloat16),
        scratch_shapes=[pltpu.VMEM((padded, width), jnp.bfloat16)],
        input_output_aliases={} if begun is None else {4: 0},
        compiler_params=pltpu.CompilerParams(vmem_limit_bytes=VMEM_LIMIT),
        cost_estimate=cost(count * (6 << 30), count * (5 << 20)),
        name="attend_back",
    )(low, projected, probs, proj, *([] if begun is None else [begun]))


def first_norm_back_kernel(
    grad_projected_ref, grad_ref, x_ref, gain_ref, qkv_ref,
    grad_x_ref, bias_grad_ref, gain_grad_ref, shift_grad_ref, slope_ref,
):
    rows, width = x_ref.shape
    slope_ref[...] = times_turned(grad_projected_ref[:, :width], qkv_ref[:, :width])
    for part in range(1, 3):
        columns = slice(part * width, (part + 1) * width)
        slope_ref[...] += times_turned(grad_projected_ref[:, columns], qkv_ref[:, columns])
    for ref in (bias_grad_ref, gain_grad_ref, shift_grad_ref):
        ref[...] = jnp.zeros_like(ref)

    def last(r):
        slope = slope_ref[r, :]
        back, terms = norm_backward(x_ref[r, :], slope, gain_ref[...])
        grad = grad_ref[r, :] + back
        grad_x_ref[r, :] = grad.astype(jnp.bfloat16)
        bias_grad_ref[...] += jnp.sum(grad, axis=0, keepdims=True)
        gain_grad_ref[...] += jnp.sum(terms, axis=0, keepdims=True)
        shift_grad_ref[...] += jnp.sum(slope, axis=0, keepdims=True)

    by_rows(rows, last)


def first_norm_back_call(grad_projected, grad, x, gain, qkv):
    rows, width = x.shape
    row = jax.ShapeDtypeStruct((1, width), jnp.float32)
    return pl.pallas_call(
        first_norm_back_kernel,
        out_shape=[jax.ShapeDtypeStruct((rows, width), jnp.bfloat16), row, row, row],
        scratch_shapes=[pltpu.VMEM((rows, width), jnp.float32)],
        compiler_params=pltpu.CompilerParams(vmem_limit_bytes=VMEM_LIMIT),
        cost_estimate=cost(1 << 30, 1 << 20),
        name="first_norm_back",
    )(grad_projected, grad, x, gain.reshape(1, width), qkv)


def attend_weights_kernel(
    core_ref, normed_ref, mixed_ref, grad_projected_ref, low_ref, kept_ref, sent_ref
):
    step = pl.program_id(0)

    @pl.when(step < 3)
    def _():
        product = turned_times(normed_ref[...], grad_projected_ref[...])
        store_halves(core_ref, product, kept_ref, sent_ref)

    @pl.when(step == 3)
    def _():
        product = turned_times(mixed_ref[...], low_ref[...])
        store_halves(core_ref, product, kept_ref, sent_ref)


def attend_weights_call(core, normed, mixed, grad_projected, low):
    rows, width = normed.shape
    half = (width, width // 2)
    return pl.pallas_call(
        attend_weights_kernel,
        grid=(4,),
        in_specs=[
            pl.BlockSpec(memory_space=pltpu.SMEM),
            whole(rows, width),
            whole(rows, width),
            pl.BlockSpec((rows, width), lambda j: (0, jnp.minimum(j, 2))),
            whole(rows, width),
        ],
        out_specs=[pl.BlockSpec((1, *half), lambda j: (j, 0, 0))] * 2,
        out_shape=[jax.ShapeDtypeStruct((4, *half), jnp.bfloat16)] * 2,
        compiler_params=pltpu.CompilerParams(vmem_limit_bytes=VMEM_LIMIT),
        cost_estimate=cost(8 * rows * width * width, 30 << 20),
        name="attend_weights",
    )(core, normed, mixed, grad_projected, low)


def fill_starts(counts_ref, starts_ref):
    images = counts_ref.shape[0]
    total, big, most, first = 0, 0, counts_ref[0], 0
    for m in range(images):
        starts_ref[m] = jnp.int32(total)
        if m:
            better = counts_ref[m] > most
            big = jnp.where(better, m, big)
            first = jnp.where(better, total, first)
            most = jnp.where(better, counts_ref[m], most)
        total = total + counts_ref[m]
    starts_ref[images] = jnp.int32(total)
    return big, first, first + most


def strided(ref, first, count, stride):
    parts = [ref[c, pl.ds(first, count, stride=stride), :] for c in range(ref.shape[0])]
    return jnp.concatenate(parts, axis=1)


def fill_choice(wave_row_ref, choice_ref, waves, big_lo, big_hi):
    slots = wave_row_ref.shape[1]
    slot = lax.broadcasted_iota(jnp.int32, (1, slots), 1)
    alone = waves + slot - jnp.where(slot >= big_hi, big_hi - big_lo, 0)
    column = jnp.where((slot >= big_lo) & (slot < big_hi), wave_row_ref[...], alone)
    index = lax.broadcasted_iota(jnp.int32, choice_ref.shape, 0)
    choice_ref[...] = jnp.where(index == column, 1.0, 0.0).astype(jnp.bfloat16)


def fill_spread(kin_ref, spread_ref):
    waves, depth = kin_ref.shape
    rows = waves * GROUP
    of_wave = lax.broadcasted_iota(jnp.int32, (rows, waves), 0) // GROUP
    pick = of_wave == lax.broadcasted_iota(jnp.int32, (rows, waves), 1)
    repeated = times(jnp.where(pick, 1.0, 0.0).astype(jnp.bfloat16), kin_ref[...])
    place = lax.broadcasted_iota(jnp.int32, (rows, depth), 0) % GROUP
    for q in range(GROUP):
        spread_ref[:, q * depth : (q + 1) * depth] = jnp.where(place == q, repeated, 0.0).astype(
            jnp.bfloat16
        )


def embed_kernel(
    place_ref, counts_ref, waves_ref, wave_row_ref, kin_ref, weight_ref, pix_ref,
    own_ref, core_ref, chip_ref, far_ref, big_out, small_out, rows_out, table_out,
    starts_ref, choice_ref, spread_ref, big_ref, small_ref, rows_ref, table_ref,
    turn_ref, wide_ref, acc_ref, semaphores,
):
    step = pl.program_id(0)
    waves, positions, width = table_ref.shape
    depth = kin_ref.shape[1]
    images = counts_ref.shape[0]
    patches, per_step, slots = pix_ref.shape
    padded = acc_ref.shape[0]
    held = own_ref.shape[0]
    big, big_lo, big_hi = fill_starts(counts_ref, starts_ref)

    @pl.when(step == 0)
    def _():
        fill_choice(wave_row_ref, choice_ref, waves, big_lo, big_hi)
        fill_spread(kin_ref, spread_ref)
        turn_ref[...] = jnp.zeros_like(turn_ref)

    first_q = pl.multiple_of(step * per_step, per_step)
    for q in range(per_step):
        rows_ref[first_q + q] = times(kin_ref[...], weight_ref[q]).astype(jnp.bfloat16)
    parts = []
    for q in range(0, per_step, GROUP):
        made = times(spread_ref[...], weight_ref[q : q + GROUP].reshape(GROUP * depth, width))
        parts.append(made.reshape(waves, GROUP, width))
    table_ref[:, pl.ds(first_q, per_step), :] = jnp.concatenate(parts, axis=1).astype(jnp.bfloat16)
    turn_ref[: patches * per_step] = times_turned(
        pix_ref[...].reshape(patches * per_step, slots), choice_ref[...]
    )
    for q in range(per_step):
        turned = turn_ref[pl.ds(q, 2 * LANES, stride=per_step), :].T
        big_ref[first_q + q] = turned[:waves, :padded].astype(jnp.bfloat16)
        for c in range(2):
            wide_ref[c, pl.ds(first_q + q, SMALL, stride=positions), :] = turned[
                waves : waves + SMALL, c * LANES : (c + 1) * LANES
            ]

    @pl.when(step == pl.num_programs(0) - 1)
    def _():
        def narrow(j, carry):
            rows = pl.ds(pl.multiple_of(j * positions, positions), positions)
            both = jnp.concatenate([wide_ref[0, rows, :], wide_ref[1, rows, :]], axis=1)
            small_ref[j] = both[:, :padded].astype(jnp.bfloat16)
            return carry

        lax.fori_loop(0, slots - (big_hi - big_lo), narrow, 0)
        pairs = ((big_ref, big_out), (small_ref, small_out), (rows_ref, rows_out), (table_ref, table_out))
        copies = [
            pltpu.make_async_copy(source, target, semaphores.at[k])
            for k, (source, target) in enumerate(pairs)
        ]
        for copy in copies:
            copy.start()

        def store(m):
            block = (m // held) ^ place_ref[0]
            low = acc_ref[...].astype(jnp.bfloat16)
            for index, ref in enumerate((own_ref, core_ref, chip_ref, far_ref)):

                @pl.when(block == index)
                def _(ref=ref):
                    ref[m % held] = low

        acc_ref[...] = jnp.zeros_like(acc_ref)

        def big_part(j, carry):
            first = pl.ds(pl.multiple_of(j * GROUP, GROUP), GROUP)
            left = big_ref[first].reshape(GROUP * waves, padded)
            acc_ref[...] += turned_times(left, rows_ref[first].reshape(GROUP * waves, width))
            return carry

        lax.fori_loop(0, positions // GROUP, big_part, 0)
        store(big)

        def image(m, carry):
            first, last = starts_ref[m], starts_ref[m + 1]
            shift = jnp.where(first >= big_hi, big_lo - big_hi, 0)

            @pl.when(m != big)
            def _():
                acc_ref[...] = jnp.zeros_like(acc_ref)

                def part(j, carry):
                    lefts, rights = [], []
                    for k in range(QUAD):
                        s = first + j * QUAD + k
                        here = jnp.minimum(s, last - 1)
                        factor = jnp.where(s < last, 1.0, 0.0).astype(jnp.bfloat16)
                        lefts.append(small_ref[here + shift] * factor)
                        rights.append(table_ref[waves_ref[here]])
                    acc_ref[...] += turned_times(
                        jnp.concatenate(lefts, axis=0), jnp.concatenate(rights, axis=0)
                    )
                    return carry

                lax.fori_loop(0, (last - first + QUAD - 1) // QUAD, part, 0)
                store(m)

            return carry

        lax.fori_loop(0, images, image, 0)
        for copy in copies:
            copy.wait()


def embed_call(place, counts, band_waves, kernel_low, kernel_weight, pixels):
    patches, positions, slots = pixels.shape
    waves = kernel_low.shape[0]
    depth, width = kernel_weight.shape[1:]
    images = counts.shape[0]
    padded = pad_rows(patches)
    per_step = positions // STEPS
    smem = pl.BlockSpec(memory_space=pltpu.SMEM)
    block = (images // 4, padded, width)
    kept = [
        (positions, waves, padded),
        (SMALL, positions, padded),
        (positions, waves, width),
        (waves, positions, width),
    ]
    return pl.pallas_call(
        embed_kernel,
        grid=(STEPS,),
        in_specs=[
            smem,
            smem,
            smem,
            whole(1, slots),
            whole(waves, depth),
            pl.BlockSpec((per_step, depth, width), lambda i: (i, 0, 0)),
            pl.BlockSpec((patches, per_step, slots), lambda i: (0, i, 0)),
        ],
        out_specs=[*[whole(*block)] * 4, *[pl.BlockSpec(memory_space=pl.ANY)] * 4],
        out_shape=[
            *[jax.ShapeDtypeStruct(block, jnp.bfloat16)] * 4,
            *[jax.ShapeDtypeStruct(shape, jnp.bfloat16) for shape in kept],
        ],
        scratch_shapes=[
            pltpu.SMEM((images + 1,), jnp.int32),
            pltpu.VMEM((LANES, slots), jnp.bfloat16),
            pltpu.VMEM((waves * GROUP, GROUP * depth), jnp.bfloat16),
            *[pltpu.VMEM(shape, jnp.bfloat16) for shape in kept],
            pltpu.VMEM((2 * LANES * per_step, LANES), jnp.float32),
            pltpu.VMEM((2, SMALL * positions, LANES), jnp.float32),
            pltpu.VMEM((padded, width), jnp.float32),
            pltpu.SemaphoreType.DMA((4,)),
        ],
        compiler_params=pltpu.CompilerParams(vmem_limit_bytes=VMEM_LIMIT),
        name="embed",
    )(place, counts, band_waves, band_waves[None], kernel_low, kernel_weight, pixels)


def embed_back_kernel(
    place_ref, odd_ref, counts_ref, waves_ref, own_ref, core_ref, chip_ref, far_ref,
    big_ref, small_ref, rows_ref, table_ref, weight_ref, vectors_ref,
    kept_ref, sent_ref, big_slope_ref, slope_ref, in_grad_ref,
    starts_ref, order_ref, grad_ref, sum_ref, wide_ref, semaphores,
):
    step = pl.program_id(0)
    waves, positions, width = table_ref.shape
    padded = big_ref.shape[2]
    images = counts_ref.shape[0]
    held = own_ref.shape[0]
    place = place_ref[0]
    count = GROUP * waves

    def grads_of(m):
        return grad_ref[((m // held) ^ place) * held + m % held]

    @pl.when(step == 0)
    def _():
        copies = [
            pltpu.make_async_copy(ref, grad_ref.at[pl.ds(k * held, held)], semaphores.at[k])
            for k, ref in enumerate((own_ref, core_ref, chip_ref, far_ref))
        ]
        for copy in copies:
            copy.start()
        big, big_lo, big_hi = fill_starts(counts_ref, starts_ref)
        row = lax.broadcasted_iota(jnp.int32, (count, count), 0)
        column = lax.broadcasted_iota(jnp.int32, (count, count), 1)
        same = (row // waves == column % GROUP) & (row % waves == column // GROUP)
        order_ref[...] = jnp.where(same, 1.0, 0.0).astype(jnp.bfloat16)
        in_grad_ref[:waves] = jnp.zeros((waves, in_grad_ref.shape[1]), jnp.float32)
        in_grad_ref[waves:] = vectors_ref[...]
        slope_ref[...] = jnp.zeros_like(slope_ref)
        wide_ref[...] = jnp.zeros_like(wide_ref)
        for copy in copies:
            copy.wait()
        grads = grads_of(big)

        def big_part(j, carry):
            first = pl.ds(pl.multiple_of(j * GROUP, GROUP), GROUP)
            slope = times_turned(rows_ref[first].reshape(count, width), grads)
            big_slope_ref[first, :, :padded] = slope.astype(jnp.bfloat16).reshape(
                GROUP, waves, padded
            )
            sum_ref[pl.ds(pl.multiple_of(j * count, count), count), :] = times(
                big_ref[first].reshape(count, padded), grads
            )
            return carry

        lax.fori_loop(0, positions // GROUP, big_part, 0)

        def image(m, carry):
            first, last = starts_ref[m], starts_ref[m + 1]
            shift = jnp.where(first >= big_hi, big_lo - big_hi, 0)

            @pl.when(m != big)
            def _():
                grads = grads_of(m)

                def part(j, carry):
                    lefts, rights, index = [], [], []
                    for k in range(QUAD):
                        s = first + j * QUAD + k
                        here = jnp.minimum(s, last - 1)
                        factor = jnp.where(s < last, 1.0, 0.0).astype(jnp.bfloat16)
                        index.append(here)
                        lefts.append(table_ref[waves_ref[here]])
                        rights.append(small_ref[here + shift] * factor)
                    own = times_turned(jnp.concatenate(lefts, axis=0), grads)
                    more = times(jnp.concatenate(rights, axis=0), grads)
                    for k in range(QUAD):
                        part_rows = slice(k * positions, (k + 1) * positions)
                        row = pl.multiple_of((index[k] + shift) * positions, positions)
                        slope_ref[0, pl.ds(row, positions), :] = own[part_rows, :LANES]
                        slope_ref[1, pl.ds(row, positions), : padded - LANES] = own[
                            part_rows, LANES:
                        ]
                        wide_ref[waves_ref[index[k]]] += more[part_rows]
                    return carry

                lax.fori_loop(0, (last - first + QUAD - 1) // QUAD, part, 0)

            return carry

        lax.fori_loop(0, images, image, 0)

    odd = odd_ref[0]
    found = jnp.zeros((waves, in_grad_ref.shape[1]), jnp.float32)
    for ref, half in ((kept_ref, odd), (sent_ref, 1 - odd)):
        first_q = pl.multiple_of((2 * step + half) * GROUP, GROUP)
        block = wide_ref[:, pl.ds(first_q, GROUP), :].reshape(count, width).astype(jnp.bfloat16)
        rows = pl.ds(pl.multiple_of(first_q * waves, count), count)
        total = (sum_ref[rows, :] + times(order_ref[...], block)).astype(jnp.bfloat16)
        ref[0] = total.reshape(GROUP, waves, width)
        for q in range(GROUP):
            part = total[q * waves : (q + 1) * waves]
            found = found + times_turned(part, weight_ref[half * GROUP + q])
    in_grad_ref[:waves] += found


def pixel_back_kernel(
    counts_ref, wave_row_ref, big_slope_ref, slope_ref, pix_grad_ref, starts_ref, choice_ref, turn_ref
):
    step = pl.program_id(0)
    patches, per_step, _ = pix_grad_ref.shape
    positions, waves, _ = big_slope_ref.shape

    @pl.when(step == 0)
    def _():
        _, big_lo, big_hi = fill_starts(counts_ref, starts_ref)
        fill_choice(wave_row_ref, choice_ref, waves, big_lo, big_hi)

    first_q = pl.multiple_of(step * per_step, per_step)
    for q in range(per_step):
        alone = strided(slope_ref, first_q + q, SMALL, positions).astype(jnp.bfloat16)
        chosen = jnp.concatenate([big_slope_ref[first_q + q], alone], axis=0)
        spread = turned_times(chosen, choice_ref[: waves + SMALL])
        for c in range(turn_ref.shape[0]):
            turn_ref[c, pl.ds(q, patches, stride=per_step), :] = spread[
                :patches, c * LANES : (c + 1) * LANES
            ]
    for c in range(turn_ref.shape[0]):
        pix_grad_ref[:, :, c * LANES : (c + 1) * LANES] = (
            turn_ref[c].astype(jnp.bfloat16).reshape(patches, per_step, LANES)
        )


def pixel_back_call(counts, band_waves, big_slope, slope, patches):
    positions = big_slope.shape[0]
    slots = band_waves.shape[0]
    per_step = positions // STEPS
    return pl.pallas_call(
        pixel_back_kernel,
        grid=(STEPS,),
        in_specs=[
            pl.BlockSpec(memory_space=pltpu.SMEM),
            whole(1, slots),
            whole(*big_slope.shape),
            whole(*slope.shape),
        ],
        out_specs=pl.BlockSpec((patches, per_step, slots), lambda i: (0, i, 0)),
        out_shape=jax.ShapeDtypeStruct((patches, positions, slots), jnp.bfloat16),
        scratch_shapes=[
            pltpu.SMEM((counts.shape[0] + 1,), jnp.int32),
            pltpu.VMEM((LANES, slots), jnp.bfloat16),
            pltpu.VMEM((slots // LANES, patches * per_step, LANES), jnp.float32),
        ],
        compiler_params=pltpu.CompilerParams(vmem_limit_bytes=VMEM_LIMIT),
        cost_estimate=cost(1 << 20, 1 << 10),
        name="pixel_back",
    )(counts, band_waves[None], big_slope, slope)


def embed_back_call(place, odd, counts, band_waves, grads, kept, kernel_weight, vectors):
    positions, waves, padded = kept[0].shape
    width = kept[2].shape[2]
    images = counts.shape[0]
    pairs = positions // (2 * GROUP)
    block = (1, GROUP, waves, width)
    depth = kernel_weight.shape[1]
    smem = pl.BlockSpec(memory_space=pltpu.SMEM)
    return pl.pallas_call(
        embed_back_kernel,
        grid=(pairs,),
        in_specs=[
            smem,
            smem,
            smem,
            smem,
            *[pl.BlockSpec(memory_space=pl.ANY)] * 4,
            *[whole(*array.shape) for array in kept],
            pl.BlockSpec((2 * GROUP, depth, width), lambda i: (i, 0, 0)),
            whole(*vectors.shape),
        ],
        out_specs=[
            *[pl.BlockSpec(block, lambda i: (i, 0, 0, 0))] * 2,
            whole(positions, waves, 2 * LANES),
            whole(2, SMALL * positions, LANES),
            whole(waves + vectors.shape[0], depth),
        ],
        out_shape=[
            *[jax.ShapeDtypeStruct((pairs, *block[1:]), jnp.bfloat16)] * 2,
            jax.ShapeDtypeStruct((positions, waves, 2 * LANES), jnp.bfloat16),
            jax.ShapeDtypeStruct((2, SMALL * positions, LANES), jnp.float32),
            jax.ShapeDtypeStruct((waves + vectors.shape[0], depth), jnp.float32),
        ],
        scratch_shapes=[
            pltpu.SMEM((images + 1,), jnp.int32),
            pltpu.VMEM((GROUP * waves, GROUP * waves), jnp.bfloat16),
            pltpu.VMEM((images, padded, width), jnp.bfloat16),
            pltpu.VMEM((positions * waves, width), jnp.float32),
            pltpu.VMEM((waves, positions, width), jnp.float32),
            pltpu.SemaphoreType.DMA((4,)),
        ],
        compiler_params=pltpu.CompilerParams(vmem_limit_bytes=VMEM_LIMIT),
        name="embed_back",
    )(place, odd, counts, band_waves, *grads, *kept, kernel_weight, vectors)


HEADS = 12
WD = 128
WHEADS = 4


highest = lax.Precision.HIGHEST


def layer_norm(values, norm_gain, norm_shift, epsilon):
    centered = values - jnp.mean(values, axis=-1, keepdims=True)
    variance = jnp.mean(centered * centered, axis=-1, keepdims=True)
    return centered * lax.rsqrt(variance + epsilon) * norm_gain + norm_shift


def wave_embed(wavelengths):
    halfwidth = WD // 2
    indices = jnp.arange(halfwidth, dtype=jnp.float32)
    frequency = 1.0 / 10000.0 ** (indices / halfwidth)
    angles = (wavelengths * 1000.0)[:, None] * frequency[None, :]
    return jnp.concatenate([jnp.sin(angles), jnp.cos(angles)], axis=1)


def product(left, right, axes=(1, 0)):
    return lax.dot_general(
        left,
        right,
        (((axes[0],), (axes[1],)), ((), ())),
        precision=highest,
        preferred_element_type=jnp.float32,
    )


@jax.custom_vjp
def dot_rows(left, right):
    return product(left, right)


def dot_rows_forward(left, right):
    return product(left, right), (left, right)


def dot_rows_backward(saved, slope):
    left, right = saved
    return product(slope, right, (1, 1)), product(left, slope, (0, 0))


dot_rows.defvjp(dot_rows_forward, dot_rows_backward)


@jax.custom_vjp
def dot_turned(left, right):
    return product(left, right, (1, 1))


def dot_turned_forward(left, right):
    return product(left, right, (1, 1)), (left, right)


def dot_turned_backward(saved, slope):
    left, right = saved
    return product(slope, right), product(slope, left, (0, 0))


dot_turned.defvjp(dot_turned_forward, dot_turned_backward)


def hypernet(sequence, length, wave_qkv, wave_proj, wave_gain, wave_shift, wave_up, wave_down, kernel_gain, kernel_shift):
    rows, width = sequence.shape
    head_width = width // WHEADS
    projected = dot_rows(sequence, wave_qkv)
    queries, keys, values = (projected[:, i * width : (i + 1) * width] for i in range(3))
    of_head = lax.broadcasted_iota(jnp.int32, (rows, width), 1) // head_width
    real = lax.broadcasted_iota(jnp.int32, (rows, rows), 1) < length
    attended = jnp.zeros((rows, width), jnp.float32)
    for h in range(WHEADS):
        mine = (of_head == h).astype(jnp.float32)
        scores = dot_turned(queries * mine, keys) * (1.0 / math.sqrt(head_width))
        scores = jnp.where(real, scores, -1e30)
        raised = jnp.exp(scores - lax.stop_gradient(jnp.max(scores, axis=-1, keepdims=True)))
        weights = raised / jnp.sum(raised, axis=-1, keepdims=True)
        attended = attended + dot_rows(weights, values * mine)
    normed_first = layer_norm(
        sequence + dot_rows(attended, wave_proj), wave_gain, wave_shift, 1e-05
    )
    upward = dot_rows(normed_first, wave_up)
    widened = 0.5 * upward * (1.0 + lax.erf(upward * math.sqrt(0.5)))
    return layer_norm(
        normed_first + dot_rows(widened, wave_down), kernel_gain, kernel_shift, 1e-05
    )


def hyper_kernel(sequence_ref, *refs):
    params, (head_ref, low_ref, bias_ref) = refs[:8], refs[8:]
    waves = low_ref.shape[0]
    second = hypernet(sequence_ref[...], waves + 1, *(ref[...] for ref in params))
    low_ref[...] = (second[:waves] + sequence_ref[:waves]).astype(jnp.bfloat16)
    bias_ref[...] = product(second[waves : waves + 8], head_ref[...])


def hyper_call(sequence, params, bias_head, waves):
    depth = sequence.shape[1]
    return pl.pallas_call(
        hyper_kernel,
        out_shape=[
            jax.ShapeDtypeStruct((waves, depth), jnp.bfloat16),
            jax.ShapeDtypeStruct((8, bias_head.shape[1]), jnp.float32),
        ],
        compiler_params=pltpu.CompilerParams(vmem_limit_bytes=VMEM_LIMIT),
        cost_estimate=cost(1 << 20, 1 << 10),
        name="hyper",
    )(sequence, *params, bias_head)


def hyper_back_kernel(sequence_ref, in_grad_ref, bias_grad_ref, *refs):
    params, head_ref, outs, head_grad_ref = refs[:8], refs[8], refs[9:18], refs[18]
    rows, depth = sequence_ref.shape
    waves = in_grad_ref.shape[0]

    def apply(sequence, *values):
        return hypernet(sequence, waves + 1, *values)

    second, back = jax.vjp(apply, sequence_ref[...], *(ref[...] for ref in params))
    row = lax.broadcasted_iota(jnp.int32, (8, 1), 0)
    bias_grad = jnp.where(row == 0, bias_grad_ref[...], 0.0)
    last = product(bias_grad, head_ref[...], (1, 1))
    parts = [in_grad_ref[...], last]
    if rows > waves + 8:
        parts.append(jnp.zeros((rows - waves - 8, depth), jnp.float32))
    sequence_grad, *grads = back(jnp.concatenate(parts, axis=0))
    outs[0][...] = sequence_grad[waves : waves + 8]
    for ref, grad in zip(outs[1:], grads, strict=True):
        ref[...] = grad
    head_grad_ref[...] = product(second[waves : waves + 8], bias_grad, (0, 0))


def hyper_back_call(sequence, in_grad, bias_grad, params, bias_head):
    depth = sequence.shape[1]
    shapes = [(8, depth), *[p.shape for p in params], bias_head.shape]
    return pl.pallas_call(
        hyper_back_kernel,
        out_shape=[jax.ShapeDtypeStruct(shape, jnp.float32) for shape in shapes],
        compiler_params=pltpu.CompilerParams(vmem_limit_bytes=VMEM_LIMIT),
        cost_estimate=cost(1 << 20, 1 << 10),
        name="hyper_back",
    )(sequence, in_grad, bias_grad, *params, bias_head)


def swap_core(array):
    return lax.ppermute(array, "rows", [(0, 1), (1, 0), (2, 3), (3, 2)])


def swap_chip(array):
    return lax.ppermute(array, "rows", [(0, 2), (2, 0), (1, 3), (3, 1)])


def add_wide(left, right):
    return left.astype(jnp.float32) + right.astype(jnp.float32)


def rows_reduce(own, core, chip, far):
    passed = add_wide(chip, swap_core(far)).astype(jnp.bfloat16)
    return own, swap_core(core), swap_chip(passed)


def swap_band(array, bit):
    count = lax.axis_size("band")
    return lax.ppermute(array, "band", [(i, i ^ (1 << bit)) for i in range(count)])


def split(array, axis, bit):
    half = array.shape[axis] // 2
    return (
        lax.dynamic_slice_in_dim(array, bit * half, half, axis),
        lax.dynamic_slice_in_dim(array, (1 - bit) * half, half, axis),
    )


def split_band(array, bit, below=1):
    place = lax.axis_index("band")
    parts, bands, *rest = array.shape
    array = array.reshape(parts, bands // (2 * below), 2, below, *rest)
    halves = split(array, 2, (place >> bit) & 1)
    return [half.reshape(parts, bands // 2, *rest) for half in halves]


def add(kept, met):
    return add_wide(kept, met).astype(kept.dtype)


def band_step(array, bit, below=1):
    kept, sent = split_band(array, bit, below)
    return add(kept, swap_band(sent, bit))


def band_rest(array, first):
    for bit in range(first, lax.axis_size("band").bit_length() - 1):
        array = band_step(array, bit)
    return array


def join(own, other, bit, axis):
    return jnp.where(
        bit == 0,
        jnp.concatenate([own, other], axis=axis),
        jnp.concatenate([other, own], axis=axis),
    )


def weight_gather(array, chip_first):
    place = lax.axis_index("rows")
    chip, core = place // 2, place % 2
    if chip_first:
        array = join(array, swap_chip(array), chip, 1)
    else:
        array = add_wide(array, swap_chip(array)).astype(array.dtype)
    return join(array, swap_core(array), core, 2).astype(jnp.float32)


def by_band(array):
    parts, rows, width = array.shape
    bands = lax.axis_size("band")
    return array.reshape(parts, bands, rows // bands, width)


def together(*arrays):
    return lax.optimization_barrier(arrays)


def side_by_side(parts):
    return parts.transpose(1, 0, 2).reshape(parts.shape[1], -1)


def band_bits():
    return range(lax.axis_size("band").bit_length() - 1)


def sum_steps(array, bits):
    for bit in bits:
        array = array + swap_band(array, bit)
    return array


def slot_masks(counts, slot_waves, waves):
    index = jnp.arange(counts.shape[0])
    ends = jnp.sum(jnp.where(index[None, :] <= index[:, None], counts[None, :], 0), axis=1)
    slots = jnp.arange(slot_waves.shape[0])
    owners = jnp.sum((ends[None, :] <= slots[:, None]).astype(jnp.int32), axis=1)
    return (
        (owners[:, None] == index[None, :]).astype(jnp.bfloat16),
        (slot_waves[:, None] == jnp.arange(waves)[None, :]).astype(jnp.bfloat16),
    )


def embed_plain(counts, slot_waves, kernel_low, kernel_weight, pixels):
    slots, positions, patches = pixels.shape
    table = jnp.einsum(
        "wk,qkc->wqc", kernel_low, kernel_weight, preferred_element_type=jnp.float32
    ).astype(jnp.bfloat16)
    of_image, of_wave = slot_masks(counts, slot_waves, table.shape[0])
    chunk = min(16, slots)

    def part(running, inputs):
        pixel, image, wave = inputs
        chosen = jnp.einsum("sw,wqc->sqc", wave, table)
        rows = jnp.einsum("sqp,sqc->spc", pixel, chosen, preferred_element_type=jnp.float32)
        image = image.astype(jnp.float32)
        return (running + jnp.einsum("si,spc->ipc", image, rows, precision=highest), None)

    shape = (counts.shape[0], patches, table.shape[2])
    total = lax.scan(
        part,
        jnp.zeros(shape, jnp.float32),
        tuple(a.reshape(-1, chunk, *a.shape[1:]) for a in (pixels, of_image, of_wave)),
    )[0]
    extra = pad_rows(patches) - patches
    return (jnp.pad(total.astype(jnp.bfloat16), ((0, 0), (0, extra), (0, 0))), table)


def embed_back_plain(counts, slot_waves, grads, table, pixels):
    slots, positions, patches = pixels.shape
    waves, _, width = table.shape
    of_image, of_wave = slot_masks(counts, slot_waves, waves)
    grads = grads[:, :patches]
    chunk = min(16, slots)

    def part(running, inputs):
        pixel, image, wave = inputs
        chosen = jnp.einsum("sw,wqc->sqc", wave, table)
        slope = jnp.einsum("si,ipc->spc", image, grads)
        own = jnp.einsum("sqc,spc->sqp", chosen, slope, preferred_element_type=jnp.float32)
        more = jnp.einsum("sqp,spc->sqc", pixel, slope, preferred_element_type=jnp.float32)
        wave = wave.astype(jnp.float32)
        added = jnp.einsum("sw,sqc->qwc", wave, more, precision=highest)
        return (running + added, own.astype(jnp.bfloat16))

    kernel_grad, pixel_grad = lax.scan(
        part,
        jnp.zeros((positions, waves, width), jnp.float32),
        tuple(a.reshape(-1, chunk, *a.shape[1:]) for a in (pixels, of_image, of_wave)),
    )
    return (pixel_grad.reshape(pixels.shape), kernel_grad.astype(jnp.bfloat16))


def body(
    pixels,
    band_counts,
    band_waves,
    wavelengths,
    bias_token,
    wave_qkv,
    wave_proj,
    wave_gain,
    wave_shift,
    wave_up,
    wave_down,
    kernel_gain,
    kernel_shift,
    bias_head,
    kernel_weight,
    attention_gain,
    attention_shift,
    block_qkv,
    block_proj,
    hidden_gain,
    hidden_shift,
    block_up,
    block_down,
    cotangent,
):
    waves, depth = wavelengths.shape[0], bias_token.shape[0]
    sequence = jnp.concatenate(
        [
            wave_embed(wavelengths),
            bias_token[None],
            jnp.zeros((-(waves + 1) % 8, depth), jnp.float32),
        ]
    )
    hyper_params = (
        wave_qkv,
        wave_proj,
        wave_gain[None],
        wave_shift[None],
        wave_up,
        wave_down,
        kernel_gain[None],
        kernel_shift[None],
    )
    kernel_low, conv_bias = hyper_call(sequence, hyper_params, bias_head, waves)
    conv_bias = conv_bias[0]
    counts = band_counts[0]
    slot_waves = band_waves[0]
    slot_total, positions, patches = pixels.shape
    images = counts.shape[0]
    width = kernel_weight.shape[2]
    bands = lax.axis_size("band")
    fits = waves * positions * width <= 1 << 21 and positions == bands * GROUP
    place = lax.axis_index("rows").astype(jnp.int32)
    padded = pad_rows(patches)
    if fits:
        turned_pixels = pixels.transpose(2, 1, 0)
        *blocks, kept_big, kept_small, kept_rows, kept_table = embed_call(
            place[None], counts, slot_waves, kernel_low, kernel_weight, turned_pixels
        )
    else:
        partial_rows, kernel_table = embed_plain(
            counts, slot_waves, kernel_low, kernel_weight, pixels
        )
        partial_rows = partial_rows.reshape(4, -1, padded, width)
        blocks = [lax.dynamic_index_in_dim(partial_rows, place ^ k, 0, False) for k in range(4)]
    terms = [term.reshape(-1, width) for term in rows_reduce(*blocks)]
    local_images = images // 4
    cot = jnp.pad(
        cotangent.reshape(local_images, patches, width), ((0, 0), (0, padded - patches), (0, 0))
    ).reshape(-1, width)
    x, normed, projected, probs, mixed, middle, normed_mid = attend_call(
        terms,
        conv_bias,
        attention_gain,
        attention_shift,
        block_qkv,
        block_proj,
        hidden_gain,
        hidden_shift,
        padded,
        patches,
    )
    core = (lax.axis_index("rows") % 2).astype(jnp.int32)[None]
    chip = lax.axis_index("rows") // 2
    (
        result,
        grad_middle,
        grad_low,
        down_kept,
        down_sent,
        up_kept,
        up_sent,
        hidden_gain_part,
        hidden_shift_part,
    ) = mlp_call(core, normed_mid, middle, cot, hidden_gain, block_up, block_down)
    layer_output = result.reshape(local_images, padded, width)[:, :patches].reshape(-1, width)
    down_met, up_met = swap_core(down_sent), swap_core(up_sent)
    grad_projected = attend_back_call(grad_low, projected, probs, block_proj, padded, 0, 1)
    grad_projected, down_met, up_met = together(grad_projected, down_met, up_met)
    down_kept, down_sent = split_band(
        by_band(add(down_kept, down_met).reshape(1, -1, width // 2)), 0
    )
    up_kept, up_sent = split(by_band(add(up_kept, up_met)), 2, chip)
    grad_projected, down_kept, down_sent, up_kept, up_sent = together(
        grad_projected, down_kept, down_sent, up_kept, up_sent
    )
    down_met, up_met = swap_band(down_sent, 0), swap_chip(up_sent)
    grad_projected = attend_back_call(
        grad_low, projected, probs, block_proj, padded, 1, local_images - 1, grad_projected
    )
    grad_x, bias_part, attention_gain_part, attention_shift_part = first_norm_back_call(
        grad_projected, grad_middle, x, attention_gain, block_qkv
    )
    grad_x, grad_projected, down_met, up_met = together(grad_x, grad_projected, down_met, up_met)
    own = grad_x.reshape(local_images, padded, width)
    near, across = swap_core(own), swap_chip(own)
    near, grad_low = together(near, grad_low)
    down_kept, down_sent = split_band(add(down_kept, down_met), 1)
    up_kept, up_sent = split_band(add(up_kept, up_met), 0)
    down_met, up_met = swap_band(down_sent, 1), swap_band(up_sent, 0)
    attend_kept, attend_sent = attend_weights_call(core, normed, mixed, grad_projected, grad_low)
    across, attend_kept, attend_sent, down_met, up_met = together(
        across, attend_kept, attend_sent, down_met, up_met
    )
    far, attend_met = swap_core(across), swap_core(attend_sent)
    down_kept, down_sent = split_band(add(down_kept, down_met), 2)
    up_kept, up_sent = split_band(add(up_kept, up_met), 1)
    far, attend_met, down_kept, down_sent, up_kept, up_sent = together(
        far, attend_met, down_kept, down_sent, up_kept, up_sent
    )
    attend_kept, attend_sent = split(by_band(add(attend_kept, attend_met)), 2, chip)
    attend_kept, attend_sent, near = together(attend_kept, attend_sent, near)
    attend_met = swap_chip(attend_sent)
    down_met, up_met = swap_band(down_sent, 2), swap_band(up_sent, 1)
    gathered = own, near, across, far
    odd = (lax.axis_index("band") % 2).astype(jnp.int32)[None]
    vectors = jnp.concatenate(
        [
            bias_part,
            attention_gain_part,
            attention_shift_part,
            hidden_gain_part,
            hidden_shift_part,
        ]
    ).reshape(-1, kernel_weight.shape[1])
    if fits:
        kernel_kept, kernel_sent, big_slope, slope, summed = embed_back_call(
            place[None],
            odd,
            counts,
            slot_waves,
            gathered,
            (kept_big, kept_small, kept_rows, kept_table),
            kernel_weight,
            vectors,
        )
        kernel_kept, kernel_sent = kernel_kept[None], kernel_sent[None]
    else:
        stacked = jnp.stack(gathered)
        ordered = jnp.concatenate(
            [lax.dynamic_index_in_dim(stacked, place ^ k, 0, False) for k in range(4)]
        )
        pixel_grad, kernel_grad = embed_back_plain(
            counts, slot_waves, ordered, kernel_table, pixels
        )
        in_part = jnp.einsum(
            "qwc,qkc->wk", kernel_grad, kernel_weight, preferred_element_type=jnp.float32
        )
        summed = jnp.concatenate([in_part, vectors])
        kernel_kept, kernel_sent = split_band(kernel_grad.reshape(1, bands, -1, waves, width), 0)
        big_slope = slope = summed
    kernel_kept, kernel_sent, big_slope, summed, down_met, up_met, attend_met = together(
        kernel_kept, kernel_sent, big_slope, summed, down_met, up_met, attend_met
    )
    bits = band_bits()
    kernel_met = swap_band(kernel_sent, 0)
    summed = summed + swap_core(summed)
    summed, big_slope, down_met, up_met, attend_met = together(
        summed, big_slope, down_met, up_met, attend_met
    )
    attend_sum = add(attend_kept, attend_met)
    for bit in bits[1:-1]:
        attend_sum = band_step(attend_sum, bit, 2)
    attend_kept, attend_sent = split_band(attend_sum, bits[-1], 2)
    attend_kept, attend_sent, big_slope = together(attend_kept, attend_sent, big_slope)
    attend_sum = add(attend_kept, swap_band(attend_sent, bits[-1]))
    down_all = band_rest(add(down_kept, down_met), 3)[:, 0]
    block_down_grad = weight_gather(down_all, False)[0]
    up_all = band_rest(add(up_kept, up_met), 2)[:, 0]
    if fits:
        pixel_grad = pixel_back_call(counts, slot_waves, big_slope, slope, patches)
        pixel_grad = pixel_grad.transpose(2, 1, 0)
    summed = sum_steps(summed, bits[1:])
    kernel_met, pixel_grad, summed, up_all, attend_sum, block_down_grad = together(
        kernel_met, pixel_grad, summed, up_all, attend_sum, block_down_grad
    )
    kernel_kept, kernel_sent = split_band(add(kernel_kept, kernel_met), 1)
    kernel_kept, kernel_sent, attend_sum = together(kernel_kept, kernel_sent, attend_sum)
    kernel_met = swap_band(kernel_sent, 1)
    attend_all = band_step(attend_sum, 0)[:, 0]
    kernel_met, attend_all, up_all, summed = together(kernel_met, attend_all, up_all, summed)
    owned = add(kernel_kept, kernel_met)
    for bit in bits[2:-1]:
        owned = band_step(owned, bit)
    owned, summed, attend_all, up_all = together(owned, summed, attend_all, up_all)
    owned_met = swap_band(owned, bits[-1])
    block_up_grad = side_by_side(weight_gather(up_all, True))
    summed = summed + swap_chip(summed)
    summed = sum_steps(summed, bits[:1])
    owned, owned_met, summed, attend_all, block_up_grad = together(
        owned, owned_met, summed, attend_all, block_up_grad
    )
    owned = add(owned, owned_met)[0]
    attend_grads = weight_gather(attend_all, True)
    block_qkv_grad, block_proj_grad = side_by_side(attend_grads[:3]), attend_grads[3]
    half_bands = bands // 2
    upper = lax.axis_index("band") // half_bands
    owned_weight = jnp.einsum(
        "wk,qwc->qkc",
        lax.dynamic_slice_in_dim(kernel_low, upper * (depth // 2), depth // 2, 1),
        owned.reshape(-1, waves, width),
        preferred_element_type=jnp.float32,
    ).astype(jnp.bfloat16)
    owned_weight, summed = together(owned_weight, summed)
    grad_kernel_in = summed[:waves]
    bias_grad, attention_gain_grad, attention_shift_grad, hidden_gain_grad, hidden_shift_grad = (
        summed[waves:].reshape(5, width)
    )
    groups = [list(range(half_bands)), list(range(half_bands, bands))]
    kernel_weight_grad = lax.all_to_all(
        owned_weight, "band", split_axis=1, concat_axis=0, tiled=True, axis_index_groups=groups
    )
    kernel_weight_grad = (
        kernel_weight_grad.reshape(half_bands, 2, positions // bands, depth // bands, width)
        .transpose(1, 0, 2, 3, 4)
        .reshape(positions, depth // bands, width)
        .astype(jnp.float32)
    )
    token_grad, *hyper_grads = hyper_back_call(
        sequence, grad_kernel_in, bias_grad[None], hyper_params, bias_head
    )
    return (
        layer_output,
        pixel_grad,
        kernel_weight_grad,
        token_grad[0],
        hyper_grads[0],
        hyper_grads[1],
        hyper_grads[2][0],
        hyper_grads[3][0],
        hyper_grads[4],
        hyper_grads[5],
        hyper_grads[6][0],
        hyper_grads[7][0],
        hyper_grads[8],
        attention_gain_grad,
        attention_shift_grad,
        block_qkv_grad,
        block_proj_grad,
        hidden_gain_grad,
        hidden_shift_grad,
        block_up_grad,
        block_down_grad,
    )


def solution(mesh):
    in_specs = (
        P("band", "rows", None),
        P("band", None),
        P("band", None),
        P(),
        P(),
        P(),
        P(),
        P(),
        P(),
        P(),
        P(),
        P(),
        P(),
        P(),
        P("rows", None, None),
        P(),
        P(),
        P(),
        P(),
        P(),
        P(),
        P(),
        P(),
        P(("band", "rows"), None),
    )
    out_specs = (
        P(("band", "rows"), None),
        P("band", "rows", None),
        P("rows", "band", None),
        P(),
        P(),
        P(),
        P(),
        P(),
        P(),
        P(),
        P(),
        P(),
        P(),
        P(),
        P(),
        P("band", None),
        P("band", None),
        P(),
        P(),
        P("band", None),
        P("band", None),
    )
    return jax.shard_map(body, mesh=mesh, in_specs=in_specs, out_specs=out_specs, check_vma=False)
```

```python
import functools
import math

import jax
import jax.numpy as jnp
from jax import lax
from jax.experimental import pallas as pl
from jax.experimental.pallas import tpu as pltpu
from jax.sharding import PartitionSpec as P

VMEM_LIMIT = 60 * 1024 * 1024
STEPS = 4
QUAD = 4
GROUP = 8
SMALL = 64
LANES = 128
EPSILON = 1e-06
ROW_STEP = 48


def pad_rows(rows):
    return (rows + 15) // 16 * 16


over_last = (((1,), (1,)), ((), ()))
over_first = (((0,), (0,)), ((), ()))


def times(left, right):
    return jnp.dot(left, right, preferred_element_type=jnp.float32)


def times_turned(left, right):
    return lax.dot_general(left, right, over_last, preferred_element_type=jnp.float32)


def turned_times(left, right):
    return lax.dot_general(left, right, over_first, preferred_element_type=jnp.float32)


def norm_parts(values):
    centered = values - jnp.mean(values, axis=-1, keepdims=True)
    variance = jnp.mean(centered * centered, axis=-1, keepdims=True)
    scale = lax.rsqrt(variance + EPSILON)
    return centered * scale, scale


def norm_backward(values, slope, gain):
    unit, scale = norm_parts(values)
    inner = slope * gain
    mean = jnp.mean(inner, axis=-1, keepdims=True)
    along = jnp.mean(inner * unit, axis=-1, keepdims=True)
    return scale * (inner - mean - unit * along), slope * unit


def by_rows(total, fn):
    step = ROW_STEP if total % ROW_STEP == 0 else 2 * 8
    for row in range(0, total, step):
        fn(slice(row, row + step))


def attend_kernel(
    own_ref, core_ref, chip_ref, bias_ref, gain_ref, shift_ref, qkv_ref, proj_ref, mid_gain_ref, mid_shift_ref,
    x_ref, normed_ref, projected_ref, probs_ref, mixed_ref, middle_ref, normed_mid_ref,
    *, patches,
):
    padded, width = x_ref.shape
    head = width // HEADS

    def first(r):
        x = sum(ref[r, :].astype(jnp.float32) for ref in (own_ref, core_ref, chip_ref))
        x = x + bias_ref[...]
        x_ref[r, :] = x
        normed_ref[r, :] = (norm_parts(x)[0] * gain_ref[...] + shift_ref[...]).astype(jnp.bfloat16)

    by_rows(padded, first)
    for part in range(3):
        columns = slice(part * width, (part + 1) * width)
        projected_ref[:, columns] = times(normed_ref[...], qkv_ref[:, columns]).astype(jnp.bfloat16)
    lane = lax.broadcasted_iota(jnp.int32, (padded, LANES), 1)
    key = lax.broadcasted_iota(jnp.int32, (padded, padded), 1)
    factor = jnp.bfloat16(1.0 / math.sqrt(head))

    def pair_of(pair):
        def columns(part):
            return slice(part * width + pair * LANES, part * width + (pair + 1) * LANES)

        queries, keys, values = (projected_ref[:, columns(part)] for part in range(3))
        found = []
        for h in range(2):
            mine = (lane // head) == h
            scores = times_turned(jnp.where(mine, queries * factor, jnp.zeros_like(queries)), keys)
            scores = jnp.where(key < patches, scores, -1e30)
            raised = jnp.exp(scores - jnp.max(scores, axis=-1, keepdims=True))
            probs = raised * (1.0 / jnp.sum(raised, axis=-1, keepdims=True))
            low = probs.astype(jnp.bfloat16)
            probs_ref[pair * 2 + h] = low
            found.append(times(low, values))
        mixed_ref[:, columns(0)] = jnp.where(lane < head, found[0], found[1]).astype(jnp.bfloat16)

    for pair in range(HEADS // 2):
        pair_of(pair)
    middle_ref[...] = times(mixed_ref[...], proj_ref[...])

    def last(r):
        middle = middle_ref[r, :] + x_ref[r, :]
        middle_ref[r, :] = middle
        normed_mid_ref[r, :] = (
            norm_parts(middle)[0] * mid_gain_ref[...] + mid_shift_ref[...]
        ).astype(jnp.bfloat16)

    by_rows(padded, last)


def cost(flops, moved):
    return pl.CostEstimate(flops=flops, bytes_accessed=moved, transcendentals=0)


def whole(*shape):
    return pl.BlockSpec(shape, lambda *index: (0,) * len(shape))


def attend_call(terms, bias, gain, shift, qkv, proj, mid_gain, mid_shift, padded, patches):
    rows, width = terms[0].shape
    images = rows // padded
    row = lambda v: v.reshape(1, width)
    shapes = [
        ((rows, width), jnp.float32),
        ((rows, width), jnp.bfloat16),
        ((rows, 3 * width), jnp.bfloat16),
        ((images * HEADS, padded, padded), jnp.bfloat16),
        ((rows, width), jnp.bfloat16),
        ((rows, width), jnp.float32),
        ((rows, width), jnp.bfloat16),
    ]
    blocks = [
        pl.BlockSpec((HEADS, padded, padded), lambda i: (i, 0, 0))
        if len(shape) == 3
        else pl.BlockSpec((padded, shape[1]), lambda i: (i, 0))
        for shape, _ in shapes
    ]
    return pl.pallas_call(
        functools.partial(attend_kernel, patches=patches),
        grid=(images,),
        in_specs=[
            *[pl.BlockSpec((padded, width), lambda i: (i, 0))] * 3,
            *[whole(1, width)] * 3,
            whole(width, 3 * width),
            whole(width, width),
            *[whole(1, width)] * 2,
        ],
        out_specs=blocks,
        out_shape=[jax.ShapeDtypeStruct(*s) for s in shapes],
        compiler_params=pltpu.CompilerParams(vmem_limit_bytes=VMEM_LIMIT),
        cost_estimate=cost(20 << 30, 25 << 20),
        name="attend",
    )(*terms, row(bias), row(gain), row(shift), qkv, proj, row(mid_gain), row(mid_shift))


def store_halves(core_ref, product, kept_ref, sent_ref):
    half = product.shape[1] // 2
    left, right = product[:, :half].astype(jnp.bfloat16), product[:, half:].astype(jnp.bfloat16)
    first = core_ref[0] == 0
    kept_ref[0] = jnp.where(first, left, right)
    sent_ref[0] = jnp.where(first, right, left)


def mlp_kernel(
    core_ref, normed_ref, middle_ref, cot_ref, gain_ref, up_ref, down_ref,
    out_ref, grad_ref, low_ref, down_kept_ref, down_sent_ref, up_kept_ref, up_sent_ref,
    gain_grad_ref, shift_grad_ref,
    result_ref, slope_ref, wide_ref, back_ref, active_ref, grad_up_ref,
):
    step = pl.program_id(0)
    rows = normed_ref.shape[0]
    wide_ref[...] = times(normed_ref[...], up_ref[...])
    back_ref[...] = times_turned(cot_ref[...], down_ref[...])

    def middle_part(r):
        x = wide_ref[r, :]
        below = 0.5 * (1.0 + lax.erf(x * math.sqrt(0.5)))
        density = jnp.exp(-0.5 * x * x) * (1.0 / math.sqrt(2.0 * math.pi))
        active_ref[r, :] = (x * below).astype(jnp.bfloat16)
        grad_up_ref[r, :] = (back_ref[r, :] * (below + x * density)).astype(jnp.bfloat16)

    by_rows(rows, middle_part)
    product = turned_times(active_ref[...], cot_ref[...])
    store_halves(core_ref, product, down_kept_ref, down_sent_ref)
    product = turned_times(normed_ref[...], grad_up_ref[...])
    store_halves(core_ref, product, up_kept_ref, up_sent_ref)

    @pl.when(step == 0)
    def _():
        result_ref[...] = times(active_ref[...], down_ref[...])
        slope_ref[...] = times_turned(grad_up_ref[...], up_ref[...])

    @pl.when(step > 0)
    def _():
        result_ref[...] += times(active_ref[...], down_ref[...])
        slope_ref[...] += times_turned(grad_up_ref[...], up_ref[...])

    @pl.when(step == pl.num_programs(0) - 1)
    def _():
        gain_grad_ref[...] = jnp.zeros_like(gain_grad_ref)
        shift_grad_ref[...] = jnp.zeros_like(shift_grad_ref)

        def last(r):
            middle, slope = middle_ref[r, :], slope_ref[r, :]
            out_ref[r, :] = (middle + result_ref[r, :]).astype(jnp.bfloat16)
            back, terms = norm_backward(middle, slope, gain_ref[...])
            grad = cot_ref[r, :].astype(jnp.float32) + back
            grad_ref[r, :] = grad
            low_ref[r, :] = grad.astype(jnp.bfloat16)
            gain_grad_ref[...] += jnp.sum(terms, axis=0, keepdims=True)
            shift_grad_ref[...] += jnp.sum(slope, axis=0, keepdims=True)

        by_rows(rows, last)


def mlp_call(core, normed, middle, cot, gain, up, down):
    rows, width = middle.shape
    hidden = up.shape[1]
    steps = hidden // width
    f32, bf16 = jnp.float32, jnp.bfloat16
    half = (1, width, width // 2)
    return pl.pallas_call(
        mlp_kernel,
        grid=(steps,),
        in_specs=[
            pl.BlockSpec(memory_space=pltpu.SMEM),
            whole(rows, width),
            whole(rows, width),
            whole(rows, width),
            whole(1, width),
            pl.BlockSpec((width, width), lambda j: (0, j)),
            pl.BlockSpec((width, width), lambda j: (j, 0)),
        ],
        out_specs=[
            whole(rows, width),
            whole(rows, width),
            whole(rows, width),
            *[pl.BlockSpec(half, lambda j: (j, 0, 0))] * 4,
            whole(1, width),
            whole(1, width),
        ],
        out_shape=[
            jax.ShapeDtypeStruct((rows, width), bf16),
            jax.ShapeDtypeStruct((rows, width), f32),
            jax.ShapeDtypeStruct((rows, width), bf16),
            *[jax.ShapeDtypeStruct((steps, width, width // 2), bf16)] * 4,
            jax.ShapeDtypeStruct((1, width), f32),
            jax.ShapeDtypeStruct((1, width), f32),
        ],
        scratch_shapes=[pltpu.VMEM((rows, width), t) for t in (f32, f32, f32, f32, bf16, bf16)],
        compiler_params=pltpu.CompilerParams(vmem_limit_bytes=VMEM_LIMIT),
        cost_estimate=cost(12 * rows * width * hidden, 30 << 20),
        name="mlp",
    )(core, normed, middle, cot, gain.reshape(1, width), up, down)


def attend_back_kernel(low_ref, projected_ref, probs_ref, proj_ref, *refs):
    grad_projected_ref, mixed_grad_ref = refs[-2:]
    padded, width = low_ref.shape
    head = width // HEADS
    mixed_grad_ref[...] = times_turned(low_ref[...], proj_ref[...]).astype(jnp.bfloat16)
    lane = lax.broadcasted_iota(jnp.int32, (padded, LANES), 1)
    factor = jnp.bfloat16(1.0 / math.sqrt(head))

    def pair_of(pair):
        def columns(part):
            return slice(part * width + pair * LANES, part * width + (pair + 1) * LANES)

        queries, keys, values = (projected_ref[:, columns(part)] for part in range(3))
        queries, keys = queries * factor, keys * factor
        grads = mixed_grad_ref[:, columns(0)]
        found = [], [], []
        for h in range(2):
            mine = (lane // head) == h
            low = probs_ref[pair * 2 + h]
            probs = low.astype(jnp.float32)
            grad_probs = times_turned(jnp.where(mine, grads, jnp.zeros_like(grads)), values)
            scaled = grad_probs * probs
            total = jnp.sum(scaled, axis=-1, keepdims=True)
            grad_scores = (scaled - probs * total).astype(jnp.bfloat16)
            found[0].append(times(grad_scores, keys))
            found[1].append(turned_times(grad_scores, queries))
            found[2].append(turned_times(low, grads))
        for part in range(3):
            grad_projected_ref[:, columns(part)] = jnp.where(
                lane < head, found[part][0], found[part][1]
            ).astype(jnp.bfloat16)

    for pair in range(HEADS // 2):
        pair_of(pair)


def attend_back_call(low, projected, probs, proj, padded, first, count, begun=None):
    rows, width = low.shape
    return pl.pallas_call(
        attend_back_kernel,
        grid=(count,),
        in_specs=[
            pl.BlockSpec((padded, width), lambda i: (i + first, 0)),
            pl.BlockSpec((padded, 3 * width), lambda i: (i + first, 0)),
            pl.BlockSpec((HEADS, padded, padded), lambda i: (i + first, 0, 0)),
            whole(width, width),
            *([] if begun is None else [pl.BlockSpec(memory_space=pl.ANY)]),
        ],
        out_specs=pl.BlockSpec((padded, 3 * width), lambda i: (i + first, 0)),
        out_shape=jax.ShapeDtypeStruct((rows, 3 * width), jnp.bfloat16),
        scratch_shapes=[pltpu.VMEM((padded, width), jnp.bfloat16)],
        input_output_aliases={} if begun is None else {4: 0},
        compiler_params=pltpu.CompilerParams(vmem_limit_bytes=VMEM_LIMIT),
        cost_estimate=cost(count * (6 << 30), count * (5 << 20)),
        name="attend_back",
    )(low, projected, probs, proj, *([] if begun is None else [begun]))


def first_norm_back_kernel(
    grad_projected_ref, grad_ref, x_ref, gain_ref, qkv_ref,
    grad_x_ref, bias_grad_ref, gain_grad_ref, shift_grad_ref, slope_ref,
):
    rows, width = x_ref.shape
    slope_ref[...] = times_turned(grad_projected_ref[:, :width], qkv_ref[:, :width])
    for part in range(1, 3):
        columns = slice(part * width, (part + 1) * width)
        slope_ref[...] += times_turned(grad_projected_ref[:, columns], qkv_ref[:, columns])
    for ref in (bias_grad_ref, gain_grad_ref, shift_grad_ref):
        ref[...] = jnp.zeros_like(ref)

    def last(r):
        slope = slope_ref[r, :]
        back, terms = norm_backward(x_ref[r, :], slope, gain_ref[...])
        grad = grad_ref[r, :] + back
        grad_x_ref[r, :] = grad.astype(jnp.bfloat16)
        bias_grad_ref[...] += jnp.sum(grad, axis=0, keepdims=True)
        gain_grad_ref[...] += jnp.sum(terms, axis=0, keepdims=True)
        shift_grad_ref[...] += jnp.sum(slope, axis=0, keepdims=True)

    by_rows(rows, last)


def first_norm_back_call(grad_projected, grad, x, gain, qkv):
    rows, width = x.shape
    row = jax.ShapeDtypeStruct((1, width), jnp.float32)
    return pl.pallas_call(
        first_norm_back_kernel,
        out_shape=[jax.ShapeDtypeStruct((rows, width), jnp.bfloat16), row, row, row],
        scratch_shapes=[pltpu.VMEM((rows, width), jnp.float32)],
        compiler_params=pltpu.CompilerParams(vmem_limit_bytes=VMEM_LIMIT),
        cost_estimate=cost(1 << 30, 1 << 20),
        name="first_norm_back",
    )(grad_projected, grad, x, gain.reshape(1, width), qkv)


def attend_weights_kernel(
    core_ref, normed_ref, mixed_ref, grad_projected_ref, low_ref, kept_ref, sent_ref
):
    step = pl.program_id(0)

    @pl.when(step < 3)
    def _():
        product = turned_times(normed_ref[...], grad_projected_ref[...])
        store_halves(core_ref, product, kept_ref, sent_ref)

    @pl.when(step == 3)
    def _():
        product = turned_times(mixed_ref[...], low_ref[...])
        store_halves(core_ref, product, kept_ref, sent_ref)


def attend_weights_call(core, normed, mixed, grad_projected, low):
    rows, width = normed.shape
    half = (width, width // 2)
    return pl.pallas_call(
        attend_weights_kernel,
        grid=(4,),
        in_specs=[
            pl.BlockSpec(memory_space=pltpu.SMEM),
            whole(rows, width),
            whole(rows, width),
            pl.BlockSpec((rows, width), lambda j: (0, jnp.minimum(j, 2))),
            whole(rows, width),
        ],
        out_specs=[pl.BlockSpec((1, *half), lambda j: (j, 0, 0))] * 2,
        out_shape=[jax.ShapeDtypeStruct((4, *half), jnp.bfloat16)] * 2,
        compiler_params=pltpu.CompilerParams(vmem_limit_bytes=VMEM_LIMIT),
        cost_estimate=cost(8 * rows * width * width, 30 << 20),
        name="attend_weights",
    )(core, normed, mixed, grad_projected, low)


def fill_starts(counts_ref, starts_ref):
    images = counts_ref.shape[0]
    total, big, most, first = 0, 0, counts_ref[0], 0
    for m in range(images):
        starts_ref[m] = jnp.int32(total)
        if m:
            better = counts_ref[m] > most
            big = jnp.where(better, m, big)
            first = jnp.where(better, total, first)
            most = jnp.where(better, counts_ref[m], most)
        total = total + counts_ref[m]
    starts_ref[images] = jnp.int32(total)
    return big, first, first + most


def strided(ref, first, count, stride):
    parts = [ref[c, pl.ds(first, count, stride=stride), :] for c in range(ref.shape[0])]
    return jnp.concatenate(parts, axis=1)


def fill_choice(wave_row_ref, choice_ref, waves, big_lo, big_hi):
    slots = wave_row_ref.shape[1]
    slot = lax.broadcasted_iota(jnp.int32, (1, slots), 1)
    alone = waves + slot - jnp.where(slot >= big_hi, big_hi - big_lo, 0)
    column = jnp.where((slot >= big_lo) & (slot < big_hi), wave_row_ref[...], alone)
    index = lax.broadcasted_iota(jnp.int32, choice_ref.shape, 0)
    choice_ref[...] = jnp.where(index == column, 1.0, 0.0).astype(jnp.bfloat16)


def fill_spread(kin_ref, spread_ref):
    waves, depth = kin_ref.shape
    rows = waves * GROUP
    of_wave = lax.broadcasted_iota(jnp.int32, (rows, waves), 0) // GROUP
    pick = of_wave == lax.broadcasted_iota(jnp.int32, (rows, waves), 1)
    repeated = times(jnp.where(pick, 1.0, 0.0).astype(jnp.bfloat16), kin_ref[...])
    place = lax.broadcasted_iota(jnp.int32, (rows, depth), 0) % GROUP
    for q in range(GROUP):
        spread_ref[:, q * depth : (q + 1) * depth] = jnp.where(place == q, repeated, 0.0).astype(
            jnp.bfloat16
        )


def embed_kernel(
    place_ref, counts_ref, waves_ref, wave_row_ref, kin_ref, weight_ref, pix_ref,
    own_ref, core_ref, chip_ref, far_ref, big_out, small_out, rows_out, table_out,
    starts_ref, choice_ref, spread_ref, big_ref, small_ref, rows_ref, table_ref,
    turn_ref, wide_ref, acc_ref, semaphores,
):
    step = pl.program_id(0)
    waves, positions, width = table_ref.shape
    depth = kin_ref.shape[1]
    images = counts_ref.shape[0]
    patches, per_step, slots = pix_ref.shape
    padded = acc_ref.shape[0]
    held = own_ref.shape[0]
    big, big_lo, big_hi = fill_starts(counts_ref, starts_ref)

    @pl.when(step == 0)
    def _():
        fill_choice(wave_row_ref, choice_ref, waves, big_lo, big_hi)
        fill_spread(kin_ref, spread_ref)
        turn_ref[...] = jnp.zeros_like(turn_ref)

    first_q = pl.multiple_of(step * per_step, per_step)
    for q in range(per_step):
        rows_ref[first_q + q] = times(kin_ref[...], weight_ref[q]).astype(jnp.bfloat16)
    parts = []
    for q in range(0, per_step, GROUP):
        made = times(spread_ref[...], weight_ref[q : q + GROUP].reshape(GROUP * depth, width))
        parts.append(made.reshape(waves, GROUP, width))
    table_ref[:, pl.ds(first_q, per_step), :] = jnp.concatenate(parts, axis=1).astype(jnp.bfloat16)
    turn_ref[: patches * per_step] = times_turned(
        pix_ref[...].reshape(patches * per_step, slots), choice_ref[...]
    )
    for q in range(per_step):
        turned = turn_ref[pl.ds(q, 2 * LANES, stride=per_step), :].T
        big_ref[first_q + q] = turned[:waves, :padded].astype(jnp.bfloat16)
        for c in range(2):
            wide_ref[c, pl.ds(first_q + q, SMALL, stride=positions), :] = turned[
                waves : waves + SMALL, c * LANES : (c + 1) * LANES
            ]

    @pl.when(step == pl.num_programs(0) - 1)
    def _():
        def narrow(j, carry):
            rows = pl.ds(pl.multiple_of(j * positions, positions), positions)
            both = jnp.concatenate([wide_ref[0, rows, :], wide_ref[1, rows, :]], axis=1)
            small_ref[j] = both[:, :padded].astype(jnp.bfloat16)
            return carry

        lax.fori_loop(0, SMALL, narrow, 0, unroll=8)
        pairs = ((big_ref, big_out), (small_ref, small_out), (rows_ref, rows_out), (table_ref, table_out))
        copies = [
            pltpu.make_async_copy(source, target, semaphores.at[k])
            for k, (source, target) in enumerate(pairs)
        ]
        for copy in copies:
            copy.start()

        def store(m):
            block = (m // held) ^ place_ref[0]
            low = acc_ref[...].astype(jnp.bfloat16)
            for index, ref in enumerate((own_ref, core_ref, chip_ref, far_ref)):

                @pl.when(block == index)
                def _(ref=ref):
                    ref[m % held] = low

        acc_ref[...] = jnp.zeros_like(acc_ref)

        def big_part(j, carry):
            first = pl.ds(pl.multiple_of(j * GROUP, GROUP), GROUP)
            left = big_ref[first].reshape(GROUP * waves, padded)
            acc_ref[...] += turned_times(left, rows_ref[first].reshape(GROUP * waves, width))
            return carry

        lax.fori_loop(0, positions // GROUP, big_part, 0, unroll=True)
        store(big)

        def image(m, carry):
            first, last = starts_ref[m], starts_ref[m + 1]
            shift = jnp.where(first >= big_hi, big_lo - big_hi, 0)

            @pl.when(m != big)
            def _():
                acc_ref[...] = jnp.zeros_like(acc_ref)

                def part(j, carry):
                    lefts, rights = [], []
                    for k in range(QUAD):
                        s = first + j * QUAD + k
                        here = jnp.minimum(s, last - 1)
                        factor = jnp.where(s < last, 1.0, 0.0).astype(jnp.bfloat16)
                        lefts.append(small_ref[here + shift] * factor)
                        rights.append(table_ref[waves_ref[here]])
                    acc_ref[...] += turned_times(
                        jnp.concatenate(lefts, axis=0), jnp.concatenate(rights, axis=0)
                    )
                    return carry

                lax.fori_loop(0, (last - first + QUAD - 1) // QUAD, part, 0)
                store(m)

            return carry

        lax.fori_loop(0, images, image, 0)
        for copy in copies:
            copy.wait()


def embed_call(place, counts, band_waves, kernel_low, kernel_weight, pixels):
    patches, positions, slots = pixels.shape
    waves = kernel_low.shape[0]
    depth, width = kernel_weight.shape[1:]
    images = counts.shape[0]
    padded = pad_rows(patches)
    per_step = positions // STEPS
    smem = pl.BlockSpec(memory_space=pltpu.SMEM)
    block = (images // 4, padded, width)
    kept = [
        (positions, waves, padded),
        (SMALL, positions, padded),
        (positions, waves, width),
        (waves, positions, width),
    ]
    return pl.pallas_call(
        embed_kernel,
        grid=(STEPS,),
        in_specs=[
            smem,
            smem,
            smem,
            whole(1, slots),
            whole(waves, depth),
            pl.BlockSpec((per_step, depth, width), lambda i: (i, 0, 0)),
            pl.BlockSpec((patches, per_step, slots), lambda i: (0, i, 0)),
        ],
        out_specs=[*[whole(*block)] * 4, *[pl.BlockSpec(memory_space=pl.ANY)] * 4],
        out_shape=[
            *[jax.ShapeDtypeStruct(block, jnp.bfloat16)] * 4,
            *[jax.ShapeDtypeStruct(shape, jnp.bfloat16) for shape in kept],
        ],
        scratch_shapes=[
            pltpu.SMEM((images + 1,), jnp.int32),
            pltpu.VMEM((LANES, slots), jnp.bfloat16),
            pltpu.VMEM((waves * GROUP, GROUP * depth), jnp.bfloat16),
            *[pltpu.VMEM(shape, jnp.bfloat16) for shape in kept],
            pltpu.VMEM((2 * LANES * per_step, LANES), jnp.float32),
            pltpu.VMEM((2, SMALL * positions, LANES), jnp.float32),
            pltpu.VMEM((padded, width), jnp.float32),
            pltpu.SemaphoreType.DMA((4,)),
        ],
        compiler_params=pltpu.CompilerParams(vmem_limit_bytes=VMEM_LIMIT),
        name="embed",
    )(place, counts, band_waves, band_waves[None], kernel_low, kernel_weight, pixels)


def embed_back_kernel(
    place_ref, odd_ref, counts_ref, waves_ref, own_ref, core_ref, chip_ref, far_ref,
    big_ref, small_ref, rows_ref, table_ref, weight_ref, vectors_ref,
    kept_ref, sent_ref, big_slope_ref, slope_ref, in_grad_ref,
    starts_ref, order_ref, grad_ref, sum_ref, wide_ref, semaphores,
):
    step = pl.program_id(0)
    waves, positions, width = table_ref.shape
    padded = big_ref.shape[2]
    images = counts_ref.shape[0]
    held = own_ref.shape[0]
    place = place_ref[0]
    count = GROUP * waves

    def grads_of(m):
        return grad_ref[((m // held) ^ place) * held + m % held]

    @pl.when(step == 0)
    def _():
        copies = [
            pltpu.make_async_copy(ref, grad_ref.at[pl.ds(k * held, held)], semaphores.at[k])
            for k, ref in enumerate((own_ref, core_ref, chip_ref, far_ref))
        ]
        for copy in copies:
            copy.start()
        big, big_lo, big_hi = fill_starts(counts_ref, starts_ref)
        row = lax.broadcasted_iota(jnp.int32, (count, count), 0)
        column = lax.broadcasted_iota(jnp.int32, (count, count), 1)
        same = (row // waves == column % GROUP) & (row % waves == column // GROUP)
        order_ref[...] = jnp.where(same, 1.0, 0.0).astype(jnp.bfloat16)
        in_grad_ref[:waves] = jnp.zeros((waves, in_grad_ref.shape[1]), jnp.float32)
        in_grad_ref[waves:] = vectors_ref[...]
        slope_ref[...] = jnp.zeros_like(slope_ref)
        wide_ref[...] = jnp.zeros_like(wide_ref)
        for copy in copies:
            copy.wait()
        grads = grads_of(big)

        def big_part(j, carry):
            first = pl.ds(pl.multiple_of(j * GROUP, GROUP), GROUP)
            slope = times_turned(rows_ref[first].reshape(count, width), grads)
            big_slope_ref[first, :, :padded] = slope.astype(jnp.bfloat16).reshape(
                GROUP, waves, padded
            )
            sum_ref[pl.ds(pl.multiple_of(j * count, count), count), :] = times(
                big_ref[first].reshape(count, padded), grads
            )
            return carry

        lax.fori_loop(0, positions // GROUP, big_part, 0, unroll=True)

        def image(m, carry):
            first, last = starts_ref[m], starts_ref[m + 1]
            shift = jnp.where(first >= big_hi, big_lo - big_hi, 0)

            @pl.when(m != big)
            def _():
                grads = grads_of(m)

                def part(j, carry):
                    lefts, rights, index = [], [], []
                    for k in range(QUAD):
                        s = first + j * QUAD + k
                        here = jnp.minimum(s, last - 1)
                        factor = jnp.where(s < last, 1.0, 0.0).astype(jnp.bfloat16)
                        index.append(here)
                        lefts.append(table_ref[waves_ref[here]])
                        rights.append(small_ref[here + shift] * factor)
                    own = times_turned(jnp.concatenate(lefts, axis=0), grads)
                    more = times(jnp.concatenate(rights, axis=0), grads)
                    for k in range(QUAD):
                        part_rows = slice(k * positions, (k + 1) * positions)
                        row = pl.multiple_of((index[k] + shift) * positions, positions)
                        slope_ref[0, pl.ds(row, positions), :] = own[part_rows, :LANES]
                        slope_ref[1, pl.ds(row, positions), : padded - LANES] = own[
                            part_rows, LANES:
                        ]
                        wide_ref[waves_ref[index[k]]] += more[part_rows]
                    return carry

                lax.fori_loop(0, (last - first + QUAD - 1) // QUAD, part, 0)

            return carry

        lax.fori_loop(0, images, image, 0)

    odd = odd_ref[0]
    found = jnp.zeros((waves, in_grad_ref.shape[1]), jnp.float32)
    for ref, half in ((kept_ref, odd), (sent_ref, 1 - odd)):
        first_q = pl.multiple_of((2 * step + half) * GROUP, GROUP)
        block = wide_ref[:, pl.ds(first_q, GROUP), :].reshape(count, width).astype(jnp.bfloat16)
        rows = pl.ds(pl.multiple_of(first_q * waves, count), count)
        total = (sum_ref[rows, :] + times(order_ref[...], block)).astype(jnp.bfloat16)
        ref[0] = total.reshape(GROUP, waves, width)
        for q in range(GROUP):
            part = total[q * waves : (q + 1) * waves]
            found = found + times_turned(part, weight_ref[half * GROUP + q])
    in_grad_ref[:waves] += found


def pixel_back_kernel(
    counts_ref, wave_row_ref, big_slope_ref, slope_ref, pix_grad_ref, starts_ref, choice_ref, turn_ref
):
    step = pl.program_id(0)
    patches, per_step, _ = pix_grad_ref.shape
    positions, waves, _ = big_slope_ref.shape

    @pl.when(step == 0)
    def _():
        _, big_lo, big_hi = fill_starts(counts_ref, starts_ref)
        fill_choice(wave_row_ref, choice_ref, waves, big_lo, big_hi)

    first_q = pl.multiple_of(step * per_step, per_step)
    for q in range(per_step):
        alone = strided(slope_ref, first_q + q, SMALL, positions).astype(jnp.bfloat16)
        chosen = jnp.concatenate([big_slope_ref[first_q + q], alone], axis=0)
        spread = turned_times(chosen, choice_ref[: waves + SMALL])
        for c in range(turn_ref.shape[0]):
            turn_ref[c, pl.ds(q, patches, stride=per_step), :] = spread[
                :patches, c * LANES : (c + 1) * LANES
            ]
    for c in range(turn_ref.shape[0]):
        pix_grad_ref[:, :, c * LANES : (c + 1) * LANES] = (
            turn_ref[c].astype(jnp.bfloat16).reshape(patches, per_step, LANES)
        )


def pixel_back_call(counts, band_waves, big_slope, slope, patches):
    positions = big_slope.shape[0]
    slots = band_waves.shape[0]
    per_step = positions // STEPS
    return pl.pallas_call(
        pixel_back_kernel,
        grid=(STEPS,),
        in_specs=[
            pl.BlockSpec(memory_space=pltpu.SMEM),
            whole(1, slots),
            whole(*big_slope.shape),
            whole(*slope.shape),
        ],
        out_specs=pl.BlockSpec((patches, per_step, slots), lambda i: (0, i, 0)),
        out_shape=jax.ShapeDtypeStruct((patches, positions, slots), jnp.bfloat16),
        scratch_shapes=[
            pltpu.SMEM((counts.shape[0] + 1,), jnp.int32),
            pltpu.VMEM((LANES, slots), jnp.bfloat16),
            pltpu.VMEM((slots // LANES, patches * per_step, LANES), jnp.float32),
        ],
        compiler_params=pltpu.CompilerParams(vmem_limit_bytes=VMEM_LIMIT),
        cost_estimate=cost(1 << 20, 1 << 10),
        name="pixel_back",
    )(counts, band_waves[None], big_slope, slope)


def embed_back_call(place, odd, counts, band_waves, grads, kept, kernel_weight, vectors):
    positions, waves, padded = kept[0].shape
    width = kept[2].shape[2]
    images = counts.shape[0]
    pairs = positions // (2 * GROUP)
    block = (1, GROUP, waves, width)
    depth = kernel_weight.shape[1]
    smem = pl.BlockSpec(memory_space=pltpu.SMEM)
    return pl.pallas_call(
        embed_back_kernel,
        grid=(pairs,),
        in_specs=[
            smem,
            smem,
            smem,
            smem,
            *[pl.BlockSpec(memory_space=pl.ANY)] * 4,
            *[whole(*array.shape) for array in kept],
            pl.BlockSpec((2 * GROUP, depth, width), lambda i: (i, 0, 0)),
            whole(*vectors.shape),
        ],
        out_specs=[
            *[pl.BlockSpec(block, lambda i: (i, 0, 0, 0))] * 2,
            whole(positions, waves, 2 * LANES),
            whole(2, SMALL * positions, LANES),
            whole(waves + vectors.shape[0], depth),
        ],
        out_shape=[
            *[jax.ShapeDtypeStruct((pairs, *block[1:]), jnp.bfloat16)] * 2,
            jax.ShapeDtypeStruct((positions, waves, 2 * LANES), jnp.bfloat16),
            jax.ShapeDtypeStruct((2, SMALL * positions, LANES), jnp.float32),
            jax.ShapeDtypeStruct((waves + vectors.shape[0], depth), jnp.float32),
        ],
        scratch_shapes=[
            pltpu.SMEM((images + 1,), jnp.int32),
            pltpu.VMEM((GROUP * waves, GROUP * waves), jnp.bfloat16),
            pltpu.VMEM((images, padded, width), jnp.bfloat16),
            pltpu.VMEM((positions * waves, width), jnp.float32),
            pltpu.VMEM((waves, positions, width), jnp.float32),
            pltpu.SemaphoreType.DMA((4,)),
        ],
        compiler_params=pltpu.CompilerParams(vmem_limit_bytes=VMEM_LIMIT),
        name="embed_back",
    )(place, odd, counts, band_waves, *grads, *kept, kernel_weight, vectors)


HEADS = 12
WD = 128
WHEADS = 4


highest = lax.Precision.HIGHEST


def layer_norm(values, norm_gain, norm_shift, epsilon):
    centered = values - jnp.mean(values, axis=-1, keepdims=True)
    variance = jnp.mean(centered * centered, axis=-1, keepdims=True)
    return centered * lax.rsqrt(variance + epsilon) * norm_gain + norm_shift


def wave_embed(wavelengths):
    halfwidth = WD // 2
    indices = jnp.arange(halfwidth, dtype=jnp.float32)
    frequency = 1.0 / 10000.0 ** (indices / halfwidth)
    angles = (wavelengths * 1000.0)[:, None] * frequency[None, :]
    return jnp.concatenate([jnp.sin(angles), jnp.cos(angles)], axis=1)


def product(left, right, axes=(1, 0)):
    return lax.dot_general(
        left,
        right,
        (((axes[0],), (axes[1],)), ((), ())),
        precision=highest,
        preferred_element_type=jnp.float32,
    )


@jax.custom_vjp
def dot_rows(left, right):
    return product(left, right)


def dot_rows_forward(left, right):
    return product(left, right), (left, right)


def dot_rows_backward(saved, slope):
    left, right = saved
    return product(slope, right, (1, 1)), product(left, slope, (0, 0))


dot_rows.defvjp(dot_rows_forward, dot_rows_backward)


@jax.custom_vjp
def dot_turned(left, right):
    return product(left, right, (1, 1))


def dot_turned_forward(left, right):
    return product(left, right, (1, 1)), (left, right)


def dot_turned_backward(saved, slope):
    left, right = saved
    return product(slope, right), product(slope, left, (0, 0))


dot_turned.defvjp(dot_turned_forward, dot_turned_backward)


def hypernet(sequence, length, wave_qkv, wave_proj, wave_gain, wave_shift, wave_up, wave_down, kernel_gain, kernel_shift):
    rows, width = sequence.shape
    head_width = width // WHEADS
    projected = dot_rows(sequence, wave_qkv)
    queries, keys, values = (projected[:, i * width : (i + 1) * width] for i in range(3))
    of_head = lax.broadcasted_iota(jnp.int32, (rows, width), 1) // head_width
    real = lax.broadcasted_iota(jnp.int32, (rows, rows), 1) < length
    attended = jnp.zeros((rows, width), jnp.float32)
    for h in range(WHEADS):
        mine = (of_head == h).astype(jnp.float32)
        scores = dot_turned(queries * mine, keys) * (1.0 / math.sqrt(head_width))
        scores = jnp.where(real, scores, -1e30)
        raised = jnp.exp(scores - lax.stop_gradient(jnp.max(scores, axis=-1, keepdims=True)))
        weights = raised / jnp.sum(raised, axis=-1, keepdims=True)
        attended = attended + dot_rows(weights, values * mine)
    normed_first = layer_norm(
        sequence + dot_rows(attended, wave_proj), wave_gain, wave_shift, 1e-05
    )
    upward = dot_rows(normed_first, wave_up)
    widened = 0.5 * upward * (1.0 + lax.erf(upward * math.sqrt(0.5)))
    return layer_norm(
        normed_first + dot_rows(widened, wave_down), kernel_gain, kernel_shift, 1e-05
    )


def hyper_kernel(sequence_ref, *refs):
    params, (head_ref, low_ref, bias_ref) = refs[:8], refs[8:]
    waves = low_ref.shape[0]
    second = hypernet(sequence_ref[...], waves + 1, *(ref[...] for ref in params))
    low_ref[...] = (second[:waves] + sequence_ref[:waves]).astype(jnp.bfloat16)
    bias_ref[...] = product(second[waves : waves + 8], head_ref[...])


def hyper_call(sequence, params, bias_head, waves):
    depth = sequence.shape[1]
    return pl.pallas_call(
        hyper_kernel,
        out_shape=[
            jax.ShapeDtypeStruct((waves, depth), jnp.bfloat16),
            jax.ShapeDtypeStruct((8, bias_head.shape[1]), jnp.float32),
        ],
        compiler_params=pltpu.CompilerParams(vmem_limit_bytes=VMEM_LIMIT),
        cost_estimate=cost(1 << 20, 1 << 10),
        name="hyper",
    )(sequence, *params, bias_head)


def hyper_back_kernel(sequence_ref, in_grad_ref, bias_grad_ref, *refs):
    params, head_ref, outs, head_grad_ref = refs[:8], refs[8], refs[9:18], refs[18]
    rows, depth = sequence_ref.shape
    waves = in_grad_ref.shape[0]

    def apply(sequence, *values):
        return hypernet(sequence, waves + 1, *values)

    second, back = jax.vjp(apply, sequence_ref[...], *(ref[...] for ref in params))
    row = lax.broadcasted_iota(jnp.int32, (8, 1), 0)
    bias_grad = jnp.where(row == 0, bias_grad_ref[...], 0.0)
    last = product(bias_grad, head_ref[...], (1, 1))
    parts = [in_grad_ref[...], last]
    if rows > waves + 8:
        parts.append(jnp.zeros((rows - waves - 8, depth), jnp.float32))
    sequence_grad, *grads = back(jnp.concatenate(parts, axis=0))
    outs[0][...] = sequence_grad[waves : waves + 8]
    for ref, grad in zip(outs[1:], grads, strict=True):
        ref[...] = grad
    head_grad_ref[...] = product(second[waves : waves + 8], bias_grad, (0, 0))


def hyper_back_call(sequence, in_grad, bias_grad, params, bias_head):
    depth = sequence.shape[1]
    shapes = [(8, depth), *[p.shape for p in params], bias_head.shape]
    return pl.pallas_call(
        hyper_back_kernel,
        out_shape=[jax.ShapeDtypeStruct(shape, jnp.float32) for shape in shapes],
        compiler_params=pltpu.CompilerParams(vmem_limit_bytes=VMEM_LIMIT),
        cost_estimate=cost(14 << 30, 16 << 20),
        name="hyper_back",
    )(sequence, in_grad, bias_grad, *params, bias_head)


def swap_core(array):
    return lax.ppermute(array, "rows", [(0, 1), (1, 0), (2, 3), (3, 2)])


def swap_chip(array):
    return lax.ppermute(array, "rows", [(0, 2), (2, 0), (1, 3), (3, 1)])


def add_wide(left, right):
    return left.astype(jnp.float32) + right.astype(jnp.float32)


def rows_reduce(own, core, chip, far):
    passed = add_wide(chip, swap_core(far)).astype(jnp.bfloat16)
    return own, swap_core(core), swap_chip(passed)


def swap_band(array, bit):
    count = lax.axis_size("band")
    return lax.ppermute(array, "band", [(i, i ^ (1 << bit)) for i in range(count)])


def split(array, axis, bit):
    half = array.shape[axis] // 2
    return (
        lax.dynamic_slice_in_dim(array, bit * half, half, axis),
        lax.dynamic_slice_in_dim(array, (1 - bit) * half, half, axis),
    )


def split_band(array, bit, below=1):
    place = lax.axis_index("band")
    parts, bands, *rest = array.shape
    array = array.reshape(parts, bands // (2 * below), 2, below, *rest)
    halves = split(array, 2, (place >> bit) & 1)
    return [half.reshape(parts, bands // 2, *rest) for half in halves]


def add(kept, met):
    return add_wide(kept, met).astype(kept.dtype)


def split_sum(splitter, kept, met):
    return [add(*pair) for pair in zip(splitter(kept), splitter(met))]


def band_step(array, bit, below=1):
    kept, sent = split_band(array, bit, below)
    return add(kept, swap_band(sent, bit))


def band_rest(array, first):
    for bit in range(first, lax.axis_size("band").bit_length() - 1):
        array = band_step(array, bit)
    return array


def join(own, other, bit, axis):
    return jnp.where(
        bit == 0,
        jnp.concatenate([own, other], axis=axis),
        jnp.concatenate([other, own], axis=axis),
    )


def weight_gather(array, chip_first):
    place = lax.axis_index("rows")
    chip, core = place // 2, place % 2
    if chip_first:
        array = join(array, swap_chip(array), chip, 1)
    else:
        array = add_wide(array, swap_chip(array)).astype(array.dtype)
    return join(array, swap_core(array), core, 2).astype(jnp.float32)


def by_band(array):
    parts, rows, width = array.shape
    bands = lax.axis_size("band")
    return array.reshape(parts, bands, rows // bands, width)


def together(*arrays):
    return lax.optimization_barrier(arrays)


def side_by_side(parts):
    return parts.transpose(1, 0, 2).reshape(parts.shape[1], -1)


def band_bits():
    return range(lax.axis_size("band").bit_length() - 1)


def sum_steps(array, bits):
    for bit in bits:
        array = array + swap_band(array, bit)
    return array


def slot_masks(counts, slot_waves, waves):
    index = jnp.arange(counts.shape[0])
    ends = jnp.sum(jnp.where(index[None, :] <= index[:, None], counts[None, :], 0), axis=1)
    slots = jnp.arange(slot_waves.shape[0])
    owners = jnp.sum((ends[None, :] <= slots[:, None]).astype(jnp.int32), axis=1)
    return (
        (owners[:, None] == index[None, :]).astype(jnp.bfloat16),
        (slot_waves[:, None] == jnp.arange(waves)[None, :]).astype(jnp.bfloat16),
    )


def embed_plain(counts, slot_waves, kernel_low, kernel_weight, pixels):
    slots, positions, patches = pixels.shape
    table = jnp.einsum(
        "wk,qkc->wqc", kernel_low, kernel_weight, preferred_element_type=jnp.float32
    ).astype(jnp.bfloat16)
    of_image, of_wave = slot_masks(counts, slot_waves, table.shape[0])
    chunk = min(16, slots)

    def part(running, inputs):
        pixel, image, wave = inputs
        chosen = jnp.einsum("sw,wqc->sqc", wave, table)
        rows = jnp.einsum("sqp,sqc->spc", pixel, chosen, preferred_element_type=jnp.float32)
        image = image.astype(jnp.float32)
        return (running + jnp.einsum("si,spc->ipc", image, rows, precision=highest), None)

    shape = (counts.shape[0], patches, table.shape[2])
    total = lax.scan(
        part,
        jnp.zeros(shape, jnp.float32),
        tuple(a.reshape(-1, chunk, *a.shape[1:]) for a in (pixels, of_image, of_wave)),
    )[0]
    extra = pad_rows(patches) - patches
    return (jnp.pad(total.astype(jnp.bfloat16), ((0, 0), (0, extra), (0, 0))), table)


def embed_back_plain(counts, slot_waves, grads, table, pixels):
    slots, positions, patches = pixels.shape
    waves, _, width = table.shape
    of_image, of_wave = slot_masks(counts, slot_waves, waves)
    grads = grads[:, :patches]
    chunk = min(16, slots)

    def part(running, inputs):
        pixel, image, wave = inputs
        chosen = jnp.einsum("sw,wqc->sqc", wave, table)
        slope = jnp.einsum("si,ipc->spc", image, grads)
        own = jnp.einsum("sqc,spc->sqp", chosen, slope, preferred_element_type=jnp.float32)
        more = jnp.einsum("sqp,spc->sqc", pixel, slope, preferred_element_type=jnp.float32)
        wave = wave.astype(jnp.float32)
        added = jnp.einsum("sw,sqc->qwc", wave, more, precision=highest)
        return (running + added, own.astype(jnp.bfloat16))

    kernel_grad, pixel_grad = lax.scan(
        part,
        jnp.zeros((positions, waves, width), jnp.float32),
        tuple(a.reshape(-1, chunk, *a.shape[1:]) for a in (pixels, of_image, of_wave)),
    )
    return (pixel_grad.reshape(pixels.shape), kernel_grad.astype(jnp.bfloat16))


def body(
    pixels,
    band_counts,
    band_waves,
    wavelengths,
    bias_token,
    wave_qkv,
    wave_proj,
    wave_gain,
    wave_shift,
    wave_up,
    wave_down,
    kernel_gain,
    kernel_shift,
    bias_head,
    kernel_weight,
    attention_gain,
    attention_shift,
    block_qkv,
    block_proj,
    hidden_gain,
    hidden_shift,
    block_up,
    block_down,
    cotangent,
):
    waves, depth = wavelengths.shape[0], bias_token.shape[0]
    sequence = jnp.concatenate(
        [
            wave_embed(wavelengths),
            bias_token[None],
            jnp.zeros((-(waves + 1) % 8, depth), jnp.float32),
        ]
    )
    hyper_params = (
        wave_qkv,
        wave_proj,
        wave_gain[None],
        wave_shift[None],
        wave_up,
        wave_down,
        kernel_gain[None],
        kernel_shift[None],
    )
    kernel_low, conv_bias = hyper_call(sequence, hyper_params, bias_head, waves)
    conv_bias = conv_bias[0]
    counts = band_counts[0]
    slot_waves = band_waves[0]
    slot_total, positions, patches = pixels.shape
    images = counts.shape[0]
    width = kernel_weight.shape[2]
    bands = lax.axis_size("band")
    fits = waves * positions * width <= 1 << 21 and positions == bands * GROUP
    place = lax.axis_index("rows").astype(jnp.int32)
    padded = pad_rows(patches)
    if fits:
        turned_pixels = pixels.transpose(2, 1, 0)
        *blocks, kept_big, kept_small, kept_rows, kept_table = embed_call(
            place[None], counts, slot_waves, kernel_low, kernel_weight, turned_pixels
        )
    else:
        partial_rows, kernel_table = embed_plain(
            counts, slot_waves, kernel_low, kernel_weight, pixels
        )
        partial_rows = partial_rows.reshape(4, -1, padded, width)
        blocks = [lax.dynamic_index_in_dim(partial_rows, place ^ k, 0, False) for k in range(4)]
    terms = [term.reshape(-1, width) for term in rows_reduce(*blocks)]
    local_images = images // 4
    cot = jnp.pad(
        cotangent.reshape(local_images, patches, width), ((0, 0), (0, padded - patches), (0, 0))
    ).reshape(-1, width)
    x, normed, projected, probs, mixed, middle, normed_mid = attend_call(
        terms,
        conv_bias,
        attention_gain,
        attention_shift,
        block_qkv,
        block_proj,
        hidden_gain,
        hidden_shift,
        padded,
        patches,
    )
    core = (lax.axis_index("rows") % 2).astype(jnp.int32)[None]
    chip = lax.axis_index("rows") // 2
    (
        result,
        grad_middle,
        grad_low,
        down_kept,
        down_sent,
        up_kept,
        up_sent,
        hidden_gain_part,
        hidden_shift_part,
    ) = mlp_call(core, normed_mid, middle, cot, hidden_gain, block_up, block_down)
    layer_output = result.reshape(local_images, padded, width)[:, :patches].reshape(-1, width)
    down_met, up_met = swap_core(down_sent), swap_core(up_sent)
    grad_projected = attend_back_call(grad_low, projected, probs, block_proj, padded, 0, 1)
    grad_projected, down_met, up_met = together(grad_projected, down_met, up_met)
    def by_bit(bit, below=1):
        return lambda array: split_band(array, bit, below)

    def by_chip(array):
        return split(by_band(array), 2, chip)

    down_kept, down_sent = split_sum(
        lambda array: split_band(by_band(array.reshape(1, -1, width // 2)), 0), down_kept, down_met
    )
    up_kept, up_sent = split_sum(by_chip, up_kept, up_met)
    grad_projected, down_kept, down_sent, up_kept, up_sent = together(
        grad_projected, down_kept, down_sent, up_kept, up_sent
    )
    down_met, up_met = swap_band(down_sent, 0), swap_chip(up_sent)
    grad_projected = attend_back_call(
        grad_low, projected, probs, block_proj, padded, 1, local_images - 1, grad_projected
    )
    grad_x, bias_part, attention_gain_part, attention_shift_part = first_norm_back_call(
        grad_projected, grad_middle, x, attention_gain, block_qkv
    )
    grad_x, grad_projected, down_met, up_met = together(grad_x, grad_projected, down_met, up_met)
    own = grad_x.reshape(local_images, padded, width)
    near, across = swap_core(own), swap_chip(own)
    near, grad_low = together(near, grad_low)
    down_kept, down_sent = split_sum(by_bit(1), down_kept, down_met)
    up_kept, up_sent = split_sum(by_bit(0), up_kept, up_met)
    down_met, up_met = swap_band(down_sent, 1), swap_band(up_sent, 0)
    attend_kept, attend_sent = attend_weights_call(core, normed, mixed, grad_projected, grad_low)
    across, attend_kept, attend_sent, down_met, up_met = together(
        across, attend_kept, attend_sent, down_met, up_met
    )
    far, attend_met = swap_core(across), swap_core(attend_sent)
    down_kept, down_sent = split_sum(by_bit(2), down_kept, down_met)
    up_kept, up_sent = split_sum(by_bit(1), up_kept, up_met)
    far, attend_met, down_kept, down_sent, up_kept, up_sent = together(
        far, attend_met, down_kept, down_sent, up_kept, up_sent
    )
    attend_kept, attend_sent = split_sum(by_chip, attend_kept, attend_met)
    attend_kept, attend_sent, near = together(attend_kept, attend_sent, near)
    attend_met = swap_chip(attend_sent)
    down_met, up_met = swap_band(down_sent, 2), swap_band(up_sent, 1)
    gathered = own, near, across, far
    odd = (lax.axis_index("band") % 2).astype(jnp.int32)[None]
    vectors = jnp.concatenate(
        [
            bias_part,
            attention_gain_part,
            attention_shift_part,
            hidden_gain_part,
            hidden_shift_part,
        ]
    ).reshape(-1, kernel_weight.shape[1])
    if fits:
        kernel_kept, kernel_sent, big_slope, slope, summed = embed_back_call(
            place[None],
            odd,
            counts,
            slot_waves,
            gathered,
            (kept_big, kept_small, kept_rows, kept_table),
            kernel_weight,
            vectors,
        )
        kernel_kept, kernel_sent = kernel_kept[None], kernel_sent[None]
    else:
        stacked = jnp.stack(gathered)
        ordered = jnp.concatenate(
            [lax.dynamic_index_in_dim(stacked, place ^ k, 0, False) for k in range(4)]
        )
        pixel_grad, kernel_grad = embed_back_plain(
            counts, slot_waves, ordered, kernel_table, pixels
        )
        in_part = jnp.einsum(
            "qwc,qkc->wk", kernel_grad, kernel_weight, preferred_element_type=jnp.float32
        )
        summed = jnp.concatenate([in_part, vectors])
        kernel_kept, kernel_sent = split_band(kernel_grad.reshape(1, bands, -1, waves, width), 0)
        big_slope = slope = summed
    kernel_kept, kernel_sent, big_slope, summed, down_met, up_met, attend_met = together(
        kernel_kept, kernel_sent, big_slope, summed, down_met, up_met, attend_met
    )
    bits = band_bits()
    kernel_met = swap_band(kernel_sent, 0)
    summed = summed + swap_core(summed)
    summed, big_slope, down_met, up_met, attend_met = together(
        summed, big_slope, down_met, up_met, attend_met
    )
    attend_kept, attend_sent = split_sum(by_bit(0), attend_kept, attend_met)
    down_all = band_rest(add(down_kept, down_met), 3)[:, 0]
    block_down_grad = weight_gather(down_all, False)[0]
    up_all = band_rest(add(up_kept, up_met), 2)[:, 0]
    if fits:
        pixel_grad = pixel_back_call(counts, slot_waves, big_slope, slope, patches)
        pixel_grad = pixel_grad.transpose(2, 1, 0)
    summed = sum_steps(summed, bits[1:])
    kernel_met, pixel_grad, summed, up_all, attend_kept, attend_sent, block_down_grad = together(
        kernel_met, pixel_grad, summed, up_all, attend_kept, attend_sent, block_down_grad
    )
    kernel_kept, kernel_sent = split_sum(by_bit(1), kernel_kept, kernel_met)
    kernel_kept, kernel_sent, attend_kept, attend_sent = together(
        kernel_kept, kernel_sent, attend_kept, attend_sent
    )
    kernel_met = swap_band(kernel_sent, 1)
    attend_met = swap_band(attend_sent, 0)
    kernel_met, attend_met, up_all, summed = together(kernel_met, attend_met, up_all, summed)
    owned = add(kernel_kept, kernel_met)
    for bit in bits[2:-1]:
        owned = band_step(owned, bit)
    attend_kept, attend_sent = split_sum(by_bit(1), attend_kept, attend_met)
    owned, summed, attend_kept, attend_sent, up_all = together(
        owned, summed, attend_kept, attend_sent, up_all
    )
    owned_met = swap_band(owned, bits[-1])
    attend_met = swap_band(attend_sent, 1)
    block_up_grad = side_by_side(weight_gather(up_all, True))
    summed = summed + swap_chip(summed)
    summed = sum_steps(summed, bits[:1])
    owned, owned_met, summed, attend_kept, attend_met, block_up_grad = together(
        owned, owned_met, summed, attend_kept, attend_met, block_up_grad
    )
    owned = add(owned, owned_met)[0]
    attend_all = band_rest(add(attend_kept, attend_met), 2)[:, 0]
    attend_grads = weight_gather(attend_all, True)
    block_qkv_grad, block_proj_grad = side_by_side(attend_grads[:3]), attend_grads[3]
    half_bands = bands // 2
    upper = lax.axis_index("band") // half_bands
    owned_weight = jnp.einsum(
        "wk,qwc->qkc",
        lax.dynamic_slice_in_dim(kernel_low, upper * (depth // 2), depth // 2, 1),
        owned.reshape(-1, waves, width),
        preferred_element_type=jnp.float32,
    ).astype(jnp.bfloat16)
    owned_weight, summed = together(owned_weight, summed)
    grad_kernel_in = summed[:waves]
    bias_grad, attention_gain_grad, attention_shift_grad, hidden_gain_grad, hidden_shift_grad = (
        summed[waves:].reshape(5, width)
    )
    groups = [list(range(half_bands)), list(range(half_bands, bands))]
    kernel_weight_grad = lax.all_to_all(
        owned_weight, "band", split_axis=1, concat_axis=0, tiled=True, axis_index_groups=groups
    )
    kernel_weight_grad = (
        kernel_weight_grad.reshape(half_bands, 2, positions // bands, depth // bands, width)
        .transpose(1, 0, 2, 3, 4)
        .reshape(positions, depth // bands, width)
        .astype(jnp.float32)
    )
    token_grad, *hyper_grads = hyper_back_call(
        sequence, grad_kernel_in, bias_grad[None], hyper_params, bias_head
    )
    return (
        layer_output,
        pixel_grad,
        kernel_weight_grad,
        token_grad[0],
        hyper_grads[0],
        hyper_grads[1],
        hyper_grads[2][0],
        hyper_grads[3][0],
        hyper_grads[4],
        hyper_grads[5],
        hyper_grads[6][0],
        hyper_grads[7][0],
        hyper_grads[8],
        attention_gain_grad,
        attention_shift_grad,
        block_qkv_grad,
        block_proj_grad,
        hidden_gain_grad,
        hidden_shift_grad,
        block_up_grad,
        block_down_grad,
    )


def solution(mesh):
    in_specs = (
        P("band", "rows", None),
        P("band", None),
        P("band", None),
        P(),
        P(),
        P(),
        P(),
        P(),
        P(),
        P(),
        P(),
        P(),
        P(),
        P(),
        P("rows", None, None),
        P(),
        P(),
        P(),
        P(),
        P(),
        P(),
        P(),
        P(),
        P(("band", "rows"), None),
    )
    out_specs = (
        P(("band", "rows"), None),
        P("band", "rows", None),
        P("rows", "band", None),
        P(),
        P(),
        P(),
        P(),
        P(),
        P(),
        P(),
        P(),
        P(),
        P(),
        P(),
        P(),
        P("band", None),
        P("band", None),
        P(),
        P(),
        P("band", None),
        P("band", None),
    )
    return jax.shard_map(body, mesh=mesh, in_specs=in_specs, out_specs=out_specs, check_vma=False)
```

```python
import functools
import math

import jax
import jax.numpy as jnp
from jax import lax
from jax.experimental import pallas as pl
from jax.experimental.pallas import tpu as pltpu
from jax.sharding import PartitionSpec as P

VMEM_LIMIT = 60 * 1024 * 1024
STEPS = 4
QUAD = 4
GROUP = 8
SMALL = 64
LANES = 128
EPSILON = 1e-06
ROW_STEP = 48


def pad_rows(rows):
    return (rows + 15) // 16 * 16


over_last = (((1,), (1,)), ((), ()))
over_first = (((0,), (0,)), ((), ()))


def times(left, right):
    return jnp.dot(left, right, preferred_element_type=jnp.float32)


def times_turned(left, right):
    return lax.dot_general(left, right, over_last, preferred_element_type=jnp.float32)


def turned_times(left, right):
    return lax.dot_general(left, right, over_first, preferred_element_type=jnp.float32)


def norm_parts(values):
    centered = values - jnp.mean(values, axis=-1, keepdims=True)
    variance = jnp.mean(centered * centered, axis=-1, keepdims=True)
    scale = lax.rsqrt(variance + EPSILON)
    return centered * scale, scale


def norm_backward(values, slope, gain):
    unit, scale = norm_parts(values)
    inner = slope * gain
    mean = jnp.mean(inner, axis=-1, keepdims=True)
    along = jnp.mean(inner * unit, axis=-1, keepdims=True)
    return scale * (inner - mean - unit * along), slope * unit


def by_rows(total, fn):
    step = ROW_STEP if total % ROW_STEP == 0 else 2 * 8
    for row in range(0, total, step):
        fn(slice(row, row + step))


def attend_kernel(
    own_ref, core_ref, chip_ref, bias_ref, gain_ref, shift_ref, qkv_ref, proj_ref, mid_gain_ref, mid_shift_ref,
    x_ref, normed_ref, projected_ref, probs_ref, mixed_ref, middle_ref, normed_mid_ref,
    *, patches,
):
    padded, width = x_ref.shape
    head = width // HEADS

    def first(r):
        x = sum(ref[r, :].astype(jnp.float32) for ref in (own_ref, core_ref, chip_ref))
        x = x + bias_ref[...]
        x_ref[r, :] = x
        normed_ref[r, :] = (norm_parts(x)[0] * gain_ref[...] + shift_ref[...]).astype(jnp.bfloat16)

    by_rows(padded, first)
    for part in range(3):
        columns = slice(part * width, (part + 1) * width)
        projected_ref[:, columns] = times(normed_ref[...], qkv_ref[:, columns]).astype(jnp.bfloat16)
    lane = lax.broadcasted_iota(jnp.int32, (padded, LANES), 1)
    key = lax.broadcasted_iota(jnp.int32, (padded, padded), 1)
    factor = jnp.bfloat16(1.0 / math.sqrt(head))

    def pair_of(pair):
        def columns(part):
            return slice(part * width + pair * LANES, part * width + (pair + 1) * LANES)

        queries, keys, values = (projected_ref[:, columns(part)] for part in range(3))
        found = []
        for h in range(2):
            mine = (lane // head) == h
            scores = times_turned(jnp.where(mine, queries * factor, jnp.zeros_like(queries)), keys)
            scores = jnp.where(key < patches, scores, -1e30)
            raised = jnp.exp(scores - jnp.max(scores, axis=-1, keepdims=True))
            probs = raised * (1.0 / jnp.sum(raised, axis=-1, keepdims=True))
            low = probs.astype(jnp.bfloat16)
            probs_ref[pair * 2 + h] = low
            found.append(times(low, values))
        mixed_ref[:, columns(0)] = jnp.where(lane < head, found[0], found[1]).astype(jnp.bfloat16)

    for pair in range(HEADS // 2):
        pair_of(pair)
    middle_ref[...] = times(mixed_ref[...], proj_ref[...])

    def last(r):
        middle = middle_ref[r, :] + x_ref[r, :]
        middle_ref[r, :] = middle
        normed_mid_ref[r, :] = (
            norm_parts(middle)[0] * mid_gain_ref[...] + mid_shift_ref[...]
        ).astype(jnp.bfloat16)

    by_rows(padded, last)


def cost(flops, moved):
    return pl.CostEstimate(flops=flops, bytes_accessed=moved, transcendentals=0)


def whole(*shape):
    return pl.BlockSpec(shape, lambda *index: (0,) * len(shape))


def attend_call(terms, bias, gain, shift, qkv, proj, mid_gain, mid_shift, padded, patches):
    rows, width = terms[0].shape
    images = rows // padded
    row = lambda v: v.reshape(1, width)
    shapes = [
        ((rows, width), jnp.float32),
        ((rows, width), jnp.bfloat16),
        ((rows, 3 * width), jnp.bfloat16),
        ((images * HEADS, padded, padded), jnp.bfloat16),
        ((rows, width), jnp.bfloat16),
        ((rows, width), jnp.float32),
        ((rows, width), jnp.bfloat16),
    ]
    blocks = [
        pl.BlockSpec((HEADS, padded, padded), lambda i: (i, 0, 0))
        if len(shape) == 3
        else pl.BlockSpec((padded, shape[1]), lambda i: (i, 0))
        for shape, _ in shapes
    ]
    return pl.pallas_call(
        functools.partial(attend_kernel, patches=patches),
        grid=(images,),
        in_specs=[
            *[pl.BlockSpec((padded, width), lambda i: (i, 0))] * 3,
            *[whole(1, width)] * 3,
            whole(width, 3 * width),
            whole(width, width),
            *[whole(1, width)] * 2,
        ],
        out_specs=blocks,
        out_shape=[jax.ShapeDtypeStruct(*s) for s in shapes],
        compiler_params=pltpu.CompilerParams(vmem_limit_bytes=VMEM_LIMIT),
        cost_estimate=cost(20 << 30, 25 << 20),
        name="attend",
    )(*terms, row(bias), row(gain), row(shift), qkv, proj, row(mid_gain), row(mid_shift))


def store_halves(core_ref, product, kept_ref, sent_ref):
    half = product.shape[1] // 2
    left, right = product[:, :half].astype(jnp.bfloat16), product[:, half:].astype(jnp.bfloat16)
    first = core_ref[0] == 0
    kept_ref[0] = jnp.where(first, left, right)
    sent_ref[0] = jnp.where(first, right, left)


def mlp_kernel(
    core_ref, normed_ref, middle_ref, cot_ref, gain_ref, up_ref, down_ref,
    out_ref, grad_ref, low_ref, down_kept_ref, down_sent_ref, up_kept_ref, up_sent_ref,
    gain_grad_ref, shift_grad_ref,
    result_ref, slope_ref, wide_ref, back_ref, active_ref, grad_up_ref,
):
    step = pl.program_id(0)
    rows = normed_ref.shape[0]
    wide_ref[...] = times(normed_ref[...], up_ref[...])
    back_ref[...] = times_turned(cot_ref[...], down_ref[...])

    def middle_part(r):
        x = wide_ref[r, :]
        below = 0.5 * (1.0 + lax.erf(x * math.sqrt(0.5)))
        density = jnp.exp(-0.5 * x * x) * (1.0 / math.sqrt(2.0 * math.pi))
        active_ref[r, :] = (x * below).astype(jnp.bfloat16)
        grad_up_ref[r, :] = (back_ref[r, :] * (below + x * density)).astype(jnp.bfloat16)

    by_rows(rows, middle_part)
    product = turned_times(active_ref[...], cot_ref[...])
    store_halves(core_ref, product, down_kept_ref, down_sent_ref)
    product = turned_times(normed_ref[...], grad_up_ref[...])
    store_halves(core_ref, product, up_kept_ref, up_sent_ref)

    @pl.when(step == 0)
    def _():
        result_ref[...] = times(active_ref[...], down_ref[...])
        slope_ref[...] = times_turned(grad_up_ref[...], up_ref[...])

    @pl.when(step > 0)
    def _():
        result_ref[...] += times(active_ref[...], down_ref[...])
        slope_ref[...] += times_turned(grad_up_ref[...], up_ref[...])

    @pl.when(step == pl.num_programs(0) - 1)
    def _():
        gain_grad_ref[...] = jnp.zeros_like(gain_grad_ref)
        shift_grad_ref[...] = jnp.zeros_like(shift_grad_ref)

        def last(r):
            middle, slope = middle_ref[r, :], slope_ref[r, :]
            out_ref[r, :] = (middle + result_ref[r, :]).astype(jnp.bfloat16)
            back, terms = norm_backward(middle, slope, gain_ref[...])
            grad = cot_ref[r, :].astype(jnp.float32) + back
            grad_ref[r, :] = grad
            low_ref[r, :] = grad.astype(jnp.bfloat16)
            gain_grad_ref[...] += jnp.sum(terms, axis=0, keepdims=True)
            shift_grad_ref[...] += jnp.sum(slope, axis=0, keepdims=True)

        by_rows(rows, last)


def mlp_call(core, normed, middle, cot, gain, up, down):
    rows, width = middle.shape
    hidden = up.shape[1]
    steps = hidden // width
    f32, bf16 = jnp.float32, jnp.bfloat16
    half = (1, width, width // 2)
    return pl.pallas_call(
        mlp_kernel,
        grid=(steps,),
        in_specs=[
            pl.BlockSpec(memory_space=pltpu.SMEM),
            whole(rows, width),
            whole(rows, width),
            whole(rows, width),
            whole(1, width),
            pl.BlockSpec((width, width), lambda j: (0, j)),
            pl.BlockSpec((width, width), lambda j: (j, 0)),
        ],
        out_specs=[
            whole(rows, width),
            whole(rows, width),
            whole(rows, width),
            *[pl.BlockSpec(half, lambda j: (j, 0, 0))] * 4,
            whole(1, width),
            whole(1, width),
        ],
        out_shape=[
            jax.ShapeDtypeStruct((rows, width), bf16),
            jax.ShapeDtypeStruct((rows, width), f32),
            jax.ShapeDtypeStruct((rows, width), bf16),
            *[jax.ShapeDtypeStruct((steps, width, width // 2), bf16)] * 4,
            jax.ShapeDtypeStruct((1, width), f32),
            jax.ShapeDtypeStruct((1, width), f32),
        ],
        scratch_shapes=[pltpu.VMEM((rows, width), t) for t in (f32, f32, f32, f32, bf16, bf16)],
        compiler_params=pltpu.CompilerParams(vmem_limit_bytes=VMEM_LIMIT),
        cost_estimate=cost(12 * rows * width * hidden, 30 << 20),
        name="mlp",
    )(core, normed, middle, cot, gain.reshape(1, width), up, down)


def attend_back_kernel(low_ref, projected_ref, probs_ref, proj_ref, *refs):
    grad_projected_ref, mixed_grad_ref = refs[-2:]
    padded, width = low_ref.shape
    head = width // HEADS
    mixed_grad_ref[...] = times_turned(low_ref[...], proj_ref[...]).astype(jnp.bfloat16)
    lane = lax.broadcasted_iota(jnp.int32, (padded, LANES), 1)
    factor = jnp.bfloat16(1.0 / math.sqrt(head))

    def pair_of(pair):
        def columns(part):
            return slice(part * width + pair * LANES, part * width + (pair + 1) * LANES)

        queries, keys, values = (projected_ref[:, columns(part)] for part in range(3))
        queries, keys = queries * factor, keys * factor
        grads = mixed_grad_ref[:, columns(0)]
        found = [], [], []
        for h in range(2):
            mine = (lane // head) == h
            low = probs_ref[pair * 2 + h]
            probs = low.astype(jnp.float32)
            grad_probs = times_turned(jnp.where(mine, grads, jnp.zeros_like(grads)), values)
            scaled = grad_probs * probs
            total = jnp.sum(scaled, axis=-1, keepdims=True)
            grad_scores = (scaled - probs * total).astype(jnp.bfloat16)
            found[0].append(times(grad_scores, keys))
            found[1].append(turned_times(grad_scores, queries))
            found[2].append(turned_times(low, grads))
        for part in range(3):
            grad_projected_ref[:, columns(part)] = jnp.where(
                lane < head, found[part][0], found[part][1]
            ).astype(jnp.bfloat16)

    for pair in range(HEADS // 2):
        pair_of(pair)


def attend_back_call(low, projected, probs, proj, padded, first, count, begun=None):
    rows, width = low.shape
    return pl.pallas_call(
        attend_back_kernel,
        grid=(count,),
        in_specs=[
            pl.BlockSpec((padded, width), lambda i: (i + first, 0)),
            pl.BlockSpec((padded, 3 * width), lambda i: (i + first, 0)),
            pl.BlockSpec((HEADS, padded, padded), lambda i: (i + first, 0, 0)),
            whole(width, width),
            *([] if begun is None else [pl.BlockSpec(memory_space=pl.ANY)]),
        ],
        out_specs=pl.BlockSpec((padded, 3 * width), lambda i: (i + first, 0)),
        out_shape=jax.ShapeDtypeStruct((rows, 3 * width), jnp.bfloat16),
        scratch_shapes=[pltpu.VMEM((padded, width), jnp.bfloat16)],
        input_output_aliases={} if begun is None else {4: 0},
        compiler_params=pltpu.CompilerParams(vmem_limit_bytes=VMEM_LIMIT),
        cost_estimate=cost(count * (6 << 30), count * (5 << 20)),
        name="attend_back",
    )(low, projected, probs, proj, *([] if begun is None else [begun]))


def first_norm_back_kernel(
    grad_projected_ref, grad_ref, x_ref, gain_ref, qkv_ref,
    grad_x_ref, bias_grad_ref, gain_grad_ref, shift_grad_ref, slope_ref,
):
    rows, width = x_ref.shape
    slope_ref[...] = times_turned(grad_projected_ref[:, :width], qkv_ref[:, :width])
    for part in range(1, 3):
        columns = slice(part * width, (part + 1) * width)
        slope_ref[...] += times_turned(grad_projected_ref[:, columns], qkv_ref[:, columns])
    for ref in (bias_grad_ref, gain_grad_ref, shift_grad_ref):
        ref[...] = jnp.zeros_like(ref)

    def last(r):
        slope = slope_ref[r, :]
        back, terms = norm_backward(x_ref[r, :], slope, gain_ref[...])
        grad = grad_ref[r, :] + back
        grad_x_ref[r, :] = grad.astype(jnp.bfloat16)
        bias_grad_ref[...] += jnp.sum(grad, axis=0, keepdims=True)
        gain_grad_ref[...] += jnp.sum(terms, axis=0, keepdims=True)
        shift_grad_ref[...] += jnp.sum(slope, axis=0, keepdims=True)

    by_rows(rows, last)


def first_norm_back_call(grad_projected, grad, x, gain, qkv):
    rows, width = x.shape
    row = jax.ShapeDtypeStruct((1, width), jnp.float32)
    return pl.pallas_call(
        first_norm_back_kernel,
        out_shape=[jax.ShapeDtypeStruct((rows, width), jnp.bfloat16), row, row, row],
        scratch_shapes=[pltpu.VMEM((rows, width), jnp.float32)],
        compiler_params=pltpu.CompilerParams(vmem_limit_bytes=VMEM_LIMIT),
        cost_estimate=cost(1 << 30, 1 << 20),
        name="first_norm_back",
    )(grad_projected, grad, x, gain.reshape(1, width), qkv)


def attend_weights_kernel(
    core_ref, normed_ref, mixed_ref, grad_projected_ref, low_ref, kept_ref, sent_ref
):
    step = pl.program_id(0)

    @pl.when(step < 3)
    def _():
        product = turned_times(normed_ref[...], grad_projected_ref[...])
        store_halves(core_ref, product, kept_ref, sent_ref)

    @pl.when(step == 3)
    def _():
        product = turned_times(mixed_ref[...], low_ref[...])
        store_halves(core_ref, product, kept_ref, sent_ref)


def attend_weights_call(core, normed, mixed, grad_projected, low):
    rows, width = normed.shape
    half = (width, width // 2)
    return pl.pallas_call(
        attend_weights_kernel,
        grid=(4,),
        in_specs=[
            pl.BlockSpec(memory_space=pltpu.SMEM),
            whole(rows, width),
            whole(rows, width),
            pl.BlockSpec((rows, width), lambda j: (0, jnp.minimum(j, 2))),
            whole(rows, width),
        ],
        out_specs=[pl.BlockSpec((1, *half), lambda j: (j, 0, 0))] * 2,
        out_shape=[jax.ShapeDtypeStruct((4, *half), jnp.bfloat16)] * 2,
        compiler_params=pltpu.CompilerParams(vmem_limit_bytes=VMEM_LIMIT),
        cost_estimate=cost(8 * rows * width * width, 30 << 20),
        name="attend_weights",
    )(core, normed, mixed, grad_projected, low)


def fill_starts(counts_ref, starts_ref):
    images = counts_ref.shape[0]
    total, big, most, first = 0, 0, counts_ref[0], 0
    for m in range(images):
        starts_ref[m] = jnp.int32(total)
        if m:
            better = counts_ref[m] > most
            big = jnp.where(better, m, big)
            first = jnp.where(better, total, first)
            most = jnp.where(better, counts_ref[m], most)
        total = total + counts_ref[m]
    starts_ref[images] = jnp.int32(total)
    return big, first, first + most


def strided(ref, first, count, stride):
    parts = [ref[c, pl.ds(first, count, stride=stride), :] for c in range(ref.shape[0])]
    return jnp.concatenate(parts, axis=1)


def fill_choice(wave_row_ref, choice_ref, waves, big_lo, big_hi):
    slots = wave_row_ref.shape[1]
    slot = lax.broadcasted_iota(jnp.int32, (1, slots), 1)
    alone = waves + slot - jnp.where(slot >= big_hi, big_hi - big_lo, 0)
    column = jnp.where((slot >= big_lo) & (slot < big_hi), wave_row_ref[...], alone)
    index = lax.broadcasted_iota(jnp.int32, choice_ref.shape, 0)
    choice_ref[...] = jnp.where(index == column, 1.0, 0.0).astype(jnp.bfloat16)


def fill_spread(kin_ref, spread_ref):
    waves, depth = kin_ref.shape
    rows = waves * GROUP
    of_wave = lax.broadcasted_iota(jnp.int32, (rows, waves), 0) // GROUP
    pick = of_wave == lax.broadcasted_iota(jnp.int32, (rows, waves), 1)
    repeated = times(jnp.where(pick, 1.0, 0.0).astype(jnp.bfloat16), kin_ref[...])
    place = lax.broadcasted_iota(jnp.int32, (rows, depth), 0) % GROUP
    for q in range(GROUP):
        spread_ref[:, q * depth : (q + 1) * depth] = jnp.where(place == q, repeated, 0.0).astype(
            jnp.bfloat16
        )


def embed_kernel(
    place_ref, counts_ref, waves_ref, wave_row_ref, kin_ref, weight_ref, pix_ref,
    own_ref, core_ref, chip_ref, far_ref, big_out, small_out, rows_out, table_out,
    starts_ref, choice_ref, spread_ref, big_ref, small_ref, rows_ref, table_ref,
    turn_ref, wide_ref, acc_ref, semaphores,
):
    step = pl.program_id(0)
    waves, positions, width = table_ref.shape
    depth = kin_ref.shape[1]
    images = counts_ref.shape[0]
    patches, per_step, slots = pix_ref.shape
    padded = acc_ref.shape[0]
    held = own_ref.shape[0]
    big, big_lo, big_hi = fill_starts(counts_ref, starts_ref)

    @pl.when(step == 0)
    def _():
        fill_choice(wave_row_ref, choice_ref, waves, big_lo, big_hi)
        fill_spread(kin_ref, spread_ref)
        turn_ref[...] = jnp.zeros_like(turn_ref)

    first_q = pl.multiple_of(step * per_step, per_step)
    for q in range(per_step):
        rows_ref[first_q + q] = times(kin_ref[...], weight_ref[q]).astype(jnp.bfloat16)
    parts = []
    for q in range(0, per_step, GROUP):
        made = times(spread_ref[...], weight_ref[q : q + GROUP].reshape(GROUP * depth, width))
        parts.append(made.reshape(waves, GROUP, width))
    table_ref[:, pl.ds(first_q, per_step), :] = jnp.concatenate(parts, axis=1).astype(jnp.bfloat16)
    turn_ref[: patches * per_step] = times_turned(
        pix_ref[...].reshape(patches * per_step, slots), choice_ref[...]
    )
    for q in range(per_step):
        turned = turn_ref[pl.ds(q, 2 * LANES, stride=per_step), :].T
        big_ref[first_q + q] = turned[:waves, :padded].astype(jnp.bfloat16)
        for c in range(2):
            wide_ref[c, pl.ds(first_q + q, SMALL, stride=positions), :] = turned[
                waves : waves + SMALL, c * LANES : (c + 1) * LANES
            ]

    @pl.when(step == pl.num_programs(0) - 1)
    def _():
        def narrow(j, carry):
            rows = pl.ds(pl.multiple_of(j * positions, positions), positions)
            both = jnp.concatenate([wide_ref[0, rows, :], wide_ref[1, rows, :]], axis=1)
            small_ref[j] = both[:, :padded].astype(jnp.bfloat16)
            return carry

        lax.fori_loop(0, SMALL, narrow, 0, unroll=8)
        pairs = ((big_ref, big_out), (small_ref, small_out), (rows_ref, rows_out), (table_ref, table_out))
        copies = [
            pltpu.make_async_copy(source, target, semaphores.at[k])
            for k, (source, target) in enumerate(pairs)
        ]
        for copy in copies:
            copy.start()

        def store(m):
            block = (m // held) ^ place_ref[0]
            low = acc_ref[...].astype(jnp.bfloat16)
            for index, ref in enumerate((own_ref, core_ref, chip_ref, far_ref)):

                @pl.when(block == index)
                def _(ref=ref):
                    ref[m % held] = low

        acc_ref[...] = jnp.zeros_like(acc_ref)

        def big_part(j, carry):
            first = pl.ds(pl.multiple_of(j * GROUP, GROUP), GROUP)
            left = big_ref[first].reshape(GROUP * waves, padded)
            acc_ref[...] += turned_times(left, rows_ref[first].reshape(GROUP * waves, width))
            return carry

        lax.fori_loop(0, positions // GROUP, big_part, 0, unroll=True)
        store(big)

        def image(m, carry):
            first, last = starts_ref[m], starts_ref[m + 1]
            shift = jnp.where(first >= big_hi, big_lo - big_hi, 0)

            @pl.when(m != big)
            def _():
                acc_ref[...] = jnp.zeros_like(acc_ref)

                def part(j, carry):
                    lefts, rights = [], []
                    for k in range(QUAD):
                        s = first + j * QUAD + k
                        here = jnp.minimum(s, last - 1)
                        factor = jnp.where(s < last, 1.0, 0.0).astype(jnp.bfloat16)
                        lefts.append(small_ref[here + shift] * factor)
                        rights.append(table_ref[waves_ref[here]])
                    acc_ref[...] += turned_times(
                        jnp.concatenate(lefts, axis=0), jnp.concatenate(rights, axis=0)
                    )
                    return carry

                lax.fori_loop(0, (last - first + QUAD - 1) // QUAD, part, 0)
                store(m)

            return carry

        lax.fori_loop(0, images, image, 0)
        for copy in copies:
            copy.wait()


def embed_call(place, counts, band_waves, kernel_low, kernel_weight, pixels):
    patches, positions, slots = pixels.shape
    waves = kernel_low.shape[0]
    depth, width = kernel_weight.shape[1:]
    images = counts.shape[0]
    padded = pad_rows(patches)
    per_step = positions // STEPS
    smem = pl.BlockSpec(memory_space=pltpu.SMEM)
    block = (images // 4, padded, width)
    kept = [
        (positions, waves, padded),
        (SMALL, positions, padded),
        (positions, waves, width),
        (waves, positions, width),
    ]
    return pl.pallas_call(
        embed_kernel,
        grid=(STEPS,),
        in_specs=[
            smem,
            smem,
            smem,
            whole(1, slots),
            whole(waves, depth),
            pl.BlockSpec((per_step, depth, width), lambda i: (i, 0, 0)),
            pl.BlockSpec((patches, per_step, slots), lambda i: (0, i, 0)),
        ],
        out_specs=[*[whole(*block)] * 4, *[pl.BlockSpec(memory_space=pl.ANY)] * 4],
        out_shape=[
            *[jax.ShapeDtypeStruct(block, jnp.bfloat16)] * 4,
            *[jax.ShapeDtypeStruct(shape, jnp.bfloat16) for shape in kept],
        ],
        scratch_shapes=[
            pltpu.SMEM((images + 1,), jnp.int32),
            pltpu.VMEM((LANES, slots), jnp.bfloat16),
            pltpu.VMEM((waves * GROUP, GROUP * depth), jnp.bfloat16),
            *[pltpu.VMEM(shape, jnp.bfloat16) for shape in kept],
            pltpu.VMEM((2 * LANES * per_step, LANES), jnp.float32),
            pltpu.VMEM((2, SMALL * positions, LANES), jnp.float32),
            pltpu.VMEM((padded, width), jnp.float32),
            pltpu.SemaphoreType.DMA((4,)),
        ],
        compiler_params=pltpu.CompilerParams(vmem_limit_bytes=VMEM_LIMIT),
        name="embed",
    )(place, counts, band_waves, band_waves[None], kernel_low, kernel_weight, pixels)


def embed_back_kernel(
    place_ref, bits_ref, counts_ref, waves_ref, own_ref, core_ref, chip_ref, far_ref,
    big_ref, small_ref, rows_ref, table_ref, weight_ref, vectors_ref,
    kept_ref, sent_ref, second_kept_ref, second_sent_ref, big_slope_ref, slope_ref, in_grad_ref,
    starts_ref, order_ref, grad_ref, sum_ref, wide_ref, semaphores,
):
    step = pl.program_id(0)
    waves, positions, width = table_ref.shape
    padded = big_ref.shape[2]
    images = counts_ref.shape[0]
    held = own_ref.shape[0]
    place = place_ref[0]
    count = GROUP * waves

    def grads_of(m):
        return grad_ref[((m // held) ^ place) * held + m % held]

    @pl.when(step == 0)
    def _():
        copies = [
            pltpu.make_async_copy(ref, grad_ref.at[pl.ds(k * held, held)], semaphores.at[k])
            for k, ref in enumerate((own_ref, core_ref, chip_ref, far_ref))
        ]
        for copy in copies:
            copy.start()
        big, big_lo, big_hi = fill_starts(counts_ref, starts_ref)
        row = lax.broadcasted_iota(jnp.int32, (count, count), 0)
        column = lax.broadcasted_iota(jnp.int32, (count, count), 1)
        same = (row // waves == column % GROUP) & (row % waves == column // GROUP)
        order_ref[...] = jnp.where(same, 1.0, 0.0).astype(jnp.bfloat16)
        in_grad_ref[:waves] = jnp.zeros((waves, in_grad_ref.shape[1]), jnp.float32)
        in_grad_ref[waves:] = vectors_ref[...]
        slope_ref[...] = jnp.zeros_like(slope_ref)
        wide_ref[...] = jnp.zeros_like(wide_ref)
        for copy in copies:
            copy.wait()
        grads = grads_of(big)

        def big_part(j, carry):
            first = pl.ds(pl.multiple_of(j * GROUP, GROUP), GROUP)
            slope = times_turned(rows_ref[first].reshape(count, width), grads)
            big_slope_ref[first, :, :padded] = slope.astype(jnp.bfloat16).reshape(
                GROUP, waves, padded
            )
            sum_ref[pl.ds(pl.multiple_of(j * count, count), count), :] = times(
                big_ref[first].reshape(count, padded), grads
            )
            return carry

        lax.fori_loop(0, positions // GROUP, big_part, 0, unroll=True)

        def image(m, carry):
            first, last = starts_ref[m], starts_ref[m + 1]
            shift = jnp.where(first >= big_hi, big_lo - big_hi, 0)

            @pl.when(m != big)
            def _():
                grads = grads_of(m)

                def part(j, carry):
                    lefts, rights, index = [], [], []
                    for k in range(QUAD):
                        s = first + j * QUAD + k
                        here = jnp.minimum(s, last - 1)
                        factor = jnp.where(s < last, 1.0, 0.0).astype(jnp.bfloat16)
                        index.append(here)
                        lefts.append(table_ref[waves_ref[here]])
                        rights.append(small_ref[here + shift] * factor)
                    own = times_turned(jnp.concatenate(lefts, axis=0), grads)
                    more = times(jnp.concatenate(rights, axis=0), grads)
                    for k in range(QUAD):
                        part_rows = slice(k * positions, (k + 1) * positions)
                        row = pl.multiple_of((index[k] + shift) * positions, positions)
                        slope_ref[0, pl.ds(row, positions), :] = own[part_rows, :LANES]
                        slope_ref[1, pl.ds(row, positions), : padded - LANES] = own[
                            part_rows, LANES:
                        ]
                        wide_ref[waves_ref[index[k]]] += more[part_rows]
                    return carry

                lax.fori_loop(0, (last - first + QUAD - 1) // QUAD, part, 0)

            return carry

        lax.fori_loop(0, images, image, 0)

    odd = bits_ref[0]
    found = jnp.zeros((waves, in_grad_ref.shape[1]), jnp.float32)
    for ref, half in ((kept_ref, odd), (sent_ref, 1 - odd)):
        first_q = pl.multiple_of((2 * step + half) * GROUP, GROUP)
        block = wide_ref[:, pl.ds(first_q, GROUP), :].reshape(count, width).astype(jnp.bfloat16)
        rows = pl.ds(pl.multiple_of(first_q * waves, count), count)
        total = (sum_ref[rows, :] + times(order_ref[...], block)).astype(jnp.bfloat16)
        low = total.reshape(GROUP, waves, width)
        ref[0] = low[:, :, : width // 2]

        @pl.when(step % 2 == bits_ref[1])
        def _(low=low, half=half):
            second_kept_ref[step // 2, half] = low[:, :, width // 2 :]

        @pl.when(step % 2 != bits_ref[1])
        def _(low=low, half=half):
            second_sent_ref[step // 2, half] = low[:, :, width // 2 :]

        for q in range(GROUP):
            part = total[q * waves : (q + 1) * waves]
            found = found + times_turned(part, weight_ref[half * GROUP + q])
    in_grad_ref[:waves] += found


def pixel_back_kernel(
    counts_ref, wave_row_ref, big_slope_ref, slope_ref, pix_grad_ref, starts_ref, choice_ref, turn_ref
):
    step = pl.program_id(0)
    patches, per_step, _ = pix_grad_ref.shape
    positions, waves, _ = big_slope_ref.shape

    @pl.when(step == 0)
    def _():
        _, big_lo, big_hi = fill_starts(counts_ref, starts_ref)
        fill_choice(wave_row_ref, choice_ref, waves, big_lo, big_hi)

    first_q = pl.multiple_of(step * per_step, per_step)
    for q in range(per_step):
        alone = strided(slope_ref, first_q + q, SMALL, positions).astype(jnp.bfloat16)
        chosen = jnp.concatenate([big_slope_ref[first_q + q], alone], axis=0)
        spread = turned_times(chosen, choice_ref[: waves + SMALL])
        for c in range(turn_ref.shape[0]):
            turn_ref[c, pl.ds(q, patches, stride=per_step), :] = spread[
                :patches, c * LANES : (c + 1) * LANES
            ]
    for c in range(turn_ref.shape[0]):
        pix_grad_ref[:, :, c * LANES : (c + 1) * LANES] = (
            turn_ref[c].astype(jnp.bfloat16).reshape(patches, per_step, LANES)
        )


def pixel_back_call(counts, band_waves, big_slope, slope, patches):
    positions = big_slope.shape[0]
    slots = band_waves.shape[0]
    per_step = positions // STEPS
    return pl.pallas_call(
        pixel_back_kernel,
        grid=(STEPS,),
        in_specs=[
            pl.BlockSpec(memory_space=pltpu.SMEM),
            whole(1, slots),
            whole(*big_slope.shape),
            whole(*slope.shape),
        ],
        out_specs=pl.BlockSpec((patches, per_step, slots), lambda i: (0, i, 0)),
        out_shape=jax.ShapeDtypeStruct((patches, positions, slots), jnp.bfloat16),
        scratch_shapes=[
            pltpu.SMEM((counts.shape[0] + 1,), jnp.int32),
            pltpu.VMEM((LANES, slots), jnp.bfloat16),
            pltpu.VMEM((slots // LANES, patches * per_step, LANES), jnp.float32),
        ],
        compiler_params=pltpu.CompilerParams(vmem_limit_bytes=VMEM_LIMIT),
        cost_estimate=cost(1 << 20, 1 << 10),
        name="pixel_back",
    )(counts, band_waves[None], big_slope, slope)


def embed_back_call(place, bits, counts, band_waves, grads, kept, kernel_weight, vectors):
    positions, waves, padded = kept[0].shape
    width = kept[2].shape[2]
    images = counts.shape[0]
    pairs = positions // (2 * GROUP)
    block = (1, GROUP, waves, width // 2)
    second = (pairs // 2, 2, *block[1:])
    depth = kernel_weight.shape[1]
    smem = pl.BlockSpec(memory_space=pltpu.SMEM)
    return pl.pallas_call(
        embed_back_kernel,
        grid=(pairs,),
        in_specs=[
            smem,
            smem,
            smem,
            smem,
            *[pl.BlockSpec(memory_space=pl.ANY)] * 4,
            *[whole(*array.shape) for array in kept],
            pl.BlockSpec((2 * GROUP, depth, width), lambda i: (i, 0, 0)),
            whole(*vectors.shape),
        ],
        out_specs=[
            *[pl.BlockSpec(block, lambda i: (i, 0, 0, 0))] * 2,
            *[whole(*second)] * 2,
            whole(positions, waves, 2 * LANES),
            whole(2, SMALL * positions, LANES),
            whole(waves + vectors.shape[0], depth),
        ],
        out_shape=[
            *[jax.ShapeDtypeStruct((pairs, *block[1:]), jnp.bfloat16)] * 2,
            *[jax.ShapeDtypeStruct(second, jnp.bfloat16)] * 2,
            jax.ShapeDtypeStruct((positions, waves, 2 * LANES), jnp.bfloat16),
            jax.ShapeDtypeStruct((2, SMALL * positions, LANES), jnp.float32),
            jax.ShapeDtypeStruct((waves + vectors.shape[0], depth), jnp.float32),
        ],
        scratch_shapes=[
            pltpu.SMEM((images + 1,), jnp.int32),
            pltpu.VMEM((GROUP * waves, GROUP * waves), jnp.bfloat16),
            pltpu.VMEM((images, padded, width), jnp.bfloat16),
            pltpu.VMEM((positions * waves, width), jnp.float32),
            pltpu.VMEM((waves, positions, width), jnp.float32),
            pltpu.SemaphoreType.DMA((4,)),
        ],
        compiler_params=pltpu.CompilerParams(vmem_limit_bytes=VMEM_LIMIT),
        name="embed_back",
    )(place, bits, counts, band_waves, *grads, *kept, kernel_weight, vectors)


HEADS = 12
WD = 128
WHEADS = 4


highest = lax.Precision.HIGHEST


def layer_norm(values, norm_gain, norm_shift, epsilon):
    centered = values - jnp.mean(values, axis=-1, keepdims=True)
    variance = jnp.mean(centered * centered, axis=-1, keepdims=True)
    return centered * lax.rsqrt(variance + epsilon) * norm_gain + norm_shift


def wave_embed(wavelengths):
    halfwidth = WD // 2
    indices = jnp.arange(halfwidth, dtype=jnp.float32)
    frequency = 1.0 / 10000.0 ** (indices / halfwidth)
    angles = (wavelengths * 1000.0)[:, None] * frequency[None, :]
    return jnp.concatenate([jnp.sin(angles), jnp.cos(angles)], axis=1)


def product(left, right, axes=(1, 0)):
    return lax.dot_general(
        left,
        right,
        (((axes[0],), (axes[1],)), ((), ())),
        precision=highest,
        preferred_element_type=jnp.float32,
    )


@jax.custom_vjp
def dot_rows(left, right):
    return product(left, right)


def dot_rows_forward(left, right):
    return product(left, right), (left, right)


def dot_rows_backward(saved, slope):
    left, right = saved
    return product(slope, right, (1, 1)), product(left, slope, (0, 0))


dot_rows.defvjp(dot_rows_forward, dot_rows_backward)


@jax.custom_vjp
def dot_turned(left, right):
    return product(left, right, (1, 1))


def dot_turned_forward(left, right):
    return product(left, right, (1, 1)), (left, right)


def dot_turned_backward(saved, slope):
    left, right = saved
    return product(slope, right), product(slope, left, (0, 0))


dot_turned.defvjp(dot_turned_forward, dot_turned_backward)


def hypernet(sequence, length, wave_qkv, wave_proj, wave_gain, wave_shift, wave_up, wave_down, kernel_gain, kernel_shift):
    rows, width = sequence.shape
    head_width = width // WHEADS
    projected = dot_rows(sequence, wave_qkv)
    queries, keys, values = (projected[:, i * width : (i + 1) * width] for i in range(3))
    of_head = lax.broadcasted_iota(jnp.int32, (rows, width), 1) // head_width
    real = lax.broadcasted_iota(jnp.int32, (rows, rows), 1) < length
    attended = jnp.zeros((rows, width), jnp.float32)
    for h in range(WHEADS):
        mine = (of_head == h).astype(jnp.float32)
        scores = dot_turned(queries * mine, keys) * (1.0 / math.sqrt(head_width))
        scores = jnp.where(real, scores, -1e30)
        raised = jnp.exp(scores - lax.stop_gradient(jnp.max(scores, axis=-1, keepdims=True)))
        weights = raised / jnp.sum(raised, axis=-1, keepdims=True)
        attended = attended + dot_rows(weights, values * mine)
    normed_first = layer_norm(
        sequence + dot_rows(attended, wave_proj), wave_gain, wave_shift, 1e-05
    )
    upward = dot_rows(normed_first, wave_up)
    widened = 0.5 * upward * (1.0 + lax.erf(upward * math.sqrt(0.5)))
    return layer_norm(
        normed_first + dot_rows(widened, wave_down), kernel_gain, kernel_shift, 1e-05
    )


def hyper_kernel(sequence_ref, *refs):
    params, (head_ref, low_ref, bias_ref) = refs[:8], refs[8:]
    waves = low_ref.shape[0]
    second = hypernet(sequence_ref[...], waves + 1, *(ref[...] for ref in params))
    low_ref[...] = (second[:waves] + sequence_ref[:waves]).astype(jnp.bfloat16)
    bias_ref[...] = product(second[waves : waves + 8], head_ref[...])


def hyper_call(sequence, params, bias_head, waves):
    depth = sequence.shape[1]
    return pl.pallas_call(
        hyper_kernel,
        out_shape=[
            jax.ShapeDtypeStruct((waves, depth), jnp.bfloat16),
            jax.ShapeDtypeStruct((8, bias_head.shape[1]), jnp.float32),
        ],
        compiler_params=pltpu.CompilerParams(vmem_limit_bytes=VMEM_LIMIT),
        cost_estimate=cost(1 << 20, 1 << 10),
        name="hyper",
    )(sequence, *params, bias_head)


def hyper_back_kernel(sequence_ref, in_grad_ref, bias_grad_ref, *refs):
    params, head_ref, outs, head_grad_ref = refs[:8], refs[8], refs[9:18], refs[18]
    rows, depth = sequence_ref.shape
    waves = in_grad_ref.shape[0]

    def apply(sequence, *values):
        return hypernet(sequence, waves + 1, *values)

    second, back = jax.vjp(apply, sequence_ref[...], *(ref[...] for ref in params))
    row = lax.broadcasted_iota(jnp.int32, (8, 1), 0)
    bias_grad = jnp.where(row == 0, bias_grad_ref[...], 0.0)
    last = product(bias_grad, head_ref[...], (1, 1))
    parts = [in_grad_ref[...], last]
    if rows > waves + 8:
        parts.append(jnp.zeros((rows - waves - 8, depth), jnp.float32))
    sequence_grad, *grads = back(jnp.concatenate(parts, axis=0))
    outs[0][...] = sequence_grad[waves : waves + 8]
    for ref, grad in zip(outs[1:], grads, strict=True):
        ref[...] = grad
    head_grad_ref[...] = product(second[waves : waves + 8], bias_grad, (0, 0))


def hyper_back_call(sequence, in_grad, bias_grad, params, bias_head):
    depth = sequence.shape[1]
    shapes = [(8, depth), *[p.shape for p in params], bias_head.shape]
    return pl.pallas_call(
        hyper_back_kernel,
        out_shape=[jax.ShapeDtypeStruct(shape, jnp.float32) for shape in shapes],
        compiler_params=pltpu.CompilerParams(vmem_limit_bytes=VMEM_LIMIT),
        cost_estimate=cost(14 << 30, 16 << 20),
        name="hyper_back",
    )(sequence, in_grad, bias_grad, *params, bias_head)


def swap_core(array):
    return lax.ppermute(array, "rows", [(0, 1), (1, 0), (2, 3), (3, 2)])


def swap_chip(array):
    return lax.ppermute(array, "rows", [(0, 2), (2, 0), (1, 3), (3, 1)])


def add_wide(left, right):
    return left.astype(jnp.float32) + right.astype(jnp.float32)


def rows_reduce(own, core, chip, far):
    passed = add_wide(chip, swap_core(far)).astype(jnp.bfloat16)
    return own, swap_core(core), swap_chip(passed)


def swap_band(array, bit):
    count = lax.axis_size("band")
    return lax.ppermute(array, "band", [(i, i ^ (1 << bit)) for i in range(count)])


def split(array, axis, bit):
    half = array.shape[axis] // 2
    return (
        lax.dynamic_slice_in_dim(array, bit * half, half, axis),
        lax.dynamic_slice_in_dim(array, (1 - bit) * half, half, axis),
    )


def split_band(array, bit, below=1):
    place = lax.axis_index("band")
    parts, bands, *rest = array.shape
    array = array.reshape(parts, bands // (2 * below), 2, below, *rest)
    halves = split(array, 2, (place >> bit) & 1)
    return [half.reshape(parts, bands // 2, *rest) for half in halves]


def add(kept, met):
    return add_wide(kept, met).astype(kept.dtype)


def split_sum(splitter, kept, met):
    return [add(*pair) for pair in zip(splitter(kept), splitter(met))]


def band_step(array, bit, below=1):
    kept, sent = split_band(array, bit, below)
    return add(kept, swap_band(sent, bit))


def band_rest(array, first):
    for bit in range(first, lax.axis_size("band").bit_length() - 1):
        array = band_step(array, bit)
    return array


def join(own, other, bit, axis):
    return jnp.where(
        bit == 0,
        jnp.concatenate([own, other], axis=axis),
        jnp.concatenate([other, own], axis=axis),
    )


def weight_gather(array, chip_first):
    place = lax.axis_index("rows")
    chip, core = place // 2, place % 2
    if chip_first:
        array = join(array, swap_chip(array), chip, 1)
    else:
        array = add_wide(array, swap_chip(array)).astype(array.dtype)
    return join(array, swap_core(array), core, 2).astype(jnp.float32)


def by_band(array):
    parts, rows, width = array.shape
    bands = lax.axis_size("band")
    return array.reshape(parts, bands, rows // bands, width)


def together(*arrays):
    return lax.optimization_barrier(arrays)


def side_by_side(parts):
    return parts.transpose(1, 0, 2).reshape(parts.shape[1], -1)


def band_bits():
    return range(lax.axis_size("band").bit_length() - 1)


def sum_steps(array, bits):
    for bit in bits:
        array = array + swap_band(array, bit)
    return array


def slot_masks(counts, slot_waves, waves):
    index = jnp.arange(counts.shape[0])
    ends = jnp.sum(jnp.where(index[None, :] <= index[:, None], counts[None, :], 0), axis=1)
    slots = jnp.arange(slot_waves.shape[0])
    owners = jnp.sum((ends[None, :] <= slots[:, None]).astype(jnp.int32), axis=1)
    return (
        (owners[:, None] == index[None, :]).astype(jnp.bfloat16),
        (slot_waves[:, None] == jnp.arange(waves)[None, :]).astype(jnp.bfloat16),
    )


def embed_plain(counts, slot_waves, kernel_low, kernel_weight, pixels):
    slots, positions, patches = pixels.shape
    table = jnp.einsum(
        "wk,qkc->wqc", kernel_low, kernel_weight, preferred_element_type=jnp.float32
    ).astype(jnp.bfloat16)
    of_image, of_wave = slot_masks(counts, slot_waves, table.shape[0])
    chunk = min(16, slots)

    def part(running, inputs):
        pixel, image, wave = inputs
        chosen = jnp.einsum("sw,wqc->sqc", wave, table)
        rows = jnp.einsum("sqp,sqc->spc", pixel, chosen, preferred_element_type=jnp.float32)
        image = image.astype(jnp.float32)
        return (running + jnp.einsum("si,spc->ipc", image, rows, precision=highest), None)

    shape = (counts.shape[0], patches, table.shape[2])
    total = lax.scan(
        part,
        jnp.zeros(shape, jnp.float32),
        tuple(a.reshape(-1, chunk, *a.shape[1:]) for a in (pixels, of_image, of_wave)),
    )[0]
    extra = pad_rows(patches) - patches
    return (jnp.pad(total.astype(jnp.bfloat16), ((0, 0), (0, extra), (0, 0))), table)


def embed_back_plain(counts, slot_waves, grads, table, pixels):
    slots, positions, patches = pixels.shape
    waves, _, width = table.shape
    of_image, of_wave = slot_masks(counts, slot_waves, waves)
    grads = grads[:, :patches]
    chunk = min(16, slots)

    def part(running, inputs):
        pixel, image, wave = inputs
        chosen = jnp.einsum("sw,wqc->sqc", wave, table)
        slope = jnp.einsum("si,ipc->spc", image, grads)
        own = jnp.einsum("sqc,spc->sqp", chosen, slope, preferred_element_type=jnp.float32)
        more = jnp.einsum("sqp,spc->sqc", pixel, slope, preferred_element_type=jnp.float32)
        wave = wave.astype(jnp.float32)
        added = jnp.einsum("sw,sqc->qwc", wave, more, precision=highest)
        return (running + added, own.astype(jnp.bfloat16))

    kernel_grad, pixel_grad = lax.scan(
        part,
        jnp.zeros((positions, waves, width), jnp.float32),
        tuple(a.reshape(-1, chunk, *a.shape[1:]) for a in (pixels, of_image, of_wave)),
    )
    return (pixel_grad.reshape(pixels.shape), kernel_grad.astype(jnp.bfloat16))


def body(
    pixels,
    band_counts,
    band_waves,
    wavelengths,
    bias_token,
    wave_qkv,
    wave_proj,
    wave_gain,
    wave_shift,
    wave_up,
    wave_down,
    kernel_gain,
    kernel_shift,
    bias_head,
    kernel_weight,
    attention_gain,
    attention_shift,
    block_qkv,
    block_proj,
    hidden_gain,
    hidden_shift,
    block_up,
    block_down,
    cotangent,
):
    waves, depth = wavelengths.shape[0], bias_token.shape[0]
    sequence = jnp.concatenate(
        [
            wave_embed(wavelengths),
            bias_token[None],
            jnp.zeros((-(waves + 1) % 8, depth), jnp.float32),
        ]
    )
    hyper_params = (
        wave_qkv,
        wave_proj,
        wave_gain[None],
        wave_shift[None],
        wave_up,
        wave_down,
        kernel_gain[None],
        kernel_shift[None],
    )
    kernel_low, conv_bias = hyper_call(sequence, hyper_params, bias_head, waves)
    conv_bias = conv_bias[0]
    counts = band_counts[0]
    slot_waves = band_waves[0]
    slot_total, positions, patches = pixels.shape
    images = counts.shape[0]
    width = kernel_weight.shape[2]
    bands = lax.axis_size("band")
    fits = waves * positions * width <= 1 << 21 and positions == bands * GROUP
    place = lax.axis_index("rows").astype(jnp.int32)
    padded = pad_rows(patches)
    if fits:
        turned_pixels = pixels.transpose(2, 1, 0)
        *blocks, kept_big, kept_small, kept_rows, kept_table = embed_call(
            place[None], counts, slot_waves, kernel_low, kernel_weight, turned_pixels
        )
    else:
        partial_rows, kernel_table = embed_plain(
            counts, slot_waves, kernel_low, kernel_weight, pixels
        )
        partial_rows = partial_rows.reshape(4, -1, padded, width)
        blocks = [lax.dynamic_index_in_dim(partial_rows, place ^ k, 0, False) for k in range(4)]
    terms = [term.reshape(-1, width) for term in rows_reduce(*blocks)]
    local_images = images // 4
    cot = jnp.pad(
        cotangent.reshape(local_images, patches, width), ((0, 0), (0, padded - patches), (0, 0))
    ).reshape(-1, width)
    x, normed, projected, probs, mixed, middle, normed_mid = attend_call(
        terms,
        conv_bias,
        attention_gain,
        attention_shift,
        block_qkv,
        block_proj,
        hidden_gain,
        hidden_shift,
        padded,
        patches,
    )
    core = (lax.axis_index("rows") % 2).astype(jnp.int32)[None]
    chip = lax.axis_index("rows") // 2
    (
        result,
        grad_middle,
        grad_low,
        down_kept,
        down_sent,
        up_kept,
        up_sent,
        hidden_gain_part,
        hidden_shift_part,
    ) = mlp_call(core, normed_mid, middle, cot, hidden_gain, block_up, block_down)
    layer_output = result.reshape(local_images, padded, width)[:, :patches].reshape(-1, width)
    down_met, up_met = swap_core(down_sent), swap_core(up_sent)
    grad_projected = attend_back_call(grad_low, projected, probs, block_proj, padded, 0, 1)
    grad_projected, down_met, up_met = together(grad_projected, down_met, up_met)
    def by_bit(bit, below=1):
        return lambda array: split_band(array, bit, below)

    def by_chip(array):
        return split(by_band(array), 2, chip)

    down_kept, down_sent = split_sum(
        lambda array: split_band(by_band(array.reshape(1, -1, width // 2)), 0), down_kept, down_met
    )
    up_kept, up_sent = split_sum(by_chip, up_kept, up_met)
    grad_projected, down_kept, down_sent, up_kept, up_sent = together(
        grad_projected, down_kept, down_sent, up_kept, up_sent
    )
    down_met, up_met = swap_band(down_sent, 0), swap_chip(up_sent)
    grad_projected = attend_back_call(
        grad_low, projected, probs, block_proj, padded, 1, local_images - 1, grad_projected
    )
    grad_x, bias_part, attention_gain_part, attention_shift_part = first_norm_back_call(
        grad_projected, grad_middle, x, attention_gain, block_qkv
    )
    grad_x, grad_projected, down_met, up_met = together(grad_x, grad_projected, down_met, up_met)
    own = grad_x.reshape(local_images, padded, width)
    near, across = swap_core(own), swap_chip(own)
    near, grad_low = together(near, grad_low)
    down_kept, down_sent = split_sum(by_bit(1), down_kept, down_met)
    up_kept, up_sent = split_sum(by_bit(0), up_kept, up_met)
    down_met, up_met = swap_band(down_sent, 1), swap_band(up_sent, 0)
    attend_kept, attend_sent = attend_weights_call(core, normed, mixed, grad_projected, grad_low)
    across, attend_kept, attend_sent, down_met, up_met = together(
        across, attend_kept, attend_sent, down_met, up_met
    )
    far, attend_met = swap_core(across), swap_core(attend_sent)
    down_kept, down_sent = split_sum(by_bit(2), down_kept, down_met)
    up_kept, up_sent = split_sum(by_bit(1), up_kept, up_met)
    far, attend_met, down_kept, down_sent, up_kept, up_sent = together(
        far, attend_met, down_kept, down_sent, up_kept, up_sent
    )
    attend_kept, attend_sent = split_sum(by_chip, attend_kept, attend_met)
    attend_kept, attend_sent, near = together(attend_kept, attend_sent, near)
    attend_met = swap_chip(attend_sent)
    down_met, up_met = swap_band(down_sent, 2), swap_band(up_sent, 1)
    gathered = own, near, across, far
    band = lax.axis_index("band").astype(jnp.int32)
    vectors = jnp.concatenate(
        [
            bias_part,
            attention_gain_part,
            attention_shift_part,
            hidden_gain_part,
            hidden_shift_part,
        ]
    ).reshape(-1, kernel_weight.shape[1])
    if fits:
        *parts, big_slope, slope, summed = embed_back_call(
            place[None],
            jnp.stack([band % 2, band // 2 % 2]),
            counts,
            slot_waves,
            gathered,
            (kept_big, kept_small, kept_rows, kept_table),
            kernel_weight,
            vectors,
        )
        first_kept, first_sent, second_kept, second_sent = (
            part.reshape(1, bands // 2, -1, waves, width // 2) for part in parts
        )
    else:
        stacked = jnp.stack(gathered)
        ordered = jnp.concatenate(
            [lax.dynamic_index_in_dim(stacked, place ^ k, 0, False) for k in range(4)]
        )
        pixel_grad, kernel_grad = embed_back_plain(
            counts, slot_waves, ordered, kernel_table, pixels
        )
        in_part = jnp.einsum(
            "qwc,qkc->wk", kernel_grad, kernel_weight, preferred_element_type=jnp.float32
        )
        summed = jnp.concatenate([in_part, vectors])
        kernel_grad = kernel_grad.reshape(1, bands, -1, waves, width)
        first_kept, first_sent = split_band(kernel_grad[..., : width // 2], 0)
        second_kept, second_sent = split_band(kernel_grad[..., width // 2 :], 1, 2)
        big_slope = slope = summed
    first_kept, first_sent, second_kept, second_sent = together(
        first_kept, first_sent, second_kept, second_sent
    )
    first_sent, second_sent, summed, down_met, up_met, attend_met = together(
        first_sent, second_sent, summed, down_met, up_met, attend_met
    )
    bits = band_bits()
    first_met, second_met = swap_band(first_sent, 0), swap_band(second_sent, 1)
    summed = summed + swap_core(summed)
    summed, down_met, up_met, attend_met = together(summed, down_met, up_met, attend_met)
    summed = sum_steps(summed + swap_chip(summed), bits[:1])
    attend_kept, attend_sent = split_sum(by_bit(0), attend_kept, attend_met)
    down_all = band_rest(add(down_kept, down_met), 3)[:, 0]
    block_down_grad = weight_gather(down_all, False)[0]
    up_all = band_rest(add(up_kept, up_met), 2)[:, 0]
    first_met, second_met, summed, block_down_grad = together(
        first_met, second_met, summed, block_down_grad
    )
    first_kept, first_sent = split_sum(by_bit(1), first_kept, first_met)
    second_kept, second_sent = split_sum(by_bit(0), second_kept, second_met)
    first_sent, second_sent, summed, attend_sent, up_all = together(
        first_sent, second_sent, summed, attend_sent, up_all
    )
    first_met, second_met = swap_band(first_sent, 1), swap_band(second_sent, 0)
    attend_met = swap_band(attend_sent, 0)
    summed = sum_steps(summed, bits[1:])
    first_met, second_met, summed, attend_met, up_all = together(
        first_met, second_met, summed, attend_met, up_all
    )
    attend_kept, attend_sent = split_sum(by_bit(1), attend_kept, attend_met)
    owned = jnp.concatenate([add(first_kept, first_met), add(second_kept, second_met)], axis=-1)
    for bit in bits[2:-1]:
        owned = band_step(owned, bit)
    owned, summed, attend_sent, up_all, big_slope = together(
        owned, summed, attend_sent, up_all, big_slope
    )
    owned_met = swap_band(owned, bits[-1])
    if fits:
        pixel_grad = pixel_back_call(counts, slot_waves, big_slope, slope, patches)
    attend_met = swap_band(attend_sent, 1)
    block_up_grad = side_by_side(weight_gather(up_all, True))
    owned, owned_met, attend_kept, attend_met, pixel_grad, block_up_grad = together(
        owned, owned_met, attend_kept, attend_met, pixel_grad, block_up_grad
    )
    if fits:
        pixel_grad = pixel_grad.transpose(2, 1, 0)
    owned = add(owned, owned_met)[0]
    attend_all = band_rest(add(attend_kept, attend_met), 2)[:, 0]
    attend_grads = weight_gather(attend_all, True)
    block_qkv_grad, block_proj_grad = side_by_side(attend_grads[:3]), attend_grads[3]
    half_bands = bands // 2
    upper = lax.axis_index("band") // half_bands
    owned_weight = jnp.einsum(
        "wk,qwc->qkc",
        lax.dynamic_slice_in_dim(kernel_low, upper * (depth // 2), depth // 2, 1),
        owned.reshape(-1, waves, width),
        preferred_element_type=jnp.float32,
    ).astype(jnp.bfloat16)
    owned_weight, summed = together(owned_weight, summed)
    grad_kernel_in = summed[:waves]
    bias_grad, attention_gain_grad, attention_shift_grad, hidden_gain_grad, hidden_shift_grad = (
        summed[waves:].reshape(5, width)
    )
    groups = [list(range(half_bands)), list(range(half_bands, bands))]
    kernel_weight_grad = lax.all_to_all(
        owned_weight, "band", split_axis=1, concat_axis=0, tiled=True, axis_index_groups=groups
    )
    kernel_weight_grad = (
        kernel_weight_grad.reshape(half_bands, 2, positions // bands, depth // bands, width)
        .transpose(1, 0, 2, 3, 4)
        .reshape(positions, depth // bands, width)
        .astype(jnp.float32)
    )
    token_grad, *hyper_grads = hyper_back_call(
        sequence, grad_kernel_in, bias_grad[None], hyper_params, bias_head
    )
    return (
        layer_output,
        pixel_grad,
        kernel_weight_grad,
        token_grad[0],
        hyper_grads[0],
        hyper_grads[1],
        hyper_grads[2][0],
        hyper_grads[3][0],
        hyper_grads[4],
        hyper_grads[5],
        hyper_grads[6][0],
        hyper_grads[7][0],
        hyper_grads[8],
        attention_gain_grad,
        attention_shift_grad,
        block_qkv_grad,
        block_proj_grad,
        hidden_gain_grad,
        hidden_shift_grad,
        block_up_grad,
        block_down_grad,
    )


def solution(mesh):
    in_specs = (
        P("band", "rows", None),
        P("band", None),
        P("band", None),
        P(),
        P(),
        P(),
        P(),
        P(),
        P(),
        P(),
        P(),
        P(),
        P(),
        P(),
        P("rows", None, None),
        P(),
        P(),
        P(),
        P(),
        P(),
        P(),
        P(),
        P(),
        P(("band", "rows"), None),
    )
    out_specs = (
        P(("band", "rows"), None),
        P("band", "rows", None),
        P("rows", "band", None),
        P(),
        P(),
        P(),
        P(),
        P(),
        P(),
        P(),
        P(),
        P(),
        P(),
        P(),
        P(),
        P("band", None),
        P("band", None),
        P(),
        P(),
        P("band", None),
        P("band", None),
    )
    return jax.shard_map(body, mesh=mesh, in_specs=in_specs, out_specs=out_specs, check_vma=False)
```

```python
import functools
import math

import jax
import jax.numpy as jnp
from jax import lax
from jax.experimental import pallas as pl
from jax.experimental.pallas import tpu as pltpu
from jax.sharding import PartitionSpec as P

VMEM_LIMIT = 60 * 1024 * 1024
STEPS = 4
QUAD = 4
GROUP = 8
SMALL = 64
LANES = 128
EPSILON = 1e-06
ROW_STEP = 48


def pad_rows(rows):
    return (rows + 15) // 16 * 16


over_last = (((1,), (1,)), ((), ()))
over_first = (((0,), (0,)), ((), ()))


def times(left, right):
    return jnp.dot(left, right, preferred_element_type=jnp.float32)


def times_turned(left, right):
    return lax.dot_general(left, right, over_last, preferred_element_type=jnp.float32)


def turned_times(left, right):
    return lax.dot_general(left, right, over_first, preferred_element_type=jnp.float32)


def norm_parts(values):
    centered = values - jnp.mean(values, axis=-1, keepdims=True)
    variance = jnp.mean(centered * centered, axis=-1, keepdims=True)
    scale = lax.rsqrt(variance + EPSILON)
    return centered * scale, scale


def norm_backward(values, slope, gain):
    unit, scale = norm_parts(values)
    inner = slope * gain
    mean = jnp.mean(inner, axis=-1, keepdims=True)
    along = jnp.mean(inner * unit, axis=-1, keepdims=True)
    return scale * (inner - mean - unit * along), slope * unit


def by_rows(total, fn):
    step = ROW_STEP if total % ROW_STEP == 0 else 2 * 8
    for row in range(0, total, step):
        fn(slice(row, row + step))


def attend_kernel(
    own_ref, core_ref, chip_ref, bias_ref, gain_ref, shift_ref, qkv_ref, proj_ref, mid_gain_ref, mid_shift_ref,
    *refs, patches,
):
    x_ref, normed_ref, projected_ref, probs_ref, mixed_ref, middle_ref, normed_mid_ref = refs[-7:]
    padded, width = x_ref.shape
    head = width // HEADS

    def first(r):
        x = sum(ref[r, :].astype(jnp.float32) for ref in (own_ref, core_ref, chip_ref))
        x = x + bias_ref[...]
        x_ref[r, :] = x
        normed_ref[r, :] = (norm_parts(x)[0] * gain_ref[...] + shift_ref[...]).astype(jnp.bfloat16)

    by_rows(padded, first)
    for part in range(3):
        columns = slice(part * width, (part + 1) * width)
        projected_ref[:, columns] = times(normed_ref[...], qkv_ref[:, columns]).astype(jnp.bfloat16)
    lane = lax.broadcasted_iota(jnp.int32, (padded, LANES), 1)
    key = lax.broadcasted_iota(jnp.int32, (padded, padded), 1)
    factor = jnp.bfloat16(1.0 / math.sqrt(head))

    def pair_of(pair):
        def columns(part):
            return slice(part * width + pair * LANES, part * width + (pair + 1) * LANES)

        queries, keys, values = (projected_ref[:, columns(part)] for part in range(3))
        found = []
        for h in range(2):
            mine = (lane // head) == h
            scores = times_turned(jnp.where(mine, queries * factor, jnp.zeros_like(queries)), keys)
            scores = jnp.where(key < patches, scores, -1e30)
            raised = jnp.exp(scores - jnp.max(scores, axis=-1, keepdims=True))
            probs = raised * (1.0 / jnp.sum(raised, axis=-1, keepdims=True))
            low = probs.astype(jnp.bfloat16)
            probs_ref[pair * 2 + h] = low
            found.append(times(low, values))
        mixed_ref[:, columns(0)] = jnp.where(lane < head, found[0], found[1]).astype(jnp.bfloat16)

    for pair in range(HEADS // 2):
        pair_of(pair)
    middle_ref[...] = times(mixed_ref[...], proj_ref[...])

    def last(r):
        middle = middle_ref[r, :] + x_ref[r, :]
        middle_ref[r, :] = middle
        normed_mid_ref[r, :] = (
            norm_parts(middle)[0] * mid_gain_ref[...] + mid_shift_ref[...]
        ).astype(jnp.bfloat16)

    by_rows(padded, last)


def cost(flops, moved):
    return pl.CostEstimate(flops=flops, bytes_accessed=moved, transcendentals=0)


def whole(*shape):
    return pl.BlockSpec(shape, lambda *index: (0,) * len(shape))


def attend_call(
    terms, bias, gain, shift, qkv, proj, mid_gain, mid_shift, padded, patches, image, begun=()
):
    rows, width = terms[0].shape
    images = rows // padded
    row = lambda v: v.reshape(1, width)
    shapes = [
        ((rows, width), jnp.float32),
        ((rows, width), jnp.bfloat16),
        ((rows, 3 * width), jnp.bfloat16),
        ((images * HEADS, padded, padded), jnp.bfloat16),
        ((rows, width), jnp.bfloat16),
        ((rows, width), jnp.float32),
        ((rows, width), jnp.bfloat16),
    ]
    blocks = [
        pl.BlockSpec((HEADS, padded, padded), lambda i: (image, 0, 0))
        if len(shape) == 3
        else pl.BlockSpec((padded, shape[1]), lambda i: (image, 0))
        for shape, _ in shapes
    ]
    return pl.pallas_call(
        functools.partial(attend_kernel, patches=patches),
        grid=(1,),
        in_specs=[
            *[pl.BlockSpec((padded, width), lambda i: (image, 0))] * 2,
            whole(padded, width),
            *[whole(1, width)] * 3,
            whole(width, 3 * width),
            whole(width, width),
            *[whole(1, width)] * 2,
            *[pl.BlockSpec(memory_space=pl.ANY)] * len(begun),
        ],
        out_specs=blocks,
        out_shape=[jax.ShapeDtypeStruct(*s) for s in shapes],
        input_output_aliases={10 + k: k for k in range(len(begun))},
        compiler_params=pltpu.CompilerParams(vmem_limit_bytes=VMEM_LIMIT),
        cost_estimate=cost(4 << 30, 8 << 20),
        name="attend",
    )(*terms, row(bias), row(gain), row(shift), qkv, proj, row(mid_gain), row(mid_shift), *begun)


def store_halves(core_ref, product, kept_ref, sent_ref):
    half = product.shape[1] // 2
    left, right = product[:, :half].astype(jnp.bfloat16), product[:, half:].astype(jnp.bfloat16)
    first = core_ref[0] == 0
    kept_ref[0] = jnp.where(first, left, right)
    sent_ref[0] = jnp.where(first, right, left)


def mlp_kernel(
    core_ref, normed_ref, middle_ref, cot_ref, gain_ref, up_ref, down_ref,
    out_ref, grad_ref, low_ref, down_kept_ref, down_sent_ref, up_kept_ref, up_sent_ref,
    gain_grad_ref, shift_grad_ref,
    result_ref, slope_ref, wide_ref, back_ref, active_ref, grad_up_ref,
):
    step = pl.program_id(0)
    rows = normed_ref.shape[0]
    wide_ref[...] = times(normed_ref[...], up_ref[...])
    back_ref[...] = times_turned(cot_ref[...], down_ref[...])

    def middle_part(r):
        x = wide_ref[r, :]
        below = 0.5 * (1.0 + lax.erf(x * math.sqrt(0.5)))
        density = jnp.exp(-0.5 * x * x) * (1.0 / math.sqrt(2.0 * math.pi))
        active_ref[r, :] = (x * below).astype(jnp.bfloat16)
        grad_up_ref[r, :] = (back_ref[r, :] * (below + x * density)).astype(jnp.bfloat16)

    by_rows(rows, middle_part)
    product = turned_times(active_ref[...], cot_ref[...])
    store_halves(core_ref, product, down_kept_ref, down_sent_ref)
    product = turned_times(normed_ref[...], grad_up_ref[...])
    store_halves(core_ref, product, up_kept_ref, up_sent_ref)

    @pl.when(step == 0)
    def _():
        result_ref[...] = times(active_ref[...], down_ref[...])
        slope_ref[...] = times_turned(grad_up_ref[...], up_ref[...])

    @pl.when(step > 0)
    def _():
        result_ref[...] += times(active_ref[...], down_ref[...])
        slope_ref[...] += times_turned(grad_up_ref[...], up_ref[...])

    @pl.when(step == pl.num_programs(0) - 1)
    def _():
        gain_grad_ref[...] = jnp.zeros_like(gain_grad_ref)
        shift_grad_ref[...] = jnp.zeros_like(shift_grad_ref)

        def last(r):
            middle, slope = middle_ref[r, :], slope_ref[r, :]
            out_ref[r, :] = (middle + result_ref[r, :]).astype(jnp.bfloat16)
            back, terms = norm_backward(middle, slope, gain_ref[...])
            grad = cot_ref[r, :].astype(jnp.float32) + back
            grad_ref[r, :] = grad
            low_ref[r, :] = grad.astype(jnp.bfloat16)
            gain_grad_ref[...] += jnp.sum(terms, axis=0, keepdims=True)
            shift_grad_ref[...] += jnp.sum(slope, axis=0, keepdims=True)

        by_rows(rows, last)


def mlp_call(core, normed, middle, cot, gain, up, down):
    rows, width = middle.shape
    hidden = up.shape[1]
    steps = hidden // width
    f32, bf16 = jnp.float32, jnp.bfloat16
    half = (1, width, width // 2)
    return pl.pallas_call(
        mlp_kernel,
        grid=(steps,),
        in_specs=[
            pl.BlockSpec(memory_space=pltpu.SMEM),
            whole(rows, width),
            whole(rows, width),
            whole(rows, width),
            whole(1, width),
            pl.BlockSpec((width, width), lambda j: (0, j)),
            pl.BlockSpec((width, width), lambda j: (j, 0)),
        ],
        out_specs=[
            whole(rows, width),
            whole(rows, width),
            whole(rows, width),
            *[pl.BlockSpec(half, lambda j: (j, 0, 0))] * 4,
            whole(1, width),
            whole(1, width),
        ],
        out_shape=[
            jax.ShapeDtypeStruct((rows, width), bf16),
            jax.ShapeDtypeStruct((rows, width), f32),
            jax.ShapeDtypeStruct((rows, width), bf16),
            *[jax.ShapeDtypeStruct((steps, width, width // 2), bf16)] * 4,
            jax.ShapeDtypeStruct((1, width), f32),
            jax.ShapeDtypeStruct((1, width), f32),
        ],
        scratch_shapes=[pltpu.VMEM((rows, width), t) for t in (f32, f32, f32, f32, bf16, bf16)],
        compiler_params=pltpu.CompilerParams(vmem_limit_bytes=VMEM_LIMIT),
        cost_estimate=cost(12 * rows * width * hidden, 30 << 20),
        name="mlp",
    )(core, normed, middle, cot, gain.reshape(1, width), up, down)


def attend_back_kernel(low_ref, projected_ref, probs_ref, proj_ref, *refs):
    grad_projected_ref, mixed_grad_ref = refs[-2:]
    padded, width = low_ref.shape
    head = width // HEADS
    mixed_grad_ref[...] = times_turned(low_ref[...], proj_ref[...]).astype(jnp.bfloat16)
    lane = lax.broadcasted_iota(jnp.int32, (padded, LANES), 1)
    factor = jnp.bfloat16(1.0 / math.sqrt(head))

    def pair_of(pair):
        def columns(part):
            return slice(part * width + pair * LANES, part * width + (pair + 1) * LANES)

        queries, keys, values = (projected_ref[:, columns(part)] for part in range(3))
        queries, keys = queries * factor, keys * factor
        grads = mixed_grad_ref[:, columns(0)]
        found = [], [], []
        for h in range(2):
            mine = (lane // head) == h
            low = probs_ref[pair * 2 + h]
            probs = low.astype(jnp.float32)
            grad_probs = times_turned(jnp.where(mine, grads, jnp.zeros_like(grads)), values)
            scaled = grad_probs * probs
            total = jnp.sum(scaled, axis=-1, keepdims=True)
            grad_scores = (scaled - probs * total).astype(jnp.bfloat16)
            found[0].append(times(grad_scores, keys))
            found[1].append(turned_times(grad_scores, queries))
            found[2].append(turned_times(low, grads))
        for part in range(3):
            grad_projected_ref[:, columns(part)] = jnp.where(
                lane < head, found[part][0], found[part][1]
            ).astype(jnp.bfloat16)

    for pair in range(HEADS // 2):
        pair_of(pair)


def attend_back_call(low, projected, probs, proj, padded, first, count, begun=None):
    rows, width = low.shape
    return pl.pallas_call(
        attend_back_kernel,
        grid=(count,),
        in_specs=[
            pl.BlockSpec((padded, width), lambda i: (i + first, 0)),
            pl.BlockSpec((padded, 3 * width), lambda i: (i + first, 0)),
            pl.BlockSpec((HEADS, padded, padded), lambda i: (i + first, 0, 0)),
            whole(width, width),
            *([] if begun is None else [pl.BlockSpec(memory_space=pl.ANY)]),
        ],
        out_specs=pl.BlockSpec((padded, 3 * width), lambda i: (i + first, 0)),
        out_shape=jax.ShapeDtypeStruct((rows, 3 * width), jnp.bfloat16),
        scratch_shapes=[pltpu.VMEM((padded, width), jnp.bfloat16)],
        input_output_aliases={} if begun is None else {4: 0},
        compiler_params=pltpu.CompilerParams(vmem_limit_bytes=VMEM_LIMIT),
        cost_estimate=cost(count * (6 << 30), count * (5 << 20)),
        name="attend_back",
    )(low, projected, probs, proj, *([] if begun is None else [begun]))


def first_norm_back_kernel(
    grad_projected_ref, grad_ref, x_ref, gain_ref, qkv_ref,
    grad_x_ref, bias_grad_ref, gain_grad_ref, shift_grad_ref, slope_ref,
):
    rows, width = x_ref.shape
    slope_ref[...] = times_turned(grad_projected_ref[:, :width], qkv_ref[:, :width])
    for part in range(1, 3):
        columns = slice(part * width, (part + 1) * width)
        slope_ref[...] += times_turned(grad_projected_ref[:, columns], qkv_ref[:, columns])
    for ref in (bias_grad_ref, gain_grad_ref, shift_grad_ref):
        ref[...] = jnp.zeros_like(ref)

    def last(r):
        slope = slope_ref[r, :]
        back, terms = norm_backward(x_ref[r, :], slope, gain_ref[...])
        grad = grad_ref[r, :] + back
        grad_x_ref[r, :] = grad.astype(jnp.bfloat16)
        bias_grad_ref[...] += jnp.sum(grad, axis=0, keepdims=True)
        gain_grad_ref[...] += jnp.sum(terms, axis=0, keepdims=True)
        shift_grad_ref[...] += jnp.sum(slope, axis=0, keepdims=True)

    by_rows(rows, last)


def first_norm_back_call(grad_projected, grad, x, gain, qkv):
    rows, width = x.shape
    row = jax.ShapeDtypeStruct((1, width), jnp.float32)
    return pl.pallas_call(
        first_norm_back_kernel,
        out_shape=[jax.ShapeDtypeStruct((rows, width), jnp.bfloat16), row, row, row],
        scratch_shapes=[pltpu.VMEM((rows, width), jnp.float32)],
        compiler_params=pltpu.CompilerParams(vmem_limit_bytes=VMEM_LIMIT),
        cost_estimate=cost(1 << 30, 1 << 20),
        name="first_norm_back",
    )(grad_projected, grad, x, gain.reshape(1, width), qkv)


def attend_weights_kernel(
    core_ref, normed_ref, mixed_ref, grad_projected_ref, low_ref, kept_ref, sent_ref
):
    step = pl.program_id(0)

    @pl.when(step < 3)
    def _():
        product = turned_times(normed_ref[...], grad_projected_ref[...])
        store_halves(core_ref, product, kept_ref, sent_ref)

    @pl.when(step == 3)
    def _():
        product = turned_times(mixed_ref[...], low_ref[...])
        store_halves(core_ref, product, kept_ref, sent_ref)


def attend_weights_call(core, normed, mixed, grad_projected, low):
    rows, width = normed.shape
    half = (width, width // 2)
    return pl.pallas_call(
        attend_weights_kernel,
        grid=(4,),
        in_specs=[
            pl.BlockSpec(memory_space=pltpu.SMEM),
            whole(rows, width),
            whole(rows, width),
            pl.BlockSpec((rows, width), lambda j: (0, jnp.minimum(j, 2))),
            whole(rows, width),
        ],
        out_specs=[pl.BlockSpec((1, *half), lambda j: (j, 0, 0))] * 2,
        out_shape=[jax.ShapeDtypeStruct((4, *half), jnp.bfloat16)] * 2,
        compiler_params=pltpu.CompilerParams(vmem_limit_bytes=VMEM_LIMIT),
        cost_estimate=cost(8 * rows * width * width, 30 << 20),
        name="attend_weights",
    )(core, normed, mixed, grad_projected, low)


def fill_starts(counts_ref, starts_ref):
    images = counts_ref.shape[0]
    total, big, most, first = 0, 0, counts_ref[0], 0
    for m in range(images):
        starts_ref[m] = jnp.int32(total)
        if m:
            better = counts_ref[m] > most
            big = jnp.where(better, m, big)
            first = jnp.where(better, total, first)
            most = jnp.where(better, counts_ref[m], most)
        total = total + counts_ref[m]
    starts_ref[images] = jnp.int32(total)
    return big, first, first + most


def strided(ref, first, count, stride):
    parts = [ref[c, pl.ds(first, count, stride=stride), :] for c in range(ref.shape[0])]
    return jnp.concatenate(parts, axis=1)


def fill_choice(wave_row_ref, choice_ref, waves, big_lo, big_hi):
    slots = wave_row_ref.shape[1]
    slot = lax.broadcasted_iota(jnp.int32, (1, slots), 1)
    alone = waves + slot - jnp.where(slot >= big_hi, big_hi - big_lo, 0)
    column = jnp.where((slot >= big_lo) & (slot < big_hi), wave_row_ref[...], alone)
    index = lax.broadcasted_iota(jnp.int32, choice_ref.shape, 0)
    choice_ref[...] = jnp.where(index == column, 1.0, 0.0).astype(jnp.bfloat16)


def fill_spread(kin_ref, spread_ref):
    waves, depth = kin_ref.shape
    rows = waves * GROUP
    of_wave = lax.broadcasted_iota(jnp.int32, (rows, waves), 0) // GROUP
    pick = of_wave == lax.broadcasted_iota(jnp.int32, (rows, waves), 1)
    repeated = times(jnp.where(pick, 1.0, 0.0).astype(jnp.bfloat16), kin_ref[...])
    place = lax.broadcasted_iota(jnp.int32, (rows, depth), 0) % GROUP
    for q in range(GROUP):
        spread_ref[:, q * depth : (q + 1) * depth] = jnp.where(place == q, repeated, 0.0).astype(
            jnp.bfloat16
        )


def embed_kernel(
    place_ref, counts_ref, waves_ref, wave_row_ref, kin_ref, weight_ref, pix_ref,
    own_ref, core_ref, chip_ref, far_ref, big_out, small_out, rows_out, table_out,
    starts_ref, choice_ref, spread_ref, big_ref, small_ref, rows_ref, table_ref,
    turn_ref, wide_ref, acc_ref, semaphores,
):
    step = pl.program_id(0)
    waves, positions, width = table_ref.shape
    depth = kin_ref.shape[1]
    images = counts_ref.shape[0]
    patches, per_step, slots = pix_ref.shape
    padded = acc_ref.shape[0]
    held = own_ref.shape[0]
    big, big_lo, big_hi = fill_starts(counts_ref, starts_ref)

    @pl.when(step == 0)
    def _():
        fill_choice(wave_row_ref, choice_ref, waves, big_lo, big_hi)
        fill_spread(kin_ref, spread_ref)
        turn_ref[...] = jnp.zeros_like(turn_ref)

    first_q = pl.multiple_of(step * per_step, per_step)
    for q in range(per_step):
        rows_ref[first_q + q] = times(kin_ref[...], weight_ref[q]).astype(jnp.bfloat16)
    parts = []
    for q in range(0, per_step, GROUP):
        made = times(spread_ref[...], weight_ref[q : q + GROUP].reshape(GROUP * depth, width))
        parts.append(made.reshape(waves, GROUP, width))
    table_ref[:, pl.ds(first_q, per_step), :] = jnp.concatenate(parts, axis=1).astype(jnp.bfloat16)
    turn_ref[: patches * per_step] = times_turned(
        pix_ref[...].reshape(patches * per_step, slots), choice_ref[...]
    )
    for q in range(per_step):
        turned = turn_ref[pl.ds(q, 2 * LANES, stride=per_step), :].T
        big_ref[first_q + q] = turned[:waves, :padded].astype(jnp.bfloat16)
        for c in range(2):
            wide_ref[c, pl.ds(first_q + q, SMALL, stride=positions), :] = turned[
                waves : waves + SMALL, c * LANES : (c + 1) * LANES
            ]

    @pl.when(step == pl.num_programs(0) - 1)
    def _():
        def narrow(j, carry):
            rows = pl.ds(pl.multiple_of(j * positions, positions), positions)
            both = jnp.concatenate([wide_ref[0, rows, :], wide_ref[1, rows, :]], axis=1)
            small_ref[j] = both[:, :padded].astype(jnp.bfloat16)
            return carry

        lax.fori_loop(0, SMALL, narrow, 0, unroll=8)
        pairs = ((big_ref, big_out), (small_ref, small_out), (rows_ref, rows_out), (table_ref, table_out))
        copies = [
            pltpu.make_async_copy(source, target, semaphores.at[k])
            for k, (source, target) in enumerate(pairs)
        ]
        for copy in copies:
            copy.start()

        def store(m):
            block = (m // held) ^ place_ref[0]
            low = acc_ref[...].astype(jnp.bfloat16)
            for index, ref in enumerate((own_ref, core_ref, chip_ref, far_ref)):

                @pl.when(block == index)
                def _(ref=ref):
                    ref[m % held] = low

        acc_ref[...] = jnp.zeros_like(acc_ref)

        def big_part(j, carry):
            first = pl.ds(pl.multiple_of(j * GROUP, GROUP), GROUP)
            left = big_ref[first].reshape(GROUP * waves, padded)
            acc_ref[...] += turned_times(left, rows_ref[first].reshape(GROUP * waves, width))
            return carry

        lax.fori_loop(0, positions // GROUP, big_part, 0, unroll=True)
        store(big)

        def image(m, carry):
            first, last = starts_ref[m], starts_ref[m + 1]
            shift = jnp.where(first >= big_hi, big_lo - big_hi, 0)

            @pl.when(m != big)
            def _():
                acc_ref[...] = jnp.zeros_like(acc_ref)

                def part(j, carry):
                    lefts, rights = [], []
                    for k in range(QUAD):
                        s = first + j * QUAD + k
                        here = jnp.minimum(s, last - 1)
                        factor = jnp.where(s < last, 1.0, 0.0).astype(jnp.bfloat16)
                        lefts.append(small_ref[here + shift] * factor)
                        rights.append(table_ref[waves_ref[here]])
                    acc_ref[...] += turned_times(
                        jnp.concatenate(lefts, axis=0), jnp.concatenate(rights, axis=0)
                    )
                    return carry

                lax.fori_loop(0, (last - first + QUAD - 1) // QUAD, part, 0)
                store(m)

            return carry

        lax.fori_loop(0, images, image, 0)
        for copy in copies:
            copy.wait()


def embed_call(place, counts, band_waves, kernel_low, kernel_weight, pixels):
    patches, positions, slots = pixels.shape
    waves = kernel_low.shape[0]
    depth, width = kernel_weight.shape[1:]
    images = counts.shape[0]
    padded = pad_rows(patches)
    per_step = positions // STEPS
    smem = pl.BlockSpec(memory_space=pltpu.SMEM)
    block = (images // 4, padded, width)
    kept = [
        (positions, waves, padded),
        (SMALL, positions, padded),
        (positions, waves, width),
        (waves, positions, width),
    ]
    return pl.pallas_call(
        embed_kernel,
        grid=(STEPS,),
        in_specs=[
            smem,
            smem,
            smem,
            whole(1, slots),
            whole(waves, depth),
            pl.BlockSpec((per_step, depth, width), lambda i: (i, 0, 0)),
            pl.BlockSpec((patches, per_step, slots), lambda i: (0, i, 0)),
        ],
        out_specs=[*[whole(*block)] * 4, *[pl.BlockSpec(memory_space=pl.ANY)] * 4],
        out_shape=[
            *[jax.ShapeDtypeStruct(block, jnp.bfloat16)] * 4,
            *[jax.ShapeDtypeStruct(shape, jnp.bfloat16) for shape in kept],
        ],
        scratch_shapes=[
            pltpu.SMEM((images + 1,), jnp.int32),
            pltpu.VMEM((LANES, slots), jnp.bfloat16),
            pltpu.VMEM((waves * GROUP, GROUP * depth), jnp.bfloat16),
            *[pltpu.VMEM(shape, jnp.bfloat16) for shape in kept],
            pltpu.VMEM((2 * LANES * per_step, LANES), jnp.float32),
            pltpu.VMEM((2, SMALL * positions, LANES), jnp.float32),
            pltpu.VMEM((padded, width), jnp.float32),
            pltpu.SemaphoreType.DMA((4,)),
        ],
        compiler_params=pltpu.CompilerParams(vmem_limit_bytes=VMEM_LIMIT),
        name="embed",
    )(place, counts, band_waves, band_waves[None], kernel_low, kernel_weight, pixels)


def embed_back_kernel(
    place_ref, bits_ref, counts_ref, waves_ref, own_ref, core_ref, chip_ref, far_ref,
    big_ref, small_ref, rows_ref, table_ref, weight_ref, vectors_ref,
    kept_ref, sent_ref, second_kept_ref, second_sent_ref, big_slope_ref, slope_ref, in_grad_ref,
    starts_ref, order_ref, grad_ref, sum_ref, wide_ref, semaphores,
):
    step = pl.program_id(0)
    waves, positions, width = table_ref.shape
    padded = big_ref.shape[2]
    images = counts_ref.shape[0]
    held = own_ref.shape[0]
    place = place_ref[0]
    count = GROUP * waves

    def grads_of(m):
        return grad_ref[((m // held) ^ place) * held + m % held]

    @pl.when(step == 0)
    def _():
        copies = [
            pltpu.make_async_copy(ref, grad_ref.at[pl.ds(k * held, held)], semaphores.at[k])
            for k, ref in enumerate((own_ref, core_ref, chip_ref, far_ref))
        ]
        for copy in copies:
            copy.start()
        big, big_lo, big_hi = fill_starts(counts_ref, starts_ref)
        row = lax.broadcasted_iota(jnp.int32, (count, count), 0)
        column = lax.broadcasted_iota(jnp.int32, (count, count), 1)
        same = (row // waves == column % GROUP) & (row % waves == column // GROUP)
        order_ref[...] = jnp.where(same, 1.0, 0.0).astype(jnp.bfloat16)
        in_grad_ref[:waves] = jnp.zeros((waves, in_grad_ref.shape[1]), jnp.float32)
        in_grad_ref[waves:] = vectors_ref[...]
        slope_ref[...] = jnp.zeros_like(slope_ref)
        wide_ref[...] = jnp.zeros_like(wide_ref)
        for copy in copies:
            copy.wait()
        grads = grads_of(big)

        def big_part(j, carry):
            first = pl.ds(pl.multiple_of(j * GROUP, GROUP), GROUP)
            slope = times_turned(rows_ref[first].reshape(count, width), grads)
            big_slope_ref[first, :, :padded] = slope.astype(jnp.bfloat16).reshape(
                GROUP, waves, padded
            )
            sum_ref[pl.ds(pl.multiple_of(j * count, count), count), :] = times(
                big_ref[first].reshape(count, padded), grads
            )
            return carry

        lax.fori_loop(0, positions // GROUP, big_part, 0, unroll=True)

        def image(m, carry):
            first, last = starts_ref[m], starts_ref[m + 1]
            shift = jnp.where(first >= big_hi, big_lo - big_hi, 0)

            @pl.when(m != big)
            def _():
                grads = grads_of(m)

                def part(j, carry):
                    lefts, rights, index = [], [], []
                    for k in range(QUAD):
                        s = first + j * QUAD + k
                        here = jnp.minimum(s, last - 1)
                        factor = jnp.where(s < last, 1.0, 0.0).astype(jnp.bfloat16)
                        index.append(here)
                        lefts.append(table_ref[waves_ref[here]])
                        rights.append(small_ref[here + shift] * factor)
                    own = times_turned(jnp.concatenate(lefts, axis=0), grads)
                    more = times(jnp.concatenate(rights, axis=0), grads)
                    for k in range(QUAD):
                        part_rows = slice(k * positions, (k + 1) * positions)
                        row = pl.multiple_of((index[k] + shift) * positions, positions)
                        slope_ref[0, pl.ds(row, positions), :] = own[part_rows, :LANES]
                        slope_ref[1, pl.ds(row, positions), : padded - LANES] = own[
                            part_rows, LANES:
                        ]
                        wide_ref[waves_ref[index[k]]] += more[part_rows]
                    return carry

                lax.fori_loop(0, (last - first + QUAD - 1) // QUAD, part, 0)

            return carry

        lax.fori_loop(0, images, image, 0)

    odd = bits_ref[0]
    found = jnp.zeros((waves, in_grad_ref.shape[1]), jnp.float32)
    for ref, half in ((kept_ref, odd), (sent_ref, 1 - odd)):
        first_q = pl.multiple_of((2 * step + half) * GROUP, GROUP)
        block = wide_ref[:, pl.ds(first_q, GROUP), :].reshape(count, width).astype(jnp.bfloat16)
        rows = pl.ds(pl.multiple_of(first_q * waves, count), count)
        total = (sum_ref[rows, :] + times(order_ref[...], block)).astype(jnp.bfloat16)
        low = total.reshape(GROUP, waves, width)
        ref[0] = low[:, :, : width // 2]

        @pl.when(step % 2 == bits_ref[1])
        def _(low=low, half=half):
            second_kept_ref[step // 2, half] = low[:, :, width // 2 :]

        @pl.when(step % 2 != bits_ref[1])
        def _(low=low, half=half):
            second_sent_ref[step // 2, half] = low[:, :, width // 2 :]

        for q in range(GROUP):
            part = total[q * waves : (q + 1) * waves]
            found = found + times_turned(part, weight_ref[half * GROUP + q])
    in_grad_ref[:waves] += found


def pixel_back_kernel(
    counts_ref, wave_row_ref, big_slope_ref, slope_ref, pix_grad_ref, starts_ref, choice_ref, turn_ref
):
    step = pl.program_id(0)
    patches, per_step, _ = pix_grad_ref.shape
    positions, waves, _ = big_slope_ref.shape

    @pl.when(step == 0)
    def _():
        _, big_lo, big_hi = fill_starts(counts_ref, starts_ref)
        fill_choice(wave_row_ref, choice_ref, waves, big_lo, big_hi)

    first_q = pl.multiple_of(step * per_step, per_step)
    for q in range(per_step):
        alone = strided(slope_ref, first_q + q, SMALL, positions).astype(jnp.bfloat16)
        chosen = jnp.concatenate([big_slope_ref[first_q + q], alone], axis=0)
        spread = turned_times(chosen, choice_ref[: waves + SMALL])
        for c in range(turn_ref.shape[0]):
            turn_ref[c, pl.ds(q, patches, stride=per_step), :] = spread[
                :patches, c * LANES : (c + 1) * LANES
            ]
    for c in range(turn_ref.shape[0]):
        pix_grad_ref[:, :, c * LANES : (c + 1) * LANES] = (
            turn_ref[c].astype(jnp.bfloat16).reshape(patches, per_step, LANES)
        )


def pixel_back_call(counts, band_waves, big_slope, slope, patches):
    positions = big_slope.shape[0]
    slots = band_waves.shape[0]
    per_step = positions // STEPS
    return pl.pallas_call(
        pixel_back_kernel,
        grid=(STEPS,),
        in_specs=[
            pl.BlockSpec(memory_space=pltpu.SMEM),
            whole(1, slots),
            whole(*big_slope.shape),
            whole(*slope.shape),
        ],
        out_specs=pl.BlockSpec((patches, per_step, slots), lambda i: (0, i, 0)),
        out_shape=jax.ShapeDtypeStruct((patches, positions, slots), jnp.bfloat16),
        scratch_shapes=[
            pltpu.SMEM((counts.shape[0] + 1,), jnp.int32),
            pltpu.VMEM((LANES, slots), jnp.bfloat16),
            pltpu.VMEM((slots // LANES, patches * per_step, LANES), jnp.float32),
        ],
        compiler_params=pltpu.CompilerParams(vmem_limit_bytes=VMEM_LIMIT),
        cost_estimate=cost(1 << 20, 1 << 10),
        name="pixel_back",
    )(counts, band_waves[None], big_slope, slope)


def embed_back_call(place, bits, counts, band_waves, grads, kept, kernel_weight, vectors):
    positions, waves, padded = kept[0].shape
    width = kept[2].shape[2]
    images = counts.shape[0]
    pairs = positions // (2 * GROUP)
    block = (1, GROUP, waves, width // 2)
    second = (pairs // 2, 2, *block[1:])
    depth = kernel_weight.shape[1]
    smem = pl.BlockSpec(memory_space=pltpu.SMEM)
    return pl.pallas_call(
        embed_back_kernel,
        grid=(pairs,),
        in_specs=[
            smem,
            smem,
            smem,
            smem,
            *[pl.BlockSpec(memory_space=pl.ANY)] * 4,
            *[whole(*array.shape) for array in kept],
            pl.BlockSpec((2 * GROUP, depth, width), lambda i: (i, 0, 0)),
            whole(*vectors.shape),
        ],
        out_specs=[
            *[pl.BlockSpec(block, lambda i: (i, 0, 0, 0))] * 2,
            *[whole(*second)] * 2,
            whole(positions, waves, 2 * LANES),
            whole(2, SMALL * positions, LANES),
            whole(waves + vectors.shape[0], depth),
        ],
        out_shape=[
            *[jax.ShapeDtypeStruct((pairs, *block[1:]), jnp.bfloat16)] * 2,
            *[jax.ShapeDtypeStruct(second, jnp.bfloat16)] * 2,
            jax.ShapeDtypeStruct((positions, waves, 2 * LANES), jnp.bfloat16),
            jax.ShapeDtypeStruct((2, SMALL * positions, LANES), jnp.float32),
            jax.ShapeDtypeStruct((waves + vectors.shape[0], depth), jnp.float32),
        ],
        scratch_shapes=[
            pltpu.SMEM((images + 1,), jnp.int32),
            pltpu.VMEM((GROUP * waves, GROUP * waves), jnp.bfloat16),
            pltpu.VMEM((images, padded, width), jnp.bfloat16),
            pltpu.VMEM((positions * waves, width), jnp.float32),
            pltpu.VMEM((waves, positions, width), jnp.float32),
            pltpu.SemaphoreType.DMA((4,)),
        ],
        compiler_params=pltpu.CompilerParams(vmem_limit_bytes=VMEM_LIMIT),
        name="embed_back",
    )(place, bits, counts, band_waves, *grads, *kept, kernel_weight, vectors)


HEADS = 12
WD = 128
WHEADS = 4


highest = lax.Precision.HIGHEST


def layer_norm(values, norm_gain, norm_shift, epsilon):
    centered = values - jnp.mean(values, axis=-1, keepdims=True)
    variance = jnp.mean(centered * centered, axis=-1, keepdims=True)
    return centered * lax.rsqrt(variance + epsilon) * norm_gain + norm_shift


def wave_embed(wavelengths):
    halfwidth = WD // 2
    indices = jnp.arange(halfwidth, dtype=jnp.float32)
    frequency = 1.0 / 10000.0 ** (indices / halfwidth)
    angles = (wavelengths * 1000.0)[:, None] * frequency[None, :]
    return jnp.concatenate([jnp.sin(angles), jnp.cos(angles)], axis=1)


def product(left, right, axes=(1, 0)):
    return lax.dot_general(
        left,
        right,
        (((axes[0],), (axes[1],)), ((), ())),
        precision=highest,
        preferred_element_type=jnp.float32,
    )


@jax.custom_vjp
def dot_rows(left, right):
    return product(left, right)


def dot_rows_forward(left, right):
    return product(left, right), (left, right)


def dot_rows_backward(saved, slope):
    left, right = saved
    return product(slope, right, (1, 1)), product(left, slope, (0, 0))


dot_rows.defvjp(dot_rows_forward, dot_rows_backward)


@jax.custom_vjp
def dot_turned(left, right):
    return product(left, right, (1, 1))


def dot_turned_forward(left, right):
    return product(left, right, (1, 1)), (left, right)


def dot_turned_backward(saved, slope):
    left, right = saved
    return product(slope, right), product(slope, left, (0, 0))


dot_turned.defvjp(dot_turned_forward, dot_turned_backward)


def hypernet(sequence, length, wave_qkv, wave_proj, wave_gain, wave_shift, wave_up, wave_down, kernel_gain, kernel_shift):
    rows, width = sequence.shape
    head_width = width // WHEADS
    projected = dot_rows(sequence, wave_qkv)
    queries, keys, values = (projected[:, i * width : (i + 1) * width] for i in range(3))
    of_head = lax.broadcasted_iota(jnp.int32, (rows, width), 1) // head_width
    real = lax.broadcasted_iota(jnp.int32, (rows, rows), 1) < length
    attended = jnp.zeros((rows, width), jnp.float32)
    for h in range(WHEADS):
        mine = (of_head == h).astype(jnp.float32)
        scores = dot_turned(queries * mine, keys) * (1.0 / math.sqrt(head_width))
        scores = jnp.where(real, scores, -1e30)
        raised = jnp.exp(scores - lax.stop_gradient(jnp.max(scores, axis=-1, keepdims=True)))
        weights = raised / jnp.sum(raised, axis=-1, keepdims=True)
        attended = attended + dot_rows(weights, values * mine)
    normed_first = layer_norm(
        sequence + dot_rows(attended, wave_proj), wave_gain, wave_shift, 1e-05
    )
    upward = dot_rows(normed_first, wave_up)
    widened = 0.5 * upward * (1.0 + lax.erf(upward * math.sqrt(0.5)))
    return layer_norm(
        normed_first + dot_rows(widened, wave_down), kernel_gain, kernel_shift, 1e-05
    )


def hyper_kernel(sequence_ref, *refs):
    params, (head_ref, low_ref, bias_ref) = refs[:8], refs[8:]
    waves = low_ref.shape[0]
    second = hypernet(sequence_ref[...], waves + 1, *(ref[...] for ref in params))
    low_ref[...] = (second[:waves] + sequence_ref[:waves]).astype(jnp.bfloat16)
    bias_ref[...] = product(second[waves : waves + 8], head_ref[...])


def hyper_call(sequence, params, bias_head, waves):
    depth = sequence.shape[1]
    return pl.pallas_call(
        hyper_kernel,
        out_shape=[
            jax.ShapeDtypeStruct((waves, depth), jnp.bfloat16),
            jax.ShapeDtypeStruct((8, bias_head.shape[1]), jnp.float32),
        ],
        compiler_params=pltpu.CompilerParams(vmem_limit_bytes=VMEM_LIMIT),
        cost_estimate=cost(1 << 20, 1 << 10),
        name="hyper",
    )(sequence, *params, bias_head)


def hyper_back_kernel(sequence_ref, in_grad_ref, bias_grad_ref, *refs):
    params, head_ref, outs, head_grad_ref = refs[:8], refs[8], refs[9:18], refs[18]
    rows, depth = sequence_ref.shape
    waves = in_grad_ref.shape[0]

    def apply(sequence, *values):
        return hypernet(sequence, waves + 1, *values)

    second, back = jax.vjp(apply, sequence_ref[...], *(ref[...] for ref in params))
    row = lax.broadcasted_iota(jnp.int32, (8, 1), 0)
    bias_grad = jnp.where(row == 0, bias_grad_ref[...], 0.0)
    last = product(bias_grad, head_ref[...], (1, 1))
    parts = [in_grad_ref[...], last]
    if rows > waves + 8:
        parts.append(jnp.zeros((rows - waves - 8, depth), jnp.float32))
    sequence_grad, *grads = back(jnp.concatenate(parts, axis=0))
    outs[0][...] = sequence_grad[waves : waves + 8]
    for ref, grad in zip(outs[1:], grads, strict=True):
        ref[...] = grad
    head_grad_ref[...] = product(second[waves : waves + 8], bias_grad, (0, 0))


def hyper_back_call(sequence, in_grad, bias_grad, params, bias_head):
    depth = sequence.shape[1]
    shapes = [(8, depth), *[p.shape for p in params], bias_head.shape]
    return pl.pallas_call(
        hyper_back_kernel,
        out_shape=[jax.ShapeDtypeStruct(shape, jnp.float32) for shape in shapes],
        compiler_params=pltpu.CompilerParams(vmem_limit_bytes=VMEM_LIMIT),
        cost_estimate=cost(14 << 30, 16 << 20),
        name="hyper_back",
    )(sequence, in_grad, bias_grad, *params, bias_head)


def swap_core(array):
    return lax.ppermute(array, "rows", [(0, 1), (1, 0), (2, 3), (3, 2)])


def swap_chip(array):
    return lax.ppermute(array, "rows", [(0, 2), (2, 0), (1, 3), (3, 1)])


def add_wide(left, right):
    return left.astype(jnp.float32) + right.astype(jnp.float32)


def rows_reduce(own, core, chip, far):
    met = swap_core(far)
    passed = [add_wide(*pair).astype(jnp.bfloat16) for pair in zip(chip, met)]
    return own, swap_core(core), [swap_chip(image) for image in passed]


def swap_band(array, bit):
    count = lax.axis_size("band")
    return lax.ppermute(array, "band", [(i, i ^ (1 << bit)) for i in range(count)])


def split(array, axis, bit):
    half = array.shape[axis] // 2
    return (
        lax.dynamic_slice_in_dim(array, bit * half, half, axis),
        lax.dynamic_slice_in_dim(array, (1 - bit) * half, half, axis),
    )


def split_band(array, bit, below=1):
    place = lax.axis_index("band")
    parts, bands, *rest = array.shape
    array = array.reshape(parts, bands // (2 * below), 2, below, *rest)
    halves = split(array, 2, (place >> bit) & 1)
    return [half.reshape(parts, bands // 2, *rest) for half in halves]


def add(kept, met):
    return add_wide(kept, met).astype(kept.dtype)


def split_sum(splitter, kept, met):
    return [add(*pair) for pair in zip(splitter(kept), splitter(met))]


def band_step(array, bit, below=1):
    kept, sent = split_band(array, bit, below)
    return add(kept, swap_band(sent, bit))


def band_rest(array, first):
    for bit in range(first, lax.axis_size("band").bit_length() - 1):
        array = band_step(array, bit)
    return array


def join(own, other, bit, axis):
    return jnp.where(
        bit == 0,
        jnp.concatenate([own, other], axis=axis),
        jnp.concatenate([other, own], axis=axis),
    )


def weight_gather(array, chip_first):
    place = lax.axis_index("rows")
    chip, core = place // 2, place % 2
    if chip_first:
        array = join(array, swap_chip(array), chip, 1)
    else:
        array = add_wide(array, swap_chip(array)).astype(array.dtype)
    return join(array, swap_core(array), core, 2).astype(jnp.float32)


def by_band(array):
    parts, rows, width = array.shape
    bands = lax.axis_size("band")
    return array.reshape(parts, bands, rows // bands, width)


def together(*arrays):
    return lax.optimization_barrier(arrays)


def side_by_side(parts):
    return parts.transpose(1, 0, 2).reshape(parts.shape[1], -1)


def band_bits():
    return range(lax.axis_size("band").bit_length() - 1)


def sum_steps(array, bits):
    for bit in bits:
        array = array + swap_band(array, bit)
    return array


def slot_masks(counts, slot_waves, waves):
    index = jnp.arange(counts.shape[0])
    ends = jnp.sum(jnp.where(index[None, :] <= index[:, None], counts[None, :], 0), axis=1)
    slots = jnp.arange(slot_waves.shape[0])
    owners = jnp.sum((ends[None, :] <= slots[:, None]).astype(jnp.int32), axis=1)
    return (
        (owners[:, None] == index[None, :]).astype(jnp.bfloat16),
        (slot_waves[:, None] == jnp.arange(waves)[None, :]).astype(jnp.bfloat16),
    )


def embed_plain(counts, slot_waves, kernel_low, kernel_weight, pixels):
    slots, positions, patches = pixels.shape
    table = jnp.einsum(
        "wk,qkc->wqc", kernel_low, kernel_weight, preferred_element_type=jnp.float32
    ).astype(jnp.bfloat16)
    of_image, of_wave = slot_masks(counts, slot_waves, table.shape[0])
    chunk = min(16, slots)

    def part(running, inputs):
        pixel, image, wave = inputs
        chosen = jnp.einsum("sw,wqc->sqc", wave, table)
        rows = jnp.einsum("sqp,sqc->spc", pixel, chosen, preferred_element_type=jnp.float32)
        image = image.astype(jnp.float32)
        return (running + jnp.einsum("si,spc->ipc", image, rows, precision=highest), None)

    shape = (counts.shape[0], patches, table.shape[2])
    total = lax.scan(
        part,
        jnp.zeros(shape, jnp.float32),
        tuple(a.reshape(-1, chunk, *a.shape[1:]) for a in (pixels, of_image, of_wave)),
    )[0]
    extra = pad_rows(patches) - patches
    return (jnp.pad(total.astype(jnp.bfloat16), ((0, 0), (0, extra), (0, 0))), table)


def embed_back_plain(counts, slot_waves, grads, table, pixels):
    slots, positions, patches = pixels.shape
    waves, _, width = table.shape
    of_image, of_wave = slot_masks(counts, slot_waves, waves)
    grads = grads[:, :patches]
    chunk = min(16, slots)

    def part(running, inputs):
        pixel, image, wave = inputs
        chosen = jnp.einsum("sw,wqc->sqc", wave, table)
        slope = jnp.einsum("si,ipc->spc", image, grads)
        own = jnp.einsum("sqc,spc->sqp", chosen, slope, preferred_element_type=jnp.float32)
        more = jnp.einsum("sqp,spc->sqc", pixel, slope, preferred_element_type=jnp.float32)
        wave = wave.astype(jnp.float32)
        added = jnp.einsum("sw,sqc->qwc", wave, more, precision=highest)
        return (running + added, own.astype(jnp.bfloat16))

    kernel_grad, pixel_grad = lax.scan(
        part,
        jnp.zeros((positions, waves, width), jnp.float32),
        tuple(a.reshape(-1, chunk, *a.shape[1:]) for a in (pixels, of_image, of_wave)),
    )
    return (pixel_grad.reshape(pixels.shape), kernel_grad.astype(jnp.bfloat16))


def body(
    pixels,
    band_counts,
    band_waves,
    wavelengths,
    bias_token,
    wave_qkv,
    wave_proj,
    wave_gain,
    wave_shift,
    wave_up,
    wave_down,
    kernel_gain,
    kernel_shift,
    bias_head,
    kernel_weight,
    attention_gain,
    attention_shift,
    block_qkv,
    block_proj,
    hidden_gain,
    hidden_shift,
    block_up,
    block_down,
    cotangent,
):
    waves, depth = wavelengths.shape[0], bias_token.shape[0]
    sequence = jnp.concatenate(
        [
            wave_embed(wavelengths),
            bias_token[None],
            jnp.zeros((-(waves + 1) % 8, depth), jnp.float32),
        ]
    )
    hyper_params = (
        wave_qkv,
        wave_proj,
        wave_gain[None],
        wave_shift[None],
        wave_up,
        wave_down,
        kernel_gain[None],
        kernel_shift[None],
    )
    kernel_low, conv_bias = hyper_call(sequence, hyper_params, bias_head, waves)
    conv_bias = conv_bias[0]
    counts = band_counts[0]
    slot_waves = band_waves[0]
    slot_total, positions, patches = pixels.shape
    images = counts.shape[0]
    width = kernel_weight.shape[2]
    bands = lax.axis_size("band")
    fits = waves * positions * width <= 1 << 21 and positions == bands * GROUP
    place = lax.axis_index("rows").astype(jnp.int32)
    padded = pad_rows(patches)
    if fits:
        turned_pixels = pixels.transpose(2, 1, 0)
        *blocks, kept_big, kept_small, kept_rows, kept_table = embed_call(
            place[None], counts, slot_waves, kernel_low, kernel_weight, turned_pixels
        )
    else:
        partial_rows, kernel_table = embed_plain(
            counts, slot_waves, kernel_low, kernel_weight, pixels
        )
        partial_rows = partial_rows.reshape(4, -1, padded, width)
        blocks = [lax.dynamic_index_in_dim(partial_rows, place ^ k, 0, False) for k in range(4)]
    own_term, core_term, chip_terms = rows_reduce(*blocks)
    terms = own_term.reshape(-1, width), core_term.reshape(-1, width)
    local_images = images // 4
    cot = jnp.pad(
        cotangent.reshape(local_images, patches, width), ((0, 0), (0, padded - patches), (0, 0))
    ).reshape(-1, width)
    attended = ()
    for image in range(local_images):
        attended = attend_call(
            (*terms, chip_terms[image]),
            conv_bias,
            attention_gain,
            attention_shift,
            block_qkv,
            block_proj,
            hidden_gain,
            hidden_shift,
            padded,
            patches,
            image,
            attended,
        )
    x, normed, projected, probs, mixed, middle, normed_mid = attended
    core = (lax.axis_index("rows") % 2).astype(jnp.int32)[None]
    chip = lax.axis_index("rows") // 2
    (
        result,
        grad_middle,
        grad_low,
        down_kept,
        down_sent,
        up_kept,
        up_sent,
        hidden_gain_part,
        hidden_shift_part,
    ) = mlp_call(core, normed_mid, middle, cot, hidden_gain, block_up, block_down)
    layer_output = result.reshape(local_images, padded, width)[:, :patches].reshape(-1, width)
    down_met, up_met = swap_core(down_sent), swap_core(up_sent)
    grad_projected = attend_back_call(grad_low, projected, probs, block_proj, padded, 0, 1)
    grad_projected, down_met, up_met = together(grad_projected, down_met, up_met)
    def by_bit(bit, below=1):
        return lambda array: split_band(array, bit, below)

    def by_chip(array):
        return split(by_band(array), 2, chip)

    down_kept, down_sent = split_sum(
        lambda array: split_band(by_band(array.reshape(1, -1, width // 2)), 0), down_kept, down_met
    )
    up_kept, up_sent = split_sum(by_chip, up_kept, up_met)
    grad_projected, down_kept, down_sent, up_kept, up_sent = together(
        grad_projected, down_kept, down_sent, up_kept, up_sent
    )
    down_met, up_met = swap_band(down_sent, 0), swap_chip(up_sent)
    grad_projected = attend_back_call(
        grad_low, projected, probs, block_proj, padded, 1, local_images - 1, grad_projected
    )
    grad_x, bias_part, attention_gain_part, attention_shift_part = first_norm_back_call(
        grad_projected, grad_middle, x, attention_gain, block_qkv
    )
    grad_x, grad_projected, down_met, up_met = together(grad_x, grad_projected, down_met, up_met)
    own = grad_x.reshape(local_images, padded, width)
    near, across = swap_core(own), swap_chip(own)
    near, grad_low = together(near, grad_low)
    down_kept, down_sent = split_sum(by_bit(1), down_kept, down_met)
    up_kept, up_sent = split_sum(by_bit(0), up_kept, up_met)
    down_met, up_met = swap_band(down_sent, 1), swap_band(up_sent, 0)
    attend_kept, attend_sent = attend_weights_call(core, normed, mixed, grad_projected, grad_low)
    vectors = jnp.concatenate(
        [
            bias_part,
            attention_gain_part,
            attention_shift_part,
            hidden_gain_part,
            hidden_shift_part,
        ]
    ).reshape(-1, kernel_weight.shape[1])
    across, attend_kept, attend_sent, down_met, up_met, vectors = together(
        across, attend_kept, attend_sent, down_met, up_met, vectors
    )
    far, attend_met = swap_core(across), swap_core(attend_sent)
    down_kept, down_sent = split_sum(by_bit(2), down_kept, down_met)
    up_kept, up_sent = split_sum(by_bit(1), up_kept, up_met)
    far, attend_met, down_kept, down_sent, up_kept, up_sent = together(
        far, attend_met, down_kept, down_sent, up_kept, up_sent
    )
    attend_kept, attend_sent = split_sum(by_chip, attend_kept, attend_met)
    attend_kept, attend_sent, near = together(attend_kept, attend_sent, near)
    attend_met = swap_chip(attend_sent)
    down_met, up_met = swap_band(down_sent, 2), swap_band(up_sent, 1)
    gathered = own, near, across, far
    band = lax.axis_index("band").astype(jnp.int32)
    if fits:
        *parts, big_slope, slope, summed = embed_back_call(
            place[None],
            jnp.stack([band % 2, band // 2 % 2]),
            counts,
            slot_waves,
            gathered,
            (kept_big, kept_small, kept_rows, kept_table),
            kernel_weight,
            vectors,
        )
        first_kept, first_sent, second_kept, second_sent = (
            part.reshape(1, bands // 2, -1, waves, width // 2) for part in parts
        )
    else:
        stacked = jnp.stack(gathered)
        ordered = jnp.concatenate(
            [lax.dynamic_index_in_dim(stacked, place ^ k, 0, False) for k in range(4)]
        )
        pixel_grad, kernel_grad = embed_back_plain(
            counts, slot_waves, ordered, kernel_table, pixels
        )
        in_part = jnp.einsum(
            "qwc,qkc->wk", kernel_grad, kernel_weight, preferred_element_type=jnp.float32
        )
        summed = jnp.concatenate([in_part, vectors])
        kernel_grad = kernel_grad.reshape(1, bands, -1, waves, width)
        first_kept, first_sent = split_band(kernel_grad[..., : width // 2], 0)
        second_kept, second_sent = split_band(kernel_grad[..., width // 2 :], 1, 2)
        big_slope = slope = summed
    first_kept, first_sent, second_kept, second_sent = together(
        first_kept, first_sent, second_kept, second_sent
    )
    first_sent, second_sent, summed, down_met, up_met, attend_met = together(
        first_sent, second_sent, summed, down_met, up_met, attend_met
    )
    bits = band_bits()
    first_met, second_met = swap_band(first_sent, 0), swap_band(second_sent, 1)
    summed = summed + swap_core(summed)
    summed, down_met, up_met, attend_met = together(summed, down_met, up_met, attend_met)
    summed = sum_steps(summed + swap_chip(summed), bits[:1])
    attend_kept, attend_sent = split_sum(by_bit(0), attend_kept, attend_met)
    down_all = band_rest(add(down_kept, down_met), 3)[:, 0]
    block_down_grad = weight_gather(down_all, False)[0]
    up_all = band_rest(add(up_kept, up_met), 2)[:, 0]
    first_met, second_met, summed, block_down_grad = together(
        first_met, second_met, summed, block_down_grad
    )
    first_kept, first_sent = split_sum(by_bit(1), first_kept, first_met)
    second_kept, second_sent = split_sum(by_bit(0), second_kept, second_met)
    first_sent, second_sent, summed, attend_sent, up_all = together(
        first_sent, second_sent, summed, attend_sent, up_all
    )
    first_met, second_met = swap_band(first_sent, 1), swap_band(second_sent, 0)
    attend_met = swap_band(attend_sent, 0)
    summed = sum_steps(summed, bits[1:])
    first_met, second_met, summed, attend_met, up_all = together(
        first_met, second_met, summed, attend_met, up_all
    )
    attend_kept, attend_sent = split_sum(by_bit(1), attend_kept, attend_met)
    owned = jnp.concatenate([add(first_kept, first_met), add(second_kept, second_met)], axis=-1)
    for bit in bits[2:-1]:
        owned = band_step(owned, bit)
    owned, summed, attend_sent, up_all, big_slope = together(
        owned, summed, attend_sent, up_all, big_slope
    )
    owned_met = swap_band(owned, bits[-1])
    if fits:
        pixel_grad = pixel_back_call(counts, slot_waves, big_slope, slope, patches)
    attend_met = swap_band(attend_sent, 1)
    block_up_grad = side_by_side(weight_gather(up_all, True))
    owned, owned_met, attend_kept, attend_met, pixel_grad, block_up_grad = together(
        owned, owned_met, attend_kept, attend_met, pixel_grad, block_up_grad
    )
    if fits:
        pixel_grad = pixel_grad.transpose(2, 1, 0)
    owned = add(owned, owned_met)[0]
    attend_all = band_rest(add(attend_kept, attend_met), 2)[:, 0]
    attend_grads = weight_gather(attend_all, True)
    block_qkv_grad, block_proj_grad = side_by_side(attend_grads[:3]), attend_grads[3]
    half_bands = bands // 2
    upper = lax.axis_index("band") // half_bands
    owned_weight = jnp.einsum(
        "wk,qwc->qkc",
        lax.dynamic_slice_in_dim(kernel_low, upper * (depth // 2), depth // 2, 1),
        owned.reshape(-1, waves, width),
        preferred_element_type=jnp.float32,
    ).astype(jnp.bfloat16)
    owned_weight, summed = together(owned_weight, summed)
    grad_kernel_in = summed[:waves]
    bias_grad, attention_gain_grad, attention_shift_grad, hidden_gain_grad, hidden_shift_grad = (
        summed[waves:].reshape(5, width)
    )
    groups = [list(range(half_bands)), list(range(half_bands, bands))]
    kernel_weight_grad = lax.all_to_all(
        owned_weight, "band", split_axis=1, concat_axis=0, tiled=True, axis_index_groups=groups
    )
    kernel_weight_grad = (
        kernel_weight_grad.reshape(half_bands, 2, positions // bands, depth // bands, width)
        .transpose(1, 0, 2, 3, 4)
        .reshape(positions, depth // bands, width)
        .astype(jnp.float32)
    )
    token_grad, *hyper_grads = hyper_back_call(
        sequence, grad_kernel_in, bias_grad[None], hyper_params, bias_head
    )
    return (
        layer_output,
        pixel_grad,
        kernel_weight_grad,
        token_grad[0],
        hyper_grads[0],
        hyper_grads[1],
        hyper_grads[2][0],
        hyper_grads[3][0],
        hyper_grads[4],
        hyper_grads[5],
        hyper_grads[6][0],
        hyper_grads[7][0],
        hyper_grads[8],
        attention_gain_grad,
        attention_shift_grad,
        block_qkv_grad,
        block_proj_grad,
        hidden_gain_grad,
        hidden_shift_grad,
        block_up_grad,
        block_down_grad,
    )


def solution(mesh):
    in_specs = (
        P("band", "rows", None),
        P("band", None),
        P("band", None),
        P(),
        P(),
        P(),
        P(),
        P(),
        P(),
        P(),
        P(),
        P(),
        P(),
        P(),
        P("rows", None, None),
        P(),
        P(),
        P(),
        P(),
        P(),
        P(),
        P(),
        P(),
        P(("band", "rows"), None),
    )
    out_specs = (
        P(("band", "rows"), None),
        P("band", "rows", None),
        P("rows", "band", None),
        P(),
        P(),
        P(),
        P(),
        P(),
        P(),
        P(),
        P(),
        P(),
        P(),
        P(),
        P(),
        P("band", None),
        P("band", None),
        P(),
        P(),
        P("band", None),
        P("band", None),
    )
    return jax.shard_map(body, mesh=mesh, in_specs=in_specs, out_specs=out_specs, check_vma=False)
```
